32 devices in a mesh: seq: 4 (over y, x), ctx: 8 (over z, core).
Axes of the slice: x: 2, y: 2, z: 4, core: 2. Of those that a mesh axis runs over, the one named last changes fastest.
Arguments:
- tokens: bfloat16 [4, 2048, 768], P('seq', 'ctx'), may hold values from -6 to 6
- gain_one: float32 [768], replicated, may hold values from 0.5 to 1.5
- bias_one: float32 [768], replicated, may hold values from -1.75 to 1.75
- w_query: bfloat16 [768, 768], replicated, may hold values from -0.3125 to 0.3125
- w_key: bfloat16 [768, 768], replicated, may hold values from -0.3125 to 0.3125
- w_value: bfloat16 [768, 768], replicated, may hold values from -0.21875 to 0.21875
- w_out: bfloat16 [768, 768], replicated, may hold values from -0.875 to 0.875
- gain_two: float32 [768], replicated, may hold values from 0.5 to 1.5
- bias_two: float32 [768], replicated, may hold values from -1.75 to 1.75
- w_up: bfloat16 [768, 3072], replicated, may hold values from -0.21875 to 0.21875
- w_down: bfloat16 [3072, 768], replicated, may hold values from -0.109375 to 0.109375
- cotangent: bfloat16 [4, 2048, 768], P('seq', 'ctx'), may hold values from -6 to 6
- cluster_ids: int32 [4, 2048, 12], P('seq', 'ctx'), may hold values from 0 to 99, as said below
- top_keys: int32 [4, 12, 100, 32], P('seq'), may hold values from 0 to 2047, as said below
Outputs:
- output: float32 [4, 2048, 768], P('seq', 'ctx')
- input_grad: float32 [4, 2048, 768], P('seq', 'ctx')
- grad_gain_one: float32 [768], P('ctx')
- grad_bias_one: float32 [768], P('ctx')
- grad_query: float32 [768, 768], P('ctx')
- grad_key: float32 [768, 768], P('ctx')
- grad_value: float32 [768, 768], P('ctx')
- grad_out: float32 [768, 768], P('ctx')
- grad_gain_two: float32 [768], P('ctx')
- grad_bias_two: float32 [768], P('ctx')
- grad_up: float32 [768, 3072], P('ctx')
- down_weight_gradient: float32 [3072, 768], P('ctx')
The draws below stay inside these ranges and needn't reach their ends.
Inputs may be any that keep to these rules, and one draw needn't show every extreme that they name: `cluster_ids`: every one of the 100 clusters of every head of every sequence holds one token or more. `top_keys`: the 32 positions of one cluster are distinct; the t-th lies in the t-th of 32 equal ranges of the sequence.
All inputs are finite; a program needn't handle non-finite values.
Results may differ from the reference program's by a relative error of at most 0.017.
Values may be sent and summed in bfloat16 or wider, within the bound.
No kernel may reach another device: no remote copies, remote signals or barrier semaphores. Data moves between devices by JAX's collectives and lax.ppermute only.
A program may use at most 192 MiB of HBM per device.

```python
import math
import jax
import jax.numpy as jnp
from jax import lax

D = 768
HEADS = 12
HEAD_DIM = 64
FF = 3072
CLUSTERS = 100
TOPK = 32
LEN = 2048
SEQS = 4


def draw_cluster_ids(key, part):
    key = jax.random.fold_in(key, 11)
    keys = jax.random.split(key, 5)
    shape = (SEQS, LEN, HEADS)
    first = jax.random.randint(keys[0], shape, 0, CLUSTERS)
    second = jax.random.randint(keys[1], shape, 0, CLUSTERS)
    third = jax.random.randint(keys[2], shape, 0, CLUSTERS)
    base = jnp.minimum(jnp.minimum(first, second), third)
    label_keys = jax.random.split(keys[3], SEQS * HEADS)
    labels = jax.vmap(lambda k: jax.random.permutation(k, CLUSTERS))(label_keys).reshape(SEQS, HEADS, CLUSTERS)
    seq_index = jnp.arange(SEQS)[:, None, None]
    head_index = jnp.arange(HEADS)[None, None, :]
    result = labels[seq_index, head_index, base]
    place_keys = jax.random.split(keys[4], SEQS * HEADS)
    places = jax.vmap(lambda k: jax.random.permutation(k, LEN)[:CLUSTERS])(place_keys).reshape(SEQS, HEADS, CLUSTERS)
    seq_fill = jnp.arange(SEQS)[:, None, None]
    head_fill = jnp.arange(HEADS)[None, :, None]
    values = jnp.broadcast_to(jnp.arange(CLUSTERS, dtype=jnp.int32)[None, None, :], (SEQS, HEADS, CLUSTERS))
    result = result.at[seq_fill, places, head_fill].set(values)
    return result.astype(jnp.int32)


def draw_top_keys(key, part):
    key = jax.random.fold_in(key, 23)
    stride = LEN // TOPK
    offsets = jax.random.randint(key, (SEQS, HEADS, CLUSTERS, TOPK), 0, stride)
    return (jnp.arange(TOPK, dtype=jnp.int32) * stride + offsets).astype(jnp.int32)


def block_scale(rng, shape, cuts, smallest, high):
    factor_of, own = 1.0, jax.random.fold_in(rng, 6)
    for position, shards_of in cuts:
        heights = jnp.exp(jax.random.uniform(jax.random.fold_in(own, position), (shards_of,), jnp.float32, smallest / len(cuts), high / len(cuts)))
        factor_of = factor_of * jnp.repeat(heights, shape[position] // shards_of).reshape([-1 if axis == position else 1 for axis in range(len(shape))])
    return factor_of


def scatter_about(rng, extent, deviation, limit, cuts=(), kind=jnp.bfloat16):
    level = block_scale(rng, extent, cuts, -0.22, 0.18) if cuts else 1.0
    array = jax.random.normal(rng, extent, jnp.float32) * deviation * level
    return jnp.minimum(jnp.maximum(array, -limit), limit).astype(kind)


def setup_inputs(seed: int = 0) -> dict:
    key_list = jax.random.split(jax.random.key(seed), 15)
    return {
        "tokens": scatter_about(key_list[0], (SEQS, LEN, D), 1.0, 6.0, ((0, 4), (1, 8))),
        "gain_one": jnp.clip(1.0 + 0.1 * jax.random.normal(key_list[1], (D,), jnp.float32), 0.5, 1.5),
        "bias_one": scatter_about(key_list[2], (D,), 0.3, 1.75, (), jnp.float32),
        "w_query": scatter_about(key_list[3], (D, D), (D // 2) ** -0.5, 0.3125),
        "w_key": scatter_about(key_list[4], (D, D), (D // 2) ** -0.5, 0.3125),
        "w_value": scatter_about(key_list[5], (D, D), D ** -0.5, 0.21875),
        "w_out": scatter_about(key_list[6], (D, D), (D // 16) ** -0.5, 0.875),
        "gain_two": jnp.clip(1.0 + 0.1 * jax.random.normal(key_list[7], (D,), jnp.float32), 0.5, 1.5),
        "bias_two": scatter_about(key_list[8], (D,), 0.3, 1.75, (), jnp.float32),
        "w_up": scatter_about(key_list[9], (D, FF), D ** -0.5, 0.21875),
        "w_down": scatter_about(key_list[10], (FF, D), FF ** -0.5, 0.109375),
        "cotangent": scatter_about(key_list[11], (SEQS, LEN, D), 1.0, 6.0, ((0, 4), (1, 8))),
        "cluster_ids": draw_cluster_ids(jax.random.fold_in(key_list[14], 71), 0),
        "top_keys": draw_top_keys(jax.random.fold_in(key_list[14], 71), 0),
    }


EPS = 1e-05
HIGH = lax.Precision.HIGHEST

@jax.custom_vjp
def low(v):
    return lax.optimization_barrier(v.astype(jnp.bfloat16)).astype(jnp.float32)

@jax.custom_vjp
def low_back(v):
    return v

def low_keep(v):
    return (low(v), None)

def low_pass(kept, grad):
    return (grad,)

def back_keep(v):
    return (v, None)

def back_low(kept, grad):
    return (low(grad),)
low.defvjp(low_keep, low_pass)
low_back.defvjp(back_keep, back_low)

def layer_norm(values, gain, bias):
    center = values - lax.optimization_barrier(jnp.mean(values, -1, keepdims=True))
    spread = lax.optimization_barrier(jnp.mean(center * center, -1, keepdims=True))
    return center * lax.rsqrt(spread + EPS) * gain + bias

def matmul(left_side, right):
    return jnp.dot(left_side, right, precision=HIGH, preferred_element_type=jnp.float32)

def softmax_last(scores):
    shifted = jnp.exp(scores - lax.optimization_barrier(jnp.max(scores, -1, keepdims=True)))
    return shifted / lax.optimization_barrier(jnp.sum(shifted, -1, keepdims=True))

def member_block(query_blk, cluster_blk, chosen, key_heads, value_heads, mass_rows, rest_rows):
    score_scale = 1.0 / math.sqrt(HEAD_DIM)
    head_index = jnp.arange(HEADS)[None, :]
    positions = chosen[head_index, cluster_blk]
    pos_heads = positions.transpose(1, 0, 2)
    key_member = jax.vmap(lambda table, index: table[index])(key_heads, pos_heads)
    value_member = jax.vmap(lambda table, index: table[index])(value_heads, pos_heads)
    scores = low_back(score_scale * jnp.einsum('bhd,hbkd->bhk', query_blk, key_member, precision=HIGH))
    weights = softmax_last(scores)
    member = low_back(jnp.einsum('bhk,hbkd->bhd', low(weights), value_member, precision=HIGH))
    mass_tok = mass_rows[head_index, cluster_blk]
    rest_tok = rest_rows[head_index, cluster_blk]
    attended = mass_tok[..., None] * member + rest_tok
    return attended.reshape(attended.shape[0], D)

def forward(params, inputs, cluster_group, chosen):
    gain_one, bias_one, w_query, w_key, w_value, w_out, gain_two, bias_two, w_up, w_down = params
    score_scale = 1.0 / math.sqrt(HEAD_DIM)
    normed_one = low(layer_norm(inputs, gain_one, bias_one))
    query = low(low_back(matmul(normed_one, w_query)))
    key = low(low_back(matmul(normed_one, w_key)))
    value = low(low_back(matmul(normed_one, w_value)))
    query_heads = query.reshape(LEN, HEADS, HEAD_DIM)
    key_heads = key.reshape(LEN, HEADS, HEAD_DIM)
    value_heads = value.reshape(LEN, HEADS, HEAD_DIM)
    onehot = (cluster_group[:, :, None] == jnp.arange(CLUSTERS)[None, None, :]).astype(jnp.float32)
    csum = low_back(jnp.einsum('lhc,lhd->hcd', onehot, query_heads, precision=HIGH))
    counts = lax.optimization_barrier(jnp.sum(onehot, 0))
    centroid = low(csum / jnp.maximum(counts, 1.0)[..., None])
    cscore = low_back(score_scale * jnp.einsum('hcd,lhd->hcl', centroid, key_heads, precision=HIGH))
    cprob = softmax_last(cscore)
    cprob_low = low(cprob)
    head_fill = jnp.arange(HEADS)[:, None, None]
    cluster_fill = jnp.arange(CLUSTERS)[None, :, None]
    topmask = jnp.zeros((HEADS, CLUSTERS, LEN), jnp.float32).at[head_fill, cluster_fill, chosen].set(1.0)
    rest_weights = cprob_low * (1.0 - topmask)
    rest_rows = low(low_back(jnp.einsum('hcl,lhd->hcd', rest_weights, value_heads, precision=HIGH)))
    prob_top = jnp.take_along_axis(cprob, chosen, axis=2)
    mass_rows = low(lax.optimization_barrier(jnp.sum(prob_top, -1)))
    key_major = key_heads.transpose(1, 0, 2)
    value_major = value_heads.transpose(1, 0, 2)
    block = min(512, LEN)
    count_blocks = LEN // block
    checked = jax.checkpoint(member_block)
    pieces = lax.map(lambda item: checked(item[0], item[1], chosen, key_major, value_major, mass_rows, rest_rows), (query_heads.reshape(count_blocks, block, HEADS, HEAD_DIM), cluster_group.reshape(count_blocks, block, HEADS)))
    attended = low(low_back(pieces.reshape(LEN, D)))
    attn = low_back(matmul(attended, w_out))
    middle = inputs + attn
    normed_two = low(layer_norm(middle, gain_two, bias_two))
    upper = low_back(matmul(normed_two, w_up))
    active = low(jax.nn.gelu(upper))
    return middle + matmul(active, w_down)

def reference(tokens, gain_one, bias_one, w_query, w_key, w_value, w_out, gain_two, bias_two, w_up, w_down, cotangent, cluster_ids, top_keys):
    params = tuple((p.astype(jnp.float32) for p in (gain_one, bias_one, w_query, w_key, w_value, w_out, gain_two, bias_two, w_up, w_down)))
    zeros = jax.tree.map(jnp.zeros_like, params)

    def one_seq(total, item):
        inputs, grad_out, cluster_group, chosen = item
        result, pull = jax.vjp(lambda p, v: forward(p, v, cluster_group, chosen), params, inputs.astype(jnp.float32))
        grads, grad_in = pull(grad_out.astype(jnp.float32))
        return (jax.tree.map(jnp.add, total, grads), (result, grad_in))
    total, (outputs, input_grads) = lax.scan(one_seq, zeros, (tokens, cotangent, cluster_ids, top_keys))
    return (outputs, input_grads, total[0], total[1], total[2], total[3], total[4], total[5], total[6], total[7], total[8], total[9])
```

```python
import functools
import math

import jax
import jax.numpy as jnp
import numpy as np
from jax import lax
from jax.experimental import pallas as pl
from jax.experimental.pallas import tpu as pltpu
from jax.sharding import PartitionSpec as P

EPS = 1e-05
NEG = -1e30
F32 = jnp.float32
BF = jnp.bfloat16
VMEM_BYTES = 52 * 1024 * 1024


def dot(a, b):
    return lax.dot_general(a, b, (((1,), (0,)), ((), ())), preferred_element_type=F32)


def dot_nt(a, b):
    return lax.dot_general(a, b, (((1,), (1,)), ((), ())), preferred_element_type=F32)


def dot_tn(a, b):
    return lax.dot_general(a, b, (((0,), (0,)), ((), ())), preferred_element_type=F32)


def low_half():
    return lax.broadcasted_iota(jnp.int32, (1, 128), 1) < 64


def norm_parts(x):
    center = x - jnp.mean(x, -1, keepdims=True)
    spread = jnp.mean(center * center, -1, keepdims=True)
    rstd = lax.rsqrt(spread + EPS)
    return center * rstd, rstd


def norm_back(d_normed, xhat, rstd, gain):
    d_hat = d_normed * gain
    first = jnp.mean(d_hat, -1, keepdims=True)
    second = jnp.mean(d_hat * xhat, -1, keepdims=True)
    return rstd * (d_hat - first - xhat * second)


def rows_at(index, size):
    return pl.ds(pl.multiple_of(index * size, size), size)


def call(body, grid, in_specs, out_specs, out_shape, scratch=(), aliases=None, flops=0, moved=0):
    return pl.pallas_call(
        body,
        grid_spec=pltpu.PrefetchScalarGridSpec(
            num_scalar_prefetch=1,
            grid=grid,
            in_specs=in_specs,
            out_specs=out_specs,
            scratch_shapes=list(scratch),
        ),
        out_shape=out_shape,
        input_output_aliases=aliases or {},
        compiler_params=pltpu.CompilerParams(
            vmem_limit_bytes=VMEM_BYTES, dimension_semantics=("arbitrary",) * len(grid)
        ),
        cost_estimate=pl.CostEstimate(flops=flops, bytes_accessed=moved, transcendentals=0),
    )


def full(shape):
    return pl.BlockSpec(shape, lambda *_: (0,) * len(shape))


ANY = pl.BlockSpec(memory_space=pl.ANY)


def qkv_body(first, info, xa, xb, gain, bias, wq, wk, wv, *rest):
    outs = rest if first else rest[3:]
    core = info[0]
    block = xa.shape[0]
    for rel, ref in enumerate((xa, xb)):
        rows = rows_at(core ^ rel, block)
        xhat, _ = norm_parts(ref[...].astype(F32))
        normed = (xhat * gain[...] + bias[...]).astype(BF)
        for weight, out in ((wq, outs[0]), (wk, outs[1]), (wv, outs[2])):
            out[rows, :] = dot(normed, weight[...]).astype(BF)
        if first:
            outs[3][rows, :] = normed


def qkv_call(info, xa, xb, gain, bias, wq, wk, wv, full_len, previous):
    block, width = xa.shape
    half = width // 2
    first = previous is None
    weight = pl.BlockSpec((width, half), lambda i, s: (0, s[0]))
    into = pl.BlockSpec((2 * block, half), lambda i, s: (s[1], 0))
    shape = jax.ShapeDtypeStruct((full_len, half), BF)
    in_specs = [full((block, width))] * 2 + [full((1, width))] * 2 + [weight] * 3
    out_specs, out_shape = [into] * 3, [shape] * 3
    operands = [xa, xb, gain, bias, wq, wk, wv]
    aliases = None
    if first:
        out_specs.append(full((2 * block, width)))
        out_shape.append(jax.ShapeDtypeStruct((2 * block, width), BF))
    else:
        in_specs += [ANY] * 3
        operands += list(previous)
        aliases = {8: 0, 9: 1, 10: 2}
    return call(
        functools.partial(qkv_body, first),
        (1,),
        in_specs,
        out_specs,
        out_shape,
        aliases=aliases,
        flops=12 * block * width * half,
        moved=6 * width * half,
    )(info, *operands)


def top_mask(offs, expand, omod):
    return dot(offs, expand) == omod


def fwd_body(scale, tile, info, ids, ids_own, offs, expand, omod, q_all, k_all, v_all, q_own,
             att, mem, prob, lse, rm, cen, cst):
    keys, values, queries = k_all[...], v_all[...], q_all[...]
    full_len = keys.shape[0]
    rows = offs.shape[2]
    own = q_own.shape[0]
    lo = low_half()
    lane = lax.broadcasted_iota(jnp.int32, (1, 128), 1)
    cluster = lax.broadcasted_iota(jnp.int32, (rows, full_len), 0)
    hits = [cluster == ids[0, e : e + 1, :] for e in range(2)]
    hot = [jnp.where(h, 1.0, 0.0) for h in hits]
    counts = [jnp.sum(h, axis=1, keepdims=True) for h in hot]
    sums = dot(jnp.concatenate([h.astype(BF) for h in hot], axis=0), queries)
    masks, packed = [], []
    for e in range(2):
        sel = lo if e == 0 else ~lo
        safe = jnp.maximum(counts[e], 1.0)
        center = jnp.where(sel, sums[e * rows : (e + 1) * rows] / safe, 0.0).astype(BF)
        score = dot_nt(center, keys) * scale
        top = jnp.max(score, axis=1, keepdims=True)
        grown = jnp.exp(score - top)
        total = jnp.sum(grown, axis=1, keepdims=True)
        cprob = grown / total
        mask = top_mask(offs[0, e], expand[...], omod[...])
        mass = jnp.sum(jnp.where(mask, cprob, 0.0), axis=1, keepdims=True).astype(BF).astype(F32)
        kept = jnp.where(mask, 0.0, cprob).astype(BF)
        rest = jnp.where(sel, dot(kept, values), 0.0).astype(BF)
        wide = jnp.where(sel, mass, 0.0).astype(BF)
        packed.append(jnp.concatenate([rest, wide], axis=1))
        masks.append(jnp.where(mask, 1.0, 0.0).astype(BF))
        cen[0, e * rows : (e + 1) * rows, :] = center
        cst[0, e * rows : (e + 1) * rows, :] = jnp.where(
            lane == 0, top + jnp.log(total), jnp.where(lane == 1, safe, mass)
        )
    both = jnp.concatenate(packed, axis=0)
    rm[0] = both
    cluster_own = lax.broadcasted_iota(jnp.int32, (rows, own), 0)
    hot_own = [
        jnp.where(cluster_own == ids_own[0, e : e + 1, :], 1.0, 0.0).astype(BF) for e in range(2)
    ]
    token = dot_tn(jnp.concatenate(hot_own, axis=0), both)
    for t in range(own // tile):
        part = slice(t * tile, (t + 1) * tile)
        members, stats = [], []
        for e in range(2):
            sel = lo if e == 0 else ~lo
            query = jnp.where(sel, q_own[part, :], jnp.zeros((), BF))
            score = dot_nt(query, keys) * scale
            mask = dot_tn(hot_own[e][:, part], masks[e])
            score = jnp.where(mask > 0.5, score, NEG)
            top = jnp.max(score, axis=1, keepdims=True)
            grown = jnp.exp(score - top)
            total = jnp.sum(grown, axis=1, keepdims=True)
            weights = (grown * (1.0 / total)).astype(BF)
            prob[e, part, :] = weights
            members.append(dot(weights, values))
            stats.append(top + jnp.log(total))
        member = jnp.where(lo, members[0], members[1])
        mem[part, :] = member
        att[part, :] = (token[part, 128:] * member + token[part, :128]).astype(BF)
        table = jnp.where(lane == 0, stats[0], jnp.where(lane == 1, stats[1], 0.0))
        lse[0, :, part] = table.T[:8]


def ffn_body(info, x, cot, att_mine, att_other, wo_mine, wo_other, gain, bias, w_up, w_down,
             out, d_mid, d_attn, da_mine, da_other, normed_out, act_out, du_mine, du_send, vecs,
             mid_ref, n2_ref, acc, dacc):
    step = pl.program_id(0)
    steps = pl.num_programs(0)

    @pl.when(step == 0)
    def _():
        mid = x[...].astype(F32) + dot(att_mine[...], wo_mine[...]) + dot(att_other[...], wo_other[...])
        mid_ref[...] = mid
        xhat, _ = norm_parts(mid)
        normed = (xhat * gain[...] + bias[...]).astype(BF)
        n2_ref[...] = normed
        normed_out[...] = normed
        acc[...] = mid
        dacc[...] = jnp.zeros_like(dacc)

    upper = dot(n2_ref[...], w_up[...])
    c0 = math.sqrt(2.0 / math.pi)
    square = upper * upper
    tanh = jnp.tanh(c0 * (upper + 0.044715 * square * upper))
    cdf = 0.5 * (1.0 + tanh)
    active = (upper * cdf).astype(BF)
    act_out[...] = active
    acc[...] += dot(active, w_down[...])
    slope = cdf + 0.5 * upper * (1.0 - tanh * tanh) * (c0 * (1.0 + 3 * 0.044715 * square))
    d_upper = (dot_nt(cot[...], w_down[...]) * slope).astype(BF)
    half = d_upper.shape[1] // 2
    first = info[0] == 0
    du_mine[0] = jnp.where(first, d_upper[:, :half], d_upper[:, half:])
    du_send[0] = jnp.where(first, d_upper[:, half:], d_upper[:, :half])
    dacc[...] += dot_nt(d_upper, w_up[...])

    @pl.when(step == steps - 1)
    def _():
        out[...] = acc[...]
        xhat, rstd = norm_parts(mid_ref[...])
        d_normed = dacc[...]
        vecs[...] = jnp.concatenate(
            [
                jnp.sum(d_normed * xhat, axis=0, keepdims=True),
                jnp.sum(d_normed, axis=0, keepdims=True),
                jnp.zeros((6, d_normed.shape[1]), F32),
            ],
            axis=0,
        )
        grad = cot[...].astype(F32) + norm_back(d_normed, xhat, rstd, gain[...])
        d_mid[...] = grad
        low = grad.astype(BF)
        d_attn[...] = low
        da_mine[...] = dot_nt(low, wo_mine[...]).astype(BF)
        da_other[...] = dot_nt(low, wo_other[...]).astype(BF)


def join_body(info, mine, other, mem, joined, rows_out):
    core = info[0]
    block = mine.shape[0]
    lo = low_half()
    lane = lax.broadcasted_iota(jnp.int32, (1, 128), 1)
    for rel, ref in enumerate((mine, other)):
        rows = rows_at(core ^ rel, block)
        joined[rows, :] = ref[...]
        for p in range(mine.shape[1] // 128):
            part = slice(p * 128, (p + 1) * 128)
            product = ref[:, part].astype(F32) * mem[rows, part]
            first = jnp.sum(jnp.where(lo, product, 0.0), axis=1, keepdims=True)
            second = jnp.sum(jnp.where(lo, 0.0, product), axis=1, keepdims=True)
            table = jnp.where(lane == 0, first, jnp.where(lane == 1, second, 0.0))
            rows_out[p, :, rows] = table.T[:8]


def query_body(scale, tile, info, ids_own, datt, rm, prob, k_all, v_all, dq):
    keys, values = k_all[...], v_all[...]
    own = datt.shape[0]
    rows = rm.shape[1] // 2
    lo = low_half()
    cluster_own = lax.broadcasted_iota(jnp.int32, (rows, own), 0)
    hot_own = [
        jnp.where(cluster_own == ids_own[0, e : e + 1, :], 1.0, 0.0).astype(BF) for e in range(2)
    ]
    mass = dot_tn(jnp.concatenate(hot_own, axis=0), rm[0, :, 128:])
    d_member = (mass * datt[...].astype(F32)).astype(BF)
    for t in range(own // tile):
        part = slice(t * tile, (t + 1) * tile)
        found = []
        for e in range(2):
            sel = lo if e == 0 else ~lo
            grad = jnp.where(sel, d_member[part], jnp.zeros((), BF))
            d_prob = dot_nt(grad, values)
            weights = prob[e, part, :].astype(F32)
            moved = weights * d_prob
            d_score = (moved - weights * jnp.sum(moved, axis=1, keepdims=True)).astype(BF)
            found.append(dot(d_score, keys))
        dq[part, :] = jnp.where(lo, found[0], found[1]) * scale


def key_body(scale, slots, tile, info, ids, ids_own, offs, expand, omod, expand_own, omod_own,
             q_all, k_all, v_all, k_own, v_own, rm, cen, cst, dqm, *rest):
    datts, lses, dmasses = rest[:slots], rest[slots : 2 * slots], rest[2 * slots : 3 * slots]
    dq, dk, dv, datt, stat, d_mem, dcs = rest[3 * slots :]
    place = info[1]
    own = k_own.shape[0]
    keys, values, queries = k_all[...], v_all[...], q_all[...]
    full_len = keys.shape[0]
    rows = offs.shape[2]
    lo = low_half()
    for s in range(slots):
        at = lax.rem(place - s + slots, slots)
        datt[rows_at(at, own), :] = datts[s][...]
        stat[0, :, rows_at(at, own)] = lses[s][0]
        stat[1, :, rows_at(at, own)] = dmasses[s][0]
    cluster = lax.broadcasted_iota(jnp.int32, (rows, full_len), 0)
    hits = [cluster == ids[0, e : e + 1, :] for e in range(2)]
    hot = [jnp.where(h, 1.0, 0.0).astype(BF) for h in hits]
    hot_both = jnp.concatenate(hot, axis=0)
    d_rest_both = dot(hot_both, datt[...])
    mass_token = dot_tn(hot_both, rm[0, :, 128:])
    d_mem[...] = (mass_token * datt[...].astype(F32)).astype(BF)
    d_sums, rests, keeps, mass_rows = [], [], [], []
    for e in range(2):
        sel = lo if e == 0 else ~lo
        part = slice(e * rows, (e + 1) * rows)
        log_total, safe, mass = cst[0, part, 0:1], cst[0, part, 1:2], cst[0, part, 2:3]
        mass_rows.append(jnp.sum(jnp.where(hits[e], mass, 0.0), axis=0, keepdims=True))
        d_rest = jnp.where(sel, d_rest_both[part], 0.0).astype(BF)
        d_mass = jnp.sum(jnp.where(hits[e], stat[1, e : e + 1, :], 0.0), axis=1, keepdims=True)
        center = cen[0, part, :]
        cprob = jnp.exp(dot_nt(center, keys) * scale - log_total)
        mask = top_mask(offs[0, e], expand[...], omod[...])
        d_prob = jnp.where(mask, d_mass, dot_nt(d_rest, values))
        moved = cprob * d_prob
        d_score = (moved - cprob * jnp.sum(moved, axis=1, keepdims=True)).astype(BF)
        dcs[0, part, :] = d_score
        dcs[1, part, :] = jnp.where(mask, 0.0, cprob).astype(BF)
        d_center = jnp.where(sel, dot(d_score, keys) * (scale / safe), 0.0)
        d_sums.append(d_center.astype(BF))
        rests.append(d_rest)
    cluster_own = lax.broadcasted_iota(jnp.int32, (rows, own), 0)
    hot_own = jnp.concatenate(
        [
            jnp.where(cluster_own == ids_own[0, e : e + 1, :], 1.0, 0.0).astype(BF)
            for e in range(2)
        ],
        axis=0,
    )
    dq[...] = (dqm[...] + dot_tn(hot_own, jnp.concatenate(d_sums, axis=0))).astype(BF)
    columns = rows_at(place, own)
    d_key = dot_tn(dcs[0, :, columns], cen[0])
    d_value = dot_tn(dcs[1, :, columns], jnp.concatenate(rests, axis=0))
    masks_own = [
        jnp.where(top_mask(offs[0, e], expand_own[...], omod_own[...]), 1.0, 0.0).astype(BF)
        for e in range(2)
    ]
    key_sides = [jnp.where(lo if e == 0 else ~lo, k_own[...], jnp.zeros((), BF)) for e in range(2)]
    value_sides = [
        jnp.where(lo if e == 0 else ~lo, v_own[...], jnp.zeros((), BF)) for e in range(2)
    ]
    dks, dvs = [0.0, 0.0], [0.0, 0.0]
    for t in range(full_len // tile):
        part = slice(t * tile, (t + 1) * tile)
        grad = d_mem[part, :]
        query = queries[part]
        for e in range(2):
            score = dot_nt(key_sides[e], query) * scale
            mask = dot_tn(masks_own[e], hot[e][:, part])
            weights = jnp.exp(jnp.where(mask > 0.5, score - stat[0, e : e + 1, part], NEG))
            d_prob = dot_nt(value_sides[e], grad)
            delta = mass_rows[e][:, part] * stat[1, e : e + 1, part]
            d_score = (weights * (d_prob - delta)).astype(BF)
            dvs[e] += dot(weights.astype(BF), grad)
            dks[e] += dot(d_score, query)
    dk[...] = ((jnp.where(lo, dks[0], dks[1]) + d_key) * scale).astype(BF)
    dv[...] = (jnp.where(lo, dvs[0], dvs[1]) + d_value).astype(BF)


def emit_chunks(info, flat, outs, places, q_count, per):
    core, place, mine = info[0], info[1], info[2]
    for r in range(q_count):
        rows = rows_at(mine ^ r, per)
        for rel in range(2):
            for s in range(places):
                at = lax.rem(place + s, places)
                outs[2 * r + rel][s] = flat[at, core ^ rel, rows, :]


def store_rows(flat, value, row, chunk):
    for owner in range(value.shape[0] // chunk):
        flat[owner // 2, owner % 2, row : row + chunk, :] = value[
            owner * chunk : (owner + 1) * chunk
        ].astype(BF)


def store_vecs(flat, vecs, row):
    half = vecs.shape[1] // 2
    lines = jnp.concatenate(
        [vecs[0:1, :half], vecs[0:1, half:], vecs[1:2, :half], vecs[1:2, half:]]
        + [jnp.zeros((12, half), F32)],
        axis=0,
    ).astype(BF)
    for z in range(flat.shape[0]):
        for c in range(2):
            flat[z, c, row : row + 16, :] = lines


def ffn_grad_body(places, q_count, per, info, n_mine, n_other, du_mine, du_other, act_mine, act_other,
                  cot_mine, cot_other, att_mine, att_other, da_mine, da_other, vecs, *rest):
    outs, (flat,) = rest[:-1], rest[-1:]
    core = info[0]
    width = n_mine.shape[1]
    chunk = width // (2 * places)
    step_count = du_mine.shape[0]
    hidden = act_mine.shape[1]
    down_chunk = hidden // (2 * places)
    block = n_mine.shape[0]
    n_t = [n_mine[...].T, n_other[...].T]
    for f in range(step_count):
        up = dot(n_t[0], du_mine[f]) + dot(n_t[1], du_other[f])
        store_rows(flat, up, f * chunk, chunk)
    base = step_count * chunk
    span = hidden // step_count
    for f in range(step_count):
        part = slice(f * span, (f + 1) * span)
        down = dot_tn(act_mine[:, part], cot_mine[...]) + dot_tn(act_other[:, part], cot_other[...])
        for i in range(span // down_chunk):
            owner = f * (span // down_chunk) + i
            flat[owner // 2, owner % 2, base : base + down_chunk, :] = down[
                i * down_chunk : (i + 1) * down_chunk
            ].astype(BF)
    base += down_chunk
    mine_rows, other_rows = rows_at(core, block), rows_at(1 - core, block)
    halves = []
    for ref in (att_mine, att_other):
        halves.append(
            dot_tn(ref[mine_rows, :], da_mine[...]) + dot_tn(ref[other_rows, :], da_other[...])
        )
    first = core == 0
    store_rows(
        flat,
        jnp.concatenate(
            [jnp.where(first, halves[0], halves[1]), jnp.where(first, halves[1], halves[0])], axis=0
        ),
        base,
        chunk,
    )
    base += chunk
    store_vecs(flat, vecs[...], base)
    emit_chunks(info, flat, outs, places, q_count, per)


def qkv_grad_body(places, q_count, per, info, normed, dq, dk, dv, wq, wk, wv, xa, xb, *rest):
    dn_mine, dn_send = rest[0], rest[1]
    outs, flat = rest[2:-1], rest[-1]
    core = info[0]
    block, width = xa.shape
    chunk = width // (2 * places)
    n_t = normed[...].T
    for i, ref in enumerate((dq, dk, dv)):
        store_rows(flat, dot(n_t, ref[...]), i * chunk, chunk)
    gains, biases = 0.0, 0.0
    for rel, (ref, out) in enumerate(((xa, dn_mine), (xb, dn_send))):
        rows = rows_at(core ^ rel, block)
        d_normed = (
            dot_nt(dq[rows, :], wq[...]) + dot_nt(dk[rows, :], wk[...]) + dot_nt(dv[rows, :], wv[...])
        )
        out[...] = d_normed
        xhat, _ = norm_parts(ref[...].astype(F32))
        gains += jnp.sum(d_normed * xhat, axis=0, keepdims=True)
        biases += jnp.sum(d_normed, axis=0, keepdims=True)
    store_vecs(flat, jnp.concatenate([gains, biases], axis=0), 3 * chunk)
    emit_chunks(info, flat, outs, places, q_count, per)


def input_body(info, x, gain, dn_mine, dn_other, d_mid, out):
    xhat, rstd = norm_parts(x[...].astype(F32))
    out[...] = d_mid[...] + norm_back(dn_mine[...] + dn_other[...], xhat, rstd, gain[...])


def gather_flat(info, mine, other, flat, per):
    own = info[2]
    for r in range(len(mine)):
        rows = rows_at(own ^ r, per)
        flat[0, rows, :] = mine[r][...]
        flat[1, rows, :] = other[r][...]


def ffn_out_body(q_count, per, info, *rest):
    mine, other = rest[:q_count], rest[q_count : 2 * q_count]
    up, down, out, vec, flat = rest[2 * q_count :]
    gather_flat(info, mine, other, flat, per)
    core = info[0]
    half = flat.shape[2]
    chunk = up.shape[0]
    steps = up.shape[1] // (2 * half)
    for c in range(2):
        src = core ^ c
        for f in range(steps):
            at = (2 * f + c) * half
            up[:, at : at + half] = flat[src, f * chunk : (f + 1) * chunk, :].astype(F32)
        base = steps * chunk
        down[:, c * half : (c + 1) * half] = flat[src, base : base + down.shape[0], :].astype(F32)
        base += down.shape[0]
        out[:, c * half : (c + 1) * half] = flat[src, base : base + chunk, :].astype(F32)
        base += chunk
    vec[...] = flat[0, base : base + 16, :].astype(F32) + flat[1, base : base + 16, :].astype(F32)


def qkv_out_body(q_count, per, info, *rest):
    mine, other = rest[:q_count], rest[q_count : 2 * q_count]
    outs, vec, flat = rest[2 * q_count : 2 * q_count + 3], rest[-2], rest[-1]
    gather_flat(info, mine, other, flat, per)
    core = info[0]
    half = flat.shape[2]
    chunk = outs[0].shape[0]
    for c in range(2):
        src = core ^ c
        for i, out in enumerate(outs):
            out[:, c * half : (c + 1) * half] = flat[src, i * chunk : (i + 1) * chunk, :].astype(F32)
    base = 3 * chunk
    vec[...] = flat[0, base : base + 16, :].astype(F32) + flat[1, base : base + 16, :].astype(F32)


def per_device(tokens, gain_one, bias_one, w_query, w_key, w_value, w_out, gain_two, bias_two,
               w_up, w_down, cotangent, cluster_ids, top_keys):
    _, block, width = tokens.shape
    heads = cluster_ids.shape[2]
    clusters, chosen = top_keys.shape[2], top_keys.shape[3]
    ctx, q_count = lax.axis_size("ctx"), lax.axis_size("seq")
    places = ctx // 2
    index, mine = lax.axis_index("ctx"), lax.axis_index("seq")
    core, place = index % 2, index // 2
    full_len = block * ctx
    own = 2 * block
    half = width // 2
    hidden = w_up.shape[1]
    pairs = half // 128
    stride = full_len // chosen
    rows = -(-clusters // 128) * 128
    scale = 1.0 / math.sqrt(width // heads)
    info = jnp.stack([core, place, mine]).astype(jnp.int32)

    swap_to = [(i, i ^ 1) for i in range(ctx)]

    def swap(a):
        return lax.ppermute(a, "ctx", swap_to)

    def along(a, s):
        to = [(2 * z + c, 2 * ((z + s) % places) + c) for z in range(places) for c in range(2)]
        return lax.ppermute(a, "ctx", to)

    def across(a, r):
        return lax.ppermute(a, "seq", [(i, i ^ r) for i in range(q_count)])

    x, cot = tokens[0], cotangent[0]
    gain1, bias1 = gain_one[None], bias_one[None]
    gain2, bias2 = gain_two[None], bias_two[None]

    x_other = swap(x)
    came = [along(x, s) for s in range(1, places)]
    came_other = [swap(a) for a in came]
    cot_other = swap(cot)
    ids_all = lax.all_gather(cluster_ids[0].T, "ctx", axis=1, tiled=True)
    ids = lax.dynamic_slice_in_dim(ids_all, core * (heads // 2), heads // 2, 0)
    ids = ids.reshape(pairs, 2, full_len)
    offs = top_keys[0] - jnp.arange(chosen, dtype=jnp.int32) * stride
    offs = lax.dynamic_slice_in_dim(offs, core * (heads // 2), heads // 2, 0).astype(BF)
    offs = jnp.pad(offs, ((0, 0), (0, rows - clusters), (0, 0))).reshape(pairs, 2, rows, chosen)
    spots = np.arange(full_len)
    expand = jnp.asarray(spots[None] // stride == np.arange(chosen)[:, None], BF)
    omod = jnp.asarray(spots[None] % stride, F32)

    def slot(s):
        return info.at[1].set(lax.rem(place - s + places, places))

    query, key, value, normed = qkv_call(
        info, x, x_other, gain1, bias1, w_query, w_key, w_value, full_len, None
    )
    for s in range(1, places):
        query, key, value = qkv_call(
            slot(s), came[s - 1], came_other[s - 1], gain1, bias1, w_query, w_key, w_value,
            full_len, (query, key, value),
        )

    pair_all = pl.BlockSpec((full_len, 128), lambda p, s: (0, p))
    pair_own = pl.BlockSpec((own, 128), lambda p, s: (s[1], p))
    pair_loc = pl.BlockSpec((own, 128), lambda p, s: (0, p))
    ids_spec = pl.BlockSpec((1, 2, full_len), lambda p, s: (p, 0, 0))
    ids_own_spec = pl.BlockSpec((1, 2, own), lambda p, s: (p, 0, s[1]))
    offs_spec = pl.BlockSpec((1, 2, rows, chosen), lambda p, s: (p, 0, 0, 0))
    expand_own_spec = pl.BlockSpec((chosen, own), lambda p, s: (0, s[1]))
    omod_own_spec = pl.BlockSpec((1, own), lambda p, s: (0, s[1]))
    prob_spec = pl.BlockSpec((2, own, full_len), lambda p, s: (p, 0, 0))
    stat_spec = pl.BlockSpec((1, 8, own), lambda p, s: (p, 0, 0))
    rm_spec = pl.BlockSpec((1, 2 * rows, 256), lambda p, s: (p, 0, 0))
    cen_spec = pl.BlockSpec((1, 2 * rows, 128), lambda p, s: (p, 0, 0))
    sds = jax.ShapeDtypeStruct
    tile = min(256, own)

    att, mem, prob, lse, rm, cen, cst = call(
        functools.partial(fwd_body, scale, tile),
        (pairs,),
        [ids_spec, ids_own_spec, offs_spec, full((chosen, full_len)), full((1, full_len)),
         pair_all, pair_all, pair_all, pair_own],
        [pair_loc, pair_loc, prob_spec, stat_spec, rm_spec, cen_spec, cen_spec],
        [sds((own, half), BF), sds((own, half), F32), sds((2 * pairs, own, full_len), BF),
         sds((pairs, 8, own), F32), sds((pairs, 2 * rows, 256), BF),
         sds((pairs, 2 * rows, 128), BF), sds((pairs, 2 * rows, 128), F32)],
        flops=heads * own * full_len * 64 * 3,
        moved=own * full_len * heads,
    )(info, ids, ids, offs, expand, omod, query, key, value, query)

    att_other = swap(att)
    lse_all = [lse] + [along(lse, s) for s in range(1, places)]

    steps = hidden // width
    whole = full((block, width))
    att_spec = pl.BlockSpec((block, half), lambda f, s: (s[0], 0))
    out, d_mid, d_attn, da_mine, da_send, normed_two, act, du_mine, du_send, vecs_two = call(
        ffn_body,
        (steps,),
        [whole, whole, att_spec, att_spec,
         pl.BlockSpec((half, width), lambda f, s: (s[0], 0)),
         pl.BlockSpec((half, width), lambda f, s: (1 - s[0], 0)),
         full((1, width)), full((1, width)),
         pl.BlockSpec((width, width), lambda f, s: (0, f)),
         pl.BlockSpec((width, width), lambda f, s: (f, 0))],
        [whole, whole, whole, full((block, half)), full((block, half)), whole,
         pl.BlockSpec((block, width), lambda f, s: (0, f)),
         pl.BlockSpec((1, block, half), lambda f, s: (f, 0, 0)),
         pl.BlockSpec((1, block, half), lambda f, s: (f, 0, 0)),
         full((8, width))],
        [sds((block, width), F32), sds((block, width), F32), sds((block, width), BF),
         sds((block, half), BF), sds((block, half), BF), sds((block, width), BF),
         sds((block, hidden), BF), sds((steps, block, half), BF), sds((steps, block, half), BF),
         sds((8, width), F32)],
        scratch=[pltpu.VMEM((block, width), F32), pltpu.VMEM((block, width), BF),
                 pltpu.VMEM((block, width), F32), pltpu.VMEM((block, width), F32)],
        flops=8 * block * width * hidden,
        moved=4 * width * hidden,
    )(info, x, cot, att, att_other, w_out, w_out, gain2, bias2, w_up, w_down)

    datt, dmass = call(
        join_body,
        (1,),
        [full((block, half)), full((block, half)), full((own, half))],
        [full((own, half)), full((pairs, 8, own))],
        [sds((own, half), BF), sds((pairs, 8, own), F32)],
        moved=own * half * 8,
    )(info, da_mine, swap(da_send), mem)
    datt_all = [datt] + [along(datt, s) for s in range(1, places)]
    dmass_all = [dmass] + [along(dmass, s) for s in range(1, places)]

    dqm = call(
        functools.partial(query_body, scale, tile),
        (pairs,),
        [ids_own_spec, pair_loc, rm_spec, prob_spec, pair_all, pair_all],
        [pair_loc],
        [sds((own, half), F32)],
        flops=heads * own * full_len * 64 * 2,
        moved=own * full_len * heads,
    )(info, ids, datt, rm, prob, key, value)[0]

    chunk, down_chunk = width // ctx, hidden // ctx
    def padded(n):
        return -(-n // (16 * q_count)) * 16 * q_count

    ffn_rows = padded(steps * chunk + down_chunk + chunk + 16)
    per = ffn_rows // q_count
    cot_spec = pl.BlockSpec((block, half), lambda i, s: (0, s[0]))
    pieces = call(
        functools.partial(ffn_grad_body, places, q_count, per),
        (1,),
        [whole, whole, full((steps, block, half)), full((steps, block, half)),
         full((block, hidden)), full((block, hidden)), cot_spec, cot_spec,
         full((own, half)), full((own, half)), cot_spec, cot_spec, full((8, width))],
        [full((places, per, half))] * (2 * q_count),
        [sds((places, per, half), BF)] * (2 * q_count),
        scratch=[pltpu.VMEM((places, 2, ffn_rows, half), BF)],
        flops=4 * own * hidden * half + 2 * own * width * half,
        moved=2 * places * ffn_rows * half * 2,
    )(info, normed_two, swap(normed_two), du_mine, swap(du_send), act, swap(act), cot, cot_other,
      att, att_other, d_attn, swap(d_attn), vecs_two)

    def add(a, b):
        return (a.astype(F32) + b.astype(F32)).astype(BF)

    def reduce_seq(parts, bits):
        parts = dict(enumerate(parts))
        for bit in bits:
            sent = {r: across(parts[r], bit) for r in parts if r & bit}
            parts = {r: add(parts[r], sent[r | bit]) for r in parts if not r & bit}
        return parts[0]

    def reduce_along(whole_part):
        total = whole_part[0].astype(F32)
        for s in range(1, places):
            total = total + along(whole_part[s], s).astype(F32)
        return total.astype(BF)

    def spread_seq(part):
        return [part] + [across(part, r) for r in range(1, q_count)]

    bits = [1 << i for i in range((q_count - 1).bit_length())]

    def reduce_all(pieces):
        own_part = reduce_along(reduce_seq(pieces[0::2], bits))
        send_part = reduce_along(reduce_seq(pieces[1::2], bits[::-1]))
        return spread_seq(own_part) + spread_seq(swap(send_part))

    ffn_parts = reduce_all(pieces)

    dq, dk, dv = call(
        functools.partial(key_body, scale, places, min(512, full_len)),
        (pairs,),
        [ids_spec, ids_own_spec, offs_spec, full((chosen, full_len)), full((1, full_len)),
         expand_own_spec, omod_own_spec, pair_all, pair_all, pair_all, pair_own, pair_own,
         rm_spec, cen_spec, cen_spec, pair_loc] + [pair_loc] * places + [stat_spec] * (2 * places),
        [pair_loc] * 3,
        [sds((own, half), BF)] * 3,
        scratch=[pltpu.VMEM((full_len, 128), BF), pltpu.VMEM((2, 8, full_len), F32),
                 pltpu.VMEM((full_len, 128), BF), pltpu.VMEM((2, 2 * rows, full_len), BF)],
        flops=heads * own * full_len * 64 * 5,
        moved=own * full_len * 4,
    )(info, ids, ids, offs, expand, omod, expand, omod, query, key, value, key, value, rm, cen, cst,
      dqm, *datt_all, *lse_all, *dmass_all)

    qkv_rows = padded(3 * chunk + 16)
    per_one = qkv_rows // q_count
    weight = pl.BlockSpec((width, half), lambda i, s: (0, s[0]))
    dn_mine, dn_send, *pieces = call(
        functools.partial(qkv_grad_body, places, q_count, per_one),
        (1,),
        [full((own, width))] + [full((own, half))] * 3 + [weight] * 3 + [whole] * 2,
        [whole] * 2 + [full((places, per_one, half))] * (2 * q_count),
        [sds((block, width), F32)] * 2 + [sds((places, per_one, half), BF)] * (2 * q_count),
        scratch=[pltpu.VMEM((places, 2, qkv_rows, half), BF)],
        flops=12 * own * width * half,
        moved=2 * places * qkv_rows * half * 2,
    )(info, normed, dq, dk, dv, w_query, w_key, w_value, x, x_other)
    qkv_parts = reduce_all(pieces)

    input_grad = call(
        input_body,
        (1,),
        [whole, full((1, width)), whole, whole, whole],
        [whole],
        [sds((block, width), F32)],
        moved=block * width * 18,
    )(info, x, gain1, dn_mine, swap(dn_send), d_mid)[0]

    grad_up, grad_down, grad_out, vec_two = call(
        functools.partial(ffn_out_body, q_count, per),
        (1,),
        [full((per, half))] * (2 * q_count),
        [full((chunk, hidden)), full((down_chunk, width)), full((chunk, width)), full((16, half))],
        [sds((chunk, hidden), F32), sds((down_chunk, width), F32), sds((chunk, width), F32),
         sds((16, half), F32)],
        scratch=[pltpu.VMEM((2, ffn_rows, half), BF)],
        moved=ffn_rows * width * 6,
    )(info, *ffn_parts)
    grad_query, grad_key, grad_value, vec_one = call(
        functools.partial(qkv_out_body, q_count, per_one),
        (1,),
        [full((per_one, half))] * (2 * q_count),
        [full((chunk, width))] * 3 + [full((16, half))],
        [sds((chunk, width), F32)] * 3 + [sds((16, half), F32)],
        scratch=[pltpu.VMEM((2, qkv_rows, half), BF)],
        moved=qkv_rows * width * 6,
    )(info, *qkv_parts)

    def vectors(vec):
        both = vec[:4].reshape(2, width)
        cut = lax.dynamic_slice_in_dim(both, index * chunk, chunk, 1)
        return cut[0], cut[1]

    grad_gain_one, grad_bias_one = vectors(vec_one)
    grad_gain_two, grad_bias_two = vectors(vec_two)
    return (out[None], input_grad[None], grad_gain_one, grad_bias_one, grad_query, grad_key,
            grad_value, grad_out, grad_gain_two, grad_bias_two, grad_up, grad_down)


def solution(mesh):
    split = P("seq", "ctx", None)
    in_specs = (split,) + (P(),) * 10 + (split, split, P("seq", None, None, None))
    vec, mat = P("ctx"), P("ctx", None)
    out_specs = (split, split, vec, vec, mat, mat, mat, mat, vec, vec, mat, mat)
    return jax.shard_map(
        per_device, mesh=mesh, in_specs=in_specs, out_specs=out_specs, check_vma=False
    )
```

```python
import functools
import math

import jax
import jax.numpy as jnp
import numpy as np
from jax import lax
from jax.experimental import pallas as pl
from jax.experimental.pallas import tpu as pltpu
from jax.sharding import PartitionSpec as P

EPS = 1e-05
NEG = -1e30
F32 = jnp.float32
BF = jnp.bfloat16
COST = 0.03
ANY = pl.BlockSpec(memory_space=pl.ANY)
VMEM_BYTES = 7 * 1024 * 1024


def dot(a, b):
    return lax.dot_general(a, b, (((1,), (0,)), ((), ())), preferred_element_type=F32)


def dot_nt(a, b):
    return lax.dot_general(a, b, (((1,), (1,)), ((), ())), preferred_element_type=F32)


def dot_tn(a, b):
    return lax.dot_general(a, b, (((0,), (0,)), ((), ())), preferred_element_type=F32)


def low_half():
    return lax.broadcasted_iota(jnp.int32, (1, 128), 1) < 64


def norm_parts(x):
    center = x - jnp.mean(x, -1, keepdims=True)
    spread = jnp.mean(center * center, -1, keepdims=True)
    rstd = lax.rsqrt(spread + EPS)
    return center * rstd, rstd


def norm_back(d_normed, xhat, rstd, gain):
    d_hat = d_normed * gain
    first = jnp.mean(d_hat, -1, keepdims=True)
    second = jnp.mean(d_hat * xhat, -1, keepdims=True)
    return rstd * (d_hat - first - xhat * second)


def rows_at(index, size):
    return pl.ds(pl.multiple_of(index * size, size), size)


def call(body, in_views, out_views, out_shape, scratch=(), us=1.0, vmem=VMEM_BYTES, steps=None):
    views = list(in_views) + list(out_views)
    taken = 1 + len(in_views)

    def run(info, *args, deps=()):
        def kernel(*refs):
            scalars, arrays = refs[0], refs[1:taken] + refs[taken + len(deps) :]
            for step in range(steps or 1):
                seen = [
                    r if v is None else v(r, step, scalars)
                    for r, v in zip(arrays, views + [None] * len(scratch))
                ]
                if steps is None:
                    body(scalars, *seen)
                else:
                    body(step, scalars, *seen)

        return pl.pallas_call(
            kernel,
            in_specs=[pl.BlockSpec(memory_space=pltpu.SMEM)]
            + [pl.BlockSpec(memory_space=pltpu.VMEM)] * len(in_views)
            + [ANY] * len(deps),
            out_specs=[pl.BlockSpec(memory_space=pltpu.VMEM)] * len(out_views),
            out_shape=out_shape,
            scratch_shapes=list(scratch),
            compiler_params=pltpu.CompilerParams(vmem_limit_bytes=vmem),
            cost_estimate=pl.CostEstimate(
                flops=int(us * COST * 1.1e9), bytes_accessed=int(us * COST * 1e6), transcendentals=0
            ),
        )(info, *args, *deps)

    return run


def lanes(ref, p, info):
    return ref.at[:, p * 128 : (p + 1) * 128]


def lead(ref, p, info):
    return ref.at[p : p + 1]


def lead_two(ref, p, info):
    return ref.at[2 * p : 2 * p + 2]


def half_lanes(ref, p, info):
    half = ref.shape[1] // 2
    return ref.at[:, pl.ds(pl.multiple_of(info[0] * half + p * 128, 128), 128)]


def my_columns(ref, p, info):
    half = ref.shape[1] // 2
    return ref.at[:, pl.ds(pl.multiple_of(info[0] * half, 128), half)]


def my_rows(ref, p, info):
    return ref.at[rows_at(info[0], ref.shape[0] // 2), :]


def other_rows(ref, p, info):
    return ref.at[rows_at(1 - info[0], ref.shape[0] // 2), :]


def split3(x):
    first = x.astype(BF)
    left = x - first.astype(F32)
    second = left.astype(BF)
    return first, second, (left - second.astype(F32)).astype(BF)


def half_of(e):
    lo = low_half()
    return lo if e == 0 else ~lo


def spare(e):
    lane = lax.broadcasted_iota(jnp.int32, (1, 128), 1)
    base = 64 if e == 0 else 0
    return [lane == base + i for i in range(3)]


def spare_ones(e):
    marks = spare(e)
    return jnp.where(marks[0] | marks[1] | marks[2], 1.0, 0.0).astype(BF)


def hits_of(ids_row, rows):
    return lax.broadcasted_iota(jnp.int32, (rows, ids_row.shape[1]), 0) == ids_row


def as_hot(hits):
    return jnp.where(hits, 1.0, 0.0).astype(BF)


def top_offsets(tops, stride):
    lane = lax.broadcasted_iota(jnp.int32, tops.shape, 1)
    return (tops - lane * stride).astype(F32).astype(BF)


def top_mask(offs, own, stride, slot):
    shape = (offs.shape[1], own)
    lane = lax.broadcasted_iota(jnp.int32, shape, 1)
    ranges = (lane >> int(math.log2(stride))) + slot * (own // stride)
    expand = as_hot(ranges == lax.broadcasted_iota(jnp.int32, shape, 0))
    spot = (lax.broadcasted_iota(jnp.int32, (1, own), 1) & (stride - 1)).astype(F32)
    return dot(offs, expand) == spot


def top_mask_t(offs, own, stride, slot):
    shape = (own, offs.shape[1])
    key = lax.broadcasted_iota(jnp.int32, shape, 0)
    ranges = (key >> int(math.log2(stride))) + slot * (own // stride)
    expand = as_hot(ranges == lax.broadcasted_iota(jnp.int32, shape, 1))
    spot = (lax.broadcasted_iota(jnp.int32, (own, 1), 0) & (stride - 1)).astype(F32)
    return dot_nt(expand, offs) == spot


def chip_at(info, slot, slots):
    return lax.rem(info[1] - slot + slots, slots)


def pair_tops(tops, p, info, stride):
    _, rows, chosen = tops.shape
    first = info[0] * (tops.shape[0] // 2) + 2 * p
    return top_offsets(tops[pl.ds(first, 2)].reshape(2 * rows, chosen), stride)


def sequence_mask(tops, p, info, own, stride, slots):
    offs = pair_tops(tops, p, info, stride)
    masks = [top_mask(offs, own, stride, chip_at(info, s, slots)) for s in range(slots)]
    return jnp.concatenate(masks, axis=1)


def pair_ids(ids, p, info):
    return [ids[2 * p + e : 2 * p + e + 1, :] for e in range(2)]


def pair_rows(rows):
    row = lax.broadcasted_iota(jnp.int32, (2 * rows, 128), 0)
    lane = lax.broadcasted_iota(jnp.int32, (2 * rows, 128), 1)
    column = lax.broadcasted_iota(jnp.int32, (2 * rows, 1), 0)
    return (row < rows) == (lane < 64), column < rows


def pair_hot(lines, rows):
    return jnp.concatenate([as_hot(hits_of(line, rows)) for line in lines], axis=0)


def slot_body(slot, slots, scale, stride, p, info, xa, xb, gain, bias, wq, wk, wv, tops, *rest):
    first = slot == 0
    if first:
        q_out, k_out, v_out, csum, acc, den, top, prob, ids, n_out, normed = rest
        ids_own = ids
    else:
        ids_own, q_own, q_out, k_out, v_out, csum, acc, den, top, prob, ids, normed = rest
    rows = tops.shape[1]
    core = info[0]
    block = xa.shape[0] - 16
    own = 2 * block

    if p == 0:
        for rel, ref in enumerate((xa, xb)):
            at = rows_at(core ^ rel, block)
            xhat, _ = norm_parts(ref[:block, :].astype(F32))
            low = (xhat * gain[...][None] + bias[...][None]).astype(BF)
            normed[at, :] = low
            if first:
                n_out[at, :] = low
        lines = [ref[block:, :block].astype(F32) for ref in (xa, xb)]
        heads = tops.shape[0] // 2
        lines = [jnp.where(core == 0, a[:heads], a[heads : 2 * heads]) for a in lines]
        lines = jnp.where(
            core == 0,
            jnp.concatenate(lines, axis=1),
            jnp.concatenate(lines[::-1], axis=1),
        )
        ids[:heads, :] = lines.astype(jnp.int32)

    weights = jnp.concatenate([wq[...], wk[...], wv[...]], axis=1)
    made = dot(normed[...], weights).astype(BF)
    query, key, value = made[:, :128], made[:, 128:256], made[:, 256:]
    q_out[...] = query
    k_out[...] = key
    v_out[...] = value
    key_t = key.T
    asked = (query if first else q_own[...]) * jnp.asarray(scale, BF)
    peaks, outs = [], []
    one = jnp.ones((), BF)
    hot = pair_hot(pair_ids(ids, p, info), rows)
    hot_own = (hot if first else pair_hot(pair_ids(ids_own, p, info), rows)).T
    count = jnp.sum(hot.astype(F32), axis=1, keepdims=True)
    csum[0] = jnp.where(pair_rows(rows)[0], dot(hot, query), count)
    mask = top_mask(pair_tops(tops, p, info, stride), own, stride, chip_at(info, slot, slots))
    bars = jnp.where(mask, 0.0, NEG).astype(BF)
    for e in range(2):
        sel = half_of(e)
        bar = bars[e * rows : (e + 1) * rows]
        right = jnp.concatenate([key_t, bar], axis=0)
        member_of = hot_own[:, e * rows : (e + 1) * rows]
        left = jnp.concatenate([jnp.where(sel, asked, jnp.zeros((), BF)), member_of], axis=1)
        score = dot(left, right)
        peak = jnp.max(score, axis=1, keepdims=True)
        grown = jnp.exp(score - peak).astype(BF)
        prob[e] = grown
        peaks.append(peak)
        outs.append(dot(grown, jnp.where(sel, value, one)))
    lo = low_half()
    acc[...] = jnp.where(lo, outs[0], outs[1])
    den[...] = pltpu.roll(jnp.where(lo, outs[1], outs[0]), 64, 1)
    top[...] = jnp.where(lo, peaks[0], peaks[1])


def cluster_body(scale, stride, slots, p, info, ids_own, keys_top, *rest):
    ks, vs, csums, accs, dens, tops = (rest[i * slots : (i + 1) * slots] for i in range(6))
    att, mem, lse, lse_col, rm, cen, cst = rest[6 * slots :]
    keys = jnp.concatenate([k[...] for k in ks], axis=0)
    values = jnp.concatenate([v[...] for v in vs], axis=0)
    own = ks[0].shape[0]
    rows = keys_top.shape[1]
    lo = low_half()
    lane = lax.broadcasted_iota(jnp.int32, (1, 128), 1)
    sel, upper = pair_rows(rows)
    sums = csums[0][0]
    for c in csums[1:]:
        sums = sums + c[0]
    safe = jnp.maximum(jnp.where(upper, sums[:, 64:65], sums[:, 0:1]), 1.0)
    center = jnp.where(sel, sums / safe, 0.0).astype(BF)
    score = dot_nt(center * jnp.asarray(scale, BF), keys)
    peak = jnp.max(score, axis=1, keepdims=True)
    grown = jnp.exp(score - peak)
    total = jnp.sum(grown, axis=1, keepdims=True)
    inverse = 1.0 / total
    mask = sequence_mask(keys_top, p, info, own, stride, slots)
    mass = (jnp.sum(jnp.where(mask, grown, 0.0), axis=1, keepdims=True) * inverse).astype(BF)
    kept = jnp.where(mask, 0.0, grown).astype(BF)
    attended = jnp.where(sel, dot(kept, values) * inverse, 0.0).astype(BF)
    wide = jnp.where(sel, mass, jnp.zeros((), BF))
    both = jnp.concatenate([attended, wide], axis=1)
    cen[0] = center
    cst[0] = jnp.where(lane == 0, peak + jnp.log(total), safe)
    rm[0] = both
    hot = pair_hot(pair_ids(ids_own, p, info), rows)
    token = dot_tn(hot, both)
    peak = tops[0][...]
    for t in tops[1:]:
        peak = jnp.maximum(peak, t[...])
    total, member = 0.0, 0.0
    for t, d, a in zip(tops, dens, accs):
        weight = jnp.exp(t[...] - peak)
        total += weight * d[...]
        member += weight * a[...]
    member = member / total
    log_total = peak + jnp.log(total)
    lse_col[...] = log_total
    turned = log_total.T
    lse[0] = jnp.concatenate([turned[0:1], turned[64:65], jnp.zeros((6, own), F32)], axis=0)
    mem[...] = member
    att[...] = (token[:, 128:] * member + token[:, :128]).astype(BF)


def ffn_body(steps, step, info, x, cot, att_mine, att_other, wo_mine, wo_other, gain, bias, w_up,
             w_down, out, d_mid, d_attn, da_mine, da_other, normed_out, act_out, du_mine, du_send,
             vecs, acc, dacc):
    if step == 0:
        mid = x[...].astype(F32) + dot(att_mine[...], wo_mine[...]) + dot(att_other[...], wo_other[...])
        d_mid[...] = mid
        xhat, _ = norm_parts(mid)
        normed_out[...] = (xhat * gain[...][None] + bias[...][None]).astype(BF)
    upper = dot(normed_out[...], w_up[...])
    c0 = math.sqrt(2.0 / math.pi)
    square = upper * upper
    tanh = jnp.tanh(c0 * (upper + 0.044715 * square * upper))
    cdf = 0.5 * (1.0 + tanh)
    active = (upper * cdf).astype(BF)
    act_out[...] = active
    more = dot(active, w_down[...])
    acc[...] = more + (d_mid[...] if step == 0 else acc[...])
    slope = cdf + 0.5 * upper * (1.0 - tanh * tanh) * (c0 * (1.0 + 3 * 0.044715 * square))
    d_upper = (dot_nt(cot[...], w_down[...]) * slope).astype(BF)
    half = d_upper.shape[1] // 2
    first = info[0] == 0
    du_mine[0] = jnp.where(first, d_upper[:, :half], d_upper[:, half:])
    du_send[0] = jnp.where(first, d_upper[:, half:], d_upper[:, :half])
    more = dot_nt(d_upper, w_up[...])
    dacc[...] = more if step == 0 else dacc[...] + more
    if step == steps - 1:
        out[...] = acc[...]
        xhat, rstd = norm_parts(d_mid[...])
        d_normed = dacc[...]
        vecs[...] = jnp.concatenate(
            [
                jnp.sum(d_normed * xhat, axis=0, keepdims=True),
                jnp.sum(d_normed, axis=0, keepdims=True),
                jnp.zeros((6, d_normed.shape[1]), F32),
            ],
            axis=0,
        )
        grad = cot[...].astype(F32) + norm_back(d_normed, xhat, rstd, gain[...][None])
        d_mid[...] = grad
        low = grad.astype(BF)
        d_attn[...] = low
        da_mine[...] = dot_nt(low, wo_mine[...]).astype(BF)
        da_other[...] = dot_nt(low, wo_other[...]).astype(BF)


def join_body(info, mine, other, mem, lse, joined):
    core = info[0]
    block, half = mine.shape
    lo = low_half()
    lane = lax.broadcasted_iota(jnp.int32, (1, 128), 1)
    found = {}
    for rel, ref in enumerate((mine, other)):
        at = rows_at(core ^ rel, block)
        joined[at, :] = ref[...]
        for p in range(half // 128):
            part = slice(p * 128, (p + 1) * 128)
            product = ref[:, part].astype(F32) * mem[at, part]
            first = jnp.sum(jnp.where(lo, product, 0.0), axis=1, keepdims=True)
            second = jnp.sum(jnp.where(lo, 0.0, product), axis=1, keepdims=True)
            table = jnp.where(lane == 0, first, jnp.where(lane == 1, second, 0.0)).T
            stat = lse[p, :, at]
            for e in range(2):
                found[p, e, rel] = split3(table[e : e + 1])[:2] + split3(-stat[e : e + 1])
    lines = []
    for p in range(half // 128):
        for e in range(2):
            for rel in range(2):
                lines += [line.astype(F32) for line in found[p, e, rel]]
    lines.append(jnp.zeros((64 - len(lines), block), F32))
    table = jnp.concatenate(lines, axis=0).astype(BF)
    joined[2 * block :, :] = jnp.concatenate(
        [table, jnp.zeros((64, half - block), BF)], axis=1
    )


def query_body(scale, slots, p, info, ids_own, message, mem, rm, lse_col, *rest):
    tops, probs, ks, vs = (rest[i * slots : (i + 1) * slots] for i in range(4))
    dq = rest[4 * slots]
    own = mem.shape[0]
    rows = rm.shape[1] // 2
    lo = low_half()
    hot = pair_hot(pair_ids(ids_own, p, info), rows)
    mass = dot_tn(hot, rm[0, :, 128:])
    grad = message[:own, p * 128 : (p + 1) * 128].astype(F32)
    product = grad * mem[...]
    d_member = (mass * grad).astype(BF)
    lefts = []
    for e in range(2):
        sel = half_of(e)
        other = 0 if e == 0 else 64
        delta = mass[:, other : other + 1] * jnp.sum(
            jnp.where(sel, product, 0.0), axis=1, keepdims=True
        )
        left = jnp.where(sel, d_member, jnp.zeros((), BF))
        for mark, term in zip(spare(e), split3(-delta)):
            left = jnp.where(mark, term, left)
        lefts.append(left)
    total = 0.0
    for s in range(slots):
        d_scores = []
        for e in range(2):
            right = jnp.where(half_of(e), vs[s][...], spare_ones(e))
            moved = dot_nt(lefts[e], right)
            d_scores.append((probs[s][e].astype(F32) * moved).astype(BF))
        made = dot(jnp.concatenate(d_scores, axis=0), ks[s][...])
        total += jnp.exp(tops[s][...] - lse_col[...]) * jnp.where(lo, made[:own], made[own:])
    dq[...] = total * scale


def key_body(scale, stride, p, info, k_own, v_own, query, message, ids, tops, rm, dk, dv, dr):
    core = info[0]
    own = k_own.shape[0]
    block = own // 2
    rows = rm.shape[1] // 2
    lo = low_half()
    picked = message[own:, :block].astype(F32)[20 * p : 20 * p + 20]
    datt = message[:own, p * 128 : (p + 1) * 128]

    def term(e, i):
        a, b = picked[10 * e + i : 10 * e + i + 1], picked[10 * e + 5 + i : 10 * e + 6 + i]
        return jnp.where(
            core == 0, jnp.concatenate([a, b], axis=1), jnp.concatenate([b, a], axis=1)
        )

    hot = [as_hot(hits_of(line, rows)) for line in pair_ids(ids, p, info)]
    offs = pair_tops(tops, p, info, stride)
    mass_t = dot_tn(rm[0, :, 128:], jnp.concatenate(hot, axis=0))
    grad = datt
    dm_t = (mass_t * grad.T.astype(F32)).astype(BF)
    d_member = dm_t.T
    asked = query[...]
    asked_t = asked.T
    blank = jnp.zeros((48, own), BF)
    weights, d_scores, d_masses = [], [], []
    pad = jnp.zeros((13, own), F32)
    for e in range(2):
        sel = half_of(e)
        other = 0 if e == 0 else 64
        d_mass = term(e, 0) + term(e, 1)
        d_masses.append(d_mass)
        delta = mass_t[other : other + 1] * d_mass
        aux_s = jnp.concatenate([term(e, 2), term(e, 3), term(e, 4), pad], axis=0).astype(BF)
        aux_d = jnp.concatenate([t.astype(F32) for t in split3(-delta)] + [pad], axis=0).astype(BF)

        def beside(turned, aux):
            if e == 0:
                return jnp.concatenate([turned[:64], aux, blank], axis=0)
            return jnp.concatenate([aux, blank, turned[64:]], axis=0)

        right = jnp.concatenate([beside(asked_t, aux_s), hot[e]], axis=0)
        bar = top_mask_t(offs[e * rows : (e + 1) * rows], own, stride, info[1])
        bar = jnp.where(bar, 0.0, NEG).astype(BF)
        ones = spare_ones(e)
        left = jnp.concatenate(
            [jnp.where(sel, k_own[...] * jnp.asarray(scale, BF), ones), bar], axis=1
        )
        weight = jnp.exp(dot(left, right))
        moved = dot(jnp.where(sel, v_own[...], ones), beside(dm_t, aux_d))
        weights.append(weight.astype(BF))
        d_scores.append((weight * moved).astype(BF))
    made = dot(jnp.concatenate(weights, axis=0), d_member)
    dv[...] = jnp.where(lo, made[:own], made[own:])
    made = dot(jnp.concatenate(d_scores, axis=0), asked)
    dk[...] = jnp.where(lo, made[:own], made[own:])
    hot_both = jnp.concatenate(hot, axis=0)
    d_mass_c = jnp.concatenate(
        [jnp.sum(h.astype(F32) * m, axis=1, keepdims=True) for h, m in zip(hot, d_masses)], axis=0
    )
    dr[0] = jnp.where(pair_rows(rows)[0], dot(hot_both, grad), d_mass_c)


def cluster_back_body(scale, stride, slots, p, info, ids_own, keys_top, cen, cst, dqm, *rest):
    ks, vs, drs, dks, dvs = (rest[i * slots : (i + 1) * slots] for i in range(5))
    dq, dk, dv = rest[5 * slots :]
    own = ks[0].shape[0]
    keys = jnp.concatenate([k[...] for k in ks], axis=0)
    values = jnp.concatenate([v[...] for v in vs], axis=0)
    rows = cen.shape[1] // 2
    sel, upper = pair_rows(rows)
    log_total, safe = cst[0, :, 0:1], cst[0, :, 1:2]
    both = drs[0][0]
    for r in drs[1:]:
        both = both + r[0]
    d_rest = jnp.where(sel, both, 0.0).astype(BF)
    d_mass = jnp.where(upper, both[:, 64:65], both[:, 0:1])
    cprob = jnp.exp(dot_nt(cen[0] * jnp.asarray(scale, BF), keys) - log_total)
    mask = sequence_mask(keys_top, p, info, own, stride, slots)
    d_prob = jnp.where(mask, d_mass, dot_nt(d_rest, values))
    inner = jnp.sum(cprob * d_prob, axis=1, keepdims=True)
    d_score = (cprob * (d_prob - inner)).astype(BF)
    keeps = jnp.where(mask[:, :own], 0.0, cprob[:, :own]).astype(BF)
    d_sums = jnp.where(sel, dot(d_score, keys) * (scale / safe), 0.0).astype(BF)
    hot = pair_hot(pair_ids(ids_own, p, info), rows)
    dq[...] = (dqm[...] + dot_tn(hot, d_sums)).astype(BF)
    d_key = dot_tn(d_score[:, :own], cen[0])
    d_value = dot_tn(keeps, d_rest)
    for a, b in zip(dks, dvs):
        d_key = d_key + a[...]
        d_value = d_value + b[...]
    dk[...] = (d_key * scale).astype(BF)
    dv[...] = d_value.astype(BF)


def halving_orders(count):
    bits = (count - 1).bit_length()
    low = sorted(range(count), key=lambda r: int(format(r, "0%db" % bits)[::-1], 2) if bits else 0)
    return low, list(range(count))


def emit_chunks(info, flat, outs, places, q_count, per):
    core, place, mine = info[0], info[1], info[2]
    for rel, order in enumerate(halving_orders(q_count)):
        for i, r in enumerate(order):
            out = outs[2 * rel + (0 if i < q_count // 2 else 1)]
            for s in range(places):
                at = lax.rem(place + s, places)
                out[i % (q_count // 2), s] = flat[at, core ^ rel, rows_at(mine ^ r, per), :]


def store_rows(flat, value, row, chunk):
    for owner in range(value.shape[0] // chunk):
        flat[owner // 2, owner % 2, row : row + chunk, :] = value[
            owner * chunk : (owner + 1) * chunk
        ].astype(BF)


def store_vecs(flat, vecs, row):
    half = vecs.shape[1] // 2
    lines = jnp.concatenate(
        [vecs[0:1, :half], vecs[0:1, half:], vecs[1:2, :half], vecs[1:2, half:]]
        + [jnp.zeros((12, half), F32)],
        axis=0,
    ).astype(BF)
    for z in range(flat.shape[0]):
        for c in range(2):
            flat[z, c, row : row + 16, :] = lines


def ffn_grad_body(places, q_count, per, info, n_mine, n_other, du_mine, du_other, act_mine, act_other,
                  cot_mine, cot_other, att_mine, att_other, da_mine, da_other, vecs, *rest):
    outs, (flat,) = rest[:-1], rest[-1:]
    core = info[0]
    width = n_mine.shape[1]
    chunk = width // (2 * places)
    step_count = du_mine.shape[0]
    hidden = act_mine.shape[1]
    down_chunk = hidden // (2 * places)
    block = n_mine.shape[0]
    n_t = [n_mine[...].T, n_other[...].T]
    for f in range(step_count):
        up = dot(n_t[0], du_mine[f]) + dot(n_t[1], du_other[f])
        store_rows(flat, up, f * chunk, chunk)
    base = step_count * chunk
    span = hidden // step_count
    for f in range(step_count):
        part = slice(f * span, (f + 1) * span)
        down = dot_tn(act_mine[:, part], cot_mine[...]) + dot_tn(act_other[:, part], cot_other[...])
        for i in range(span // down_chunk):
            owner = f * (span // down_chunk) + i
            flat[owner // 2, owner % 2, base : base + down_chunk, :] = down[
                i * down_chunk : (i + 1) * down_chunk
            ].astype(BF)
    base += down_chunk
    mine_rows, other_rows = rows_at(core, block), rows_at(1 - core, block)
    halves = []
    for ref in (att_mine, att_other):
        halves.append(
            dot_tn(ref[mine_rows, :], da_mine[...]) + dot_tn(ref[other_rows, :], da_other[...])
        )
    first = core == 0
    store_rows(
        flat,
        jnp.concatenate(
            [jnp.where(first, halves[0], halves[1]), jnp.where(first, halves[1], halves[0])], axis=0
        ),
        base,
        chunk,
    )
    base += chunk
    store_vecs(flat, vecs[...], base)
    emit_chunks(info, flat, outs, places, q_count, per)


def qkv_grad_body(places, q_count, per, info, normed, dq, dk, dv, wq, wk, wv, xa, xb, *rest):
    dn_mine, dn_send = rest[0], rest[1]
    outs, flat = rest[2:-1], rest[-1]
    core = info[0]
    block, width = dn_mine.shape
    chunk = width // (2 * places)
    n_t = normed[...].T
    for i, ref in enumerate((dq, dk, dv)):
        store_rows(flat, dot(n_t, ref[...]), i * chunk, chunk)
    gains, biases = 0.0, 0.0
    for rel, (ref, out) in enumerate(((xa, dn_mine), (xb, dn_send))):
        rows = rows_at(core ^ rel, block)
        d_normed = (
            dot_nt(dq[rows, :], wq[...]) + dot_nt(dk[rows, :], wk[...]) + dot_nt(dv[rows, :], wv[...])
        )
        out[...] = d_normed
        xhat, _ = norm_parts(ref[:block, :].astype(F32))
        gains += jnp.sum(d_normed * xhat, axis=0, keepdims=True)
        biases += jnp.sum(d_normed, axis=0, keepdims=True)
    store_vecs(flat, jnp.concatenate([gains, biases], axis=0), 3 * chunk)
    emit_chunks(info, flat, outs, places, q_count, per)


def input_body(info, x, gain, dn_mine, dn_other, d_mid, out):
    xhat, rstd = norm_parts(x[...].astype(F32))
    out[...] = d_mid[...] + norm_back(dn_mine[...] + dn_other[...], xhat, rstd, gain[...][None])


def gather_flat(info, parts, flat, per):
    own = info[2]
    for r, part in enumerate(parts):
        rows = rows_at(own ^ r, per)
        flat[0, rows, :] = part[0]
        flat[1, rows, :] = part[1]


def ffn_out_body(q_count, per, info, *rest):
    up, down, out, vec, flat = rest[q_count:]
    gather_flat(info, rest[:q_count], flat, per)
    core = info[0]
    half = flat.shape[2]
    chunk = up.shape[0]
    steps = up.shape[1] // (2 * half)
    for c in range(2):
        src = core ^ c
        for f in range(steps):
            at = (2 * f + c) * half
            up[:, at : at + half] = flat[src, f * chunk : (f + 1) * chunk, :].astype(F32)
        base = steps * chunk
        down[:, c * half : (c + 1) * half] = flat[src, base : base + down.shape[0], :].astype(F32)
        base += down.shape[0]
        out[:, c * half : (c + 1) * half] = flat[src, base : base + chunk, :].astype(F32)
        base += chunk
    vec[...] = flat[0, base : base + 16, :].astype(F32) + flat[1, base : base + 16, :].astype(F32)


def qkv_out_body(q_count, per, info, *rest):
    outs, vec, flat = rest[q_count : q_count + 3], rest[-2], rest[-1]
    gather_flat(info, rest[:q_count], flat, per)
    core = info[0]
    half = flat.shape[2]
    chunk = outs[0].shape[0]
    for c in range(2):
        src = core ^ c
        for i, out in enumerate(outs):
            out[:, c * half : (c + 1) * half] = flat[src, i * chunk : (i + 1) * chunk, :].astype(F32)
    base = 3 * chunk
    vec[...] = flat[0, base : base + 16, :].astype(F32) + flat[1, base : base + 16, :].astype(F32)


def pack_body(info, x, ids, out):
    block, width = x.shape
    heads = ids.shape[0]
    out[:block, :] = x[...]
    lines = jnp.concatenate([ids[...].astype(F32), jnp.zeros((16 - heads, block), F32)], axis=0)
    out[block:, :] = jnp.concatenate(
        [lines, jnp.zeros((16, width - block), F32)], axis=1
    ).astype(BF)


def hold_body(info, *refs):
    count = len(refs) // 2
    for source, target in zip(refs[:count], refs[count:]):
        target[...] = source[...]


def fold_body(info, keep_a, came_a, keep_b, came_b, *outs):
    for i, (keep, came) in enumerate(((keep_a, came_a), (keep_b, came_b))):
        cut = keep.shape[0] // 2
        for j in range(2):
            part = slice(j * cut, (j + 1) * cut)
            outs[2 * i + j][...] = (keep[part].astype(F32) + came[part].astype(F32)).astype(BF)


def merge_body(info, keep_a, came_a, keep_b, came_b, *outs):
    for s, out in enumerate(outs):
        out[0] = (keep_a[0, s].astype(F32) + came_a[0, s].astype(F32)).astype(BF)
        out[1] = (keep_b[0, s].astype(F32) + came_b[0, s].astype(F32)).astype(BF)


def total_body(info, *refs):
    parts, stay, go = refs[:-2], refs[-2], refs[-1]
    for i, out in enumerate((stay, go)):
        total = parts[0][i].astype(F32)
        for part in parts[1:]:
            total = total + part[i].astype(F32)
        out[...] = total.astype(BF)


def per_device(tokens, gain_one, bias_one, w_query, w_key, w_value, w_out, gain_two, bias_two,
               w_up, w_down, cotangent, cluster_ids, top_keys):
    _, block, width = tokens.shape
    heads = cluster_ids.shape[2]
    clusters, chosen = top_keys.shape[2], top_keys.shape[3]
    ctx, q_count = lax.axis_size("ctx"), lax.axis_size("seq")
    places = ctx // 2
    index, mine = lax.axis_index("ctx"), lax.axis_index("seq")
    core, place = index % 2, index // 2
    full_len = block * ctx
    own = 2 * block
    half = width // 2
    hidden = w_up.shape[1]
    pairs = half // 128
    stride = full_len // chosen
    rows = -(-clusters // 128) * 128
    scale = 1.0 / math.sqrt(width // heads)
    info = jnp.stack([core, place, mine]).astype(jnp.int32)
    sds = jax.ShapeDtypeStruct
    swap_to = [(i, i ^ 1) for i in range(ctx)]

    def swap(a):
        return lax.ppermute(a, "ctx", swap_to)

    def along(a, s):
        to = [(2 * z + c, 2 * ((z + s) % places) + c) for z in range(places) for c in range(2)]
        return lax.ppermute(a, "ctx", to)

    def hold(arrays, deps):
        shapes = [sds(a.shape, a.dtype) for a in arrays]
        return call(hold_body, [None] * len(arrays), [None] * len(arrays), shapes)(
            info, *arrays, deps=tuple(deps)
        )

    def across(a, r):
        return lax.ppermute(a, "seq", [(i, i ^ r) for i in range(q_count)])

    stages = [sorted({s, places - s}) for s in range(1, places // 2 + 1)]
    order = [0] + [s for stage in stages for s in stage]
    x, cot = tokens[0], cotangent[0]

    packed = call(pack_body, [None] * 2, [None], [sds((block + 16, width), BF)])(
        info, x, cluster_ids[0].T
    )[0]
    came = {s: along(packed, s) for s in stages[0]}
    packed_other = swap(packed)
    cot_other = swap(cot)
    keys_top = jnp.pad(top_keys[0], ((0, 0), (0, rows - clusters), (0, 0)))

    flat_half = sds((own, half), F32)

    def slot_call(s, xa, xb, slot0=None, deps=()):
        first = s == 0
        in_views = [None] * 4 + [half_lanes] * 3 + [None]
        operands = [xa, xb, gain_one, bias_one, w_query, w_key, w_value, keys_top]
        out_views = [lanes] * 3 + [lead] + [lanes] * 3 + [lead_two, None]
        out_shape = [sds((own, half), BF)] * 3 + [sds((pairs, 2 * rows, 128), F32)]
        out_shape += [flat_half] * 3 + [sds((2 * pairs, own, own), BF), sds((8, own), jnp.int32)]
        if first:
            out_views.append(None)
            out_shape.append(sds((own, width), BF))
        else:
            in_views += [None, lanes]
            operands += [slot0[8], slot0[0]]
        return call(
            functools.partial(slot_body, s, places, scale, stride),
            in_views, out_views, out_shape,
            scratch=[pltpu.VMEM((own, width), BF)], us=8.0, steps=pairs,
        )(info, *operands, deps=deps)

    *slot0, normed = slot_call(0, packed, packed_other)
    slots = {0: slot0}
    last = slot0[0]
    for i, stage in enumerate(stages):
        arrays = [came[s] for s in stage]
        if i + 1 < len(stages):
            sent, *arrays = hold([packed] + arrays, (last,))
            came.update({s: along(sent, s) for s in stages[i + 1]})
        else:
            arrays = hold(arrays, (last,))
        others = [swap(a) for a in arrays]
        for s, mine_block, other_block in zip(stage, arrays, others):
            deps = (last,) if s == stage[-1] else ()
            slots[s] = slot_call(s, mine_block, other_block, slot0, deps)
            last = slots[s][0] if s == stage[0] else last
    slots = [slots[s] for s in range(places)]
    query, key, value, csums, accs, dens, tops, probs, ids = zip(*slots)

    att, mem, lse, lse_col, rm, cen, cst = call(
        functools.partial(cluster_body, scale, stride, places),
        [None] * 2 + [lanes] * (2 * places) + [lead] * places + [lanes] * (3 * places),
        [lanes, lanes, lead, lanes, lead, lead, lead],
        [sds((own, half), BF), flat_half, sds((pairs, 8, own), F32), flat_half,
         sds((pairs, 2 * rows, 256), BF), sds((pairs, 2 * rows, 128), BF),
         sds((pairs, 2 * rows, 128), F32)],
        us=10.0, steps=pairs,
    )(info, ids[0], keys_top, *key, *value, *csums, *accs, *dens, *tops)

    att_other = swap(att)

    steps = hidden // width
    def step_columns(ref, f, info):
        return ref.at[:, f * width : (f + 1) * width]

    def step_rows(ref, f, info):
        return ref.at[f * width : (f + 1) * width, :]

    out, d_mid, d_attn, da_mine, da_send, normed_two, act, du_mine, du_send, vecs_two = call(
        functools.partial(ffn_body, steps),
        [None, None, my_rows, my_rows, my_rows, other_rows, None, None, step_columns, step_rows],
        [None] * 6 + [step_columns, lead, lead, None],
        [sds((block, width), F32), sds((block, width), F32), sds((block, width), BF),
         sds((block, half), BF), sds((block, half), BF), sds((block, width), BF),
         sds((block, hidden), BF), sds((steps, block, half), BF), sds((steps, block, half), BF),
         sds((8, width), F32)],
        scratch=[pltpu.VMEM((block, width), F32), pltpu.VMEM((block, width), F32)],
        us=13.0, steps=steps,
    )(info, x, cot, att, att_other, w_out, w_out, gain_two, bias_two, w_up, w_down)

    message = call(
        join_body,
        [None] * 4,
        [None],
        [sds((own + 64, half), BF)],
        us=1.5,
    )(info, da_mine, swap(da_send), mem, lse)[0]
    messages = {0: message}
    messages.update({s: along(message, s) for s in stages[0]})

    chunk, down_chunk = width // ctx, hidden // ctx

    def padded(n):
        return -(-n // (16 * q_count)) * 16 * q_count

    def chunk_outs(count):
        shape = (q_count // 2, places, count // q_count, half)
        return [None] * 4, [sds(shape, BF)] * 4

    ffn_rows = padded(steps * chunk + down_chunk + chunk + 16)
    per = ffn_rows // q_count
    ffn_pieces = call(
        functools.partial(ffn_grad_body, places, q_count, per),
        [None] * 6 + [my_columns, my_columns, None, None, my_columns, my_columns, None],
        *chunk_outs(ffn_rows),
        scratch=[pltpu.VMEM((places, 2, ffn_rows, half), BF)],
        us=9.0,
    )(info, normed_two, swap(normed_two), du_mine, swap(du_send), act, swap(act), cot, cot_other,
      att, att_other, d_attn, swap(d_attn), vecs_two, deps=(message,))

    bits = [1 << i for i in range((q_count - 1).bit_length())]

    def reduce_first(pieces):
        return across(pieces[1], bits[0]), across(pieces[3], bits[-1])

    def reduce_second(pieces, got, deps=()):
        ends = [pieces[0], got[0], pieces[2], got[1]]
        for low_bit, high_bit in zip(bits[1:], bits[-2::-1]):
            shape = sds((ends[0].shape[0] // 2,) + ends[0].shape[1:], BF)
            keep_a, send_a, keep_b, send_b = call(fold_body, [None] * 4, [None] * 4, [shape] * 4)(
                info, *ends, deps=deps
            )
            ends = [keep_a, across(send_a, low_bit), keep_b, across(send_b, high_bit)]
        return ends

    def reduce_third(ends, deps=()):
        shape = sds((2,) + ends[0].shape[2:], BF)
        parts = call(merge_body, [None] * 4, [None] * places, [shape] * places)(info, *ends, deps=deps)
        return parts[0], [along(parts[s], s) for s in range(1, places)], parts

    def reduce_total(part, others):
        one = sds(part.shape[1:], BF)
        return call(total_body, [None] * places, [None] * 2, [one] * 2, us=1.5)(info, part, *others)

    def spread(stay, go):
        mixed = jnp.stack([stay, swap(go)])
        return [mixed] + [across(mixed, r) for r in range(1, q_count)]

    ffn_got = reduce_first(ffn_pieces)

    def key_call(s, deps):
        return call(
            functools.partial(key_body, scale, stride),
            [lanes] * 3 + [None] * 3 + [lead],
            [lanes, lanes, lead],
            [flat_half, flat_half, sds((pairs, 2 * rows, 128), F32)],
            us=6.0, steps=pairs,
        )(info, key[0], value[0], query[s], messages[s], ids[s], keys_top, rm, deps=deps)

    grads = {0: key_call(0, (ffn_pieces[0],))}
    dqm = call(
        functools.partial(query_body, scale, places),
        [None, None, lanes, lead, lanes] + [lanes] * places + [lead_two] * places
        + [lanes] * (2 * places),
        [lanes],
        [flat_half],
        us=10.0, steps=pairs,
    )(info, ids[0], message, mem, rm, lse_col, *tops, *probs, *key, *value, deps=(grads[0][0],))[0]
    last = dqm
    for i, stage in enumerate(stages):
        deps = (last,)
        if i + 1 < len(stages):
            sent = hold([message], [messages[s] for s in stage] + [last])[0]
            messages.update({s: along(sent, s) for s in stages[i + 1]})
            deps = (sent,)
        for s in stage:
            grads[s] = key_call(s, deps)
            last = grads[s][0]
            deps = (last,)
    ffn_third = reduce_third(reduce_second(ffn_pieces, ffn_got, (grads[order[1]][0],)))
    dks, dvs, drs = zip(*[grads[s] for s in range(places)])

    dq, dk, dv = call(
        functools.partial(cluster_back_body, scale, stride, places),
        [None] * 2 + [lead] * 2 + [lanes] * (2 * places + 1) + [lead] * places + [lanes] * (2 * places),
        [lanes] * 3,
        [sds((own, half), BF)] * 3,
        us=10.0, steps=pairs,
    )(info, ids[0], keys_top, cen, cst, dqm, *key, *value, *drs, *dks, *dvs, deps=tuple(ffn_third[2]))

    qkv_rows = padded(3 * chunk + 16)
    per_one = qkv_rows // q_count
    specs, shapes = chunk_outs(qkv_rows)
    dn_mine, dn_send, *qkv_pieces = call(
        functools.partial(qkv_grad_body, places, q_count, per_one),
        [None] * 4 + [my_columns] * 3 + [None] * 2,
        [None] * 2 + specs,
        [sds((block, width), F32)] * 2 + shapes,
        scratch=[pltpu.VMEM((places, 2, qkv_rows, half), BF)],
        us=7.0,
    )(info, normed, dq, dk, dv, w_query, w_key, w_value, packed, packed_other)
    qkv_got = reduce_first(qkv_pieces)
    ffn_total = reduce_total(*ffn_third[:2])
    qkv_third = reduce_third(reduce_second(qkv_pieces, qkv_got), deps=(ffn_total[0],))
    ffn_parts = spread(*ffn_total)
    qkv_parts = spread(*reduce_total(*qkv_third[:2]))

    input_grad = call(
        input_body,
        [None] * 5,
        [None],
        [sds((block, width), F32)],
        us=2.3,
    )(info, x, gain_one, dn_mine, swap(dn_send), d_mid)[0]

    grad_up, grad_down, grad_out, vec_two = call(
        functools.partial(ffn_out_body, q_count, per),
        [None] * q_count,
        [None] * 4,
        [sds((chunk, hidden), F32), sds((down_chunk, width), F32), sds((chunk, width), F32),
         sds((16, half), F32)],
        scratch=[pltpu.VMEM((2, ffn_rows, half), BF)],
        us=3.0,
    )(info, *ffn_parts)
    grad_query, grad_key, grad_value, vec_one = call(
        functools.partial(qkv_out_body, q_count, per_one),
        [None] * q_count,
        [None] * 4,
        [sds((chunk, width), F32)] * 3 + [sds((16, half), F32)],
        scratch=[pltpu.VMEM((2, qkv_rows, half), BF)],
        us=1.5,
    )(info, *qkv_parts)

    def vectors(lines):
        both = lines[:4].reshape(2, width)
        cut = lax.dynamic_slice_in_dim(both, index * chunk, chunk, 1)
        return cut[0], cut[1]

    grad_gain_one, grad_bias_one = vectors(vec_one)
    grad_gain_two, grad_bias_two = vectors(vec_two)
    return (out[None], input_grad[None], grad_gain_one, grad_bias_one, grad_query, grad_key,
            grad_value, grad_out, grad_gain_two, grad_bias_two, grad_up, grad_down)


def solution(mesh):
    split = P("seq", "ctx", None)
    in_specs = (split,) + (P(),) * 10 + (split, split, P("seq", None, None, None))
    vec, mat = P("ctx"), P("ctx", None)
    out_specs = (split, split, vec, vec, mat, mat, mat, mat, vec, vec, mat, mat)
    return jax.shard_map(
        per_device, mesh=mesh, in_specs=in_specs, out_specs=out_specs, check_vma=False
    )
```

```python
import functools
import math

import jax
import jax.numpy as jnp
import numpy as np
from jax import lax
from jax.experimental import pallas as pl
from jax.experimental.pallas import tpu as pltpu
from jax.sharding import PartitionSpec as P

EPS = 1e-05
NEG = -1e30
F32 = jnp.float32
BF = jnp.bfloat16
COST = 0.5
ANY = pl.BlockSpec(memory_space=pl.ANY)
VMEM_BYTES = 7 * 1024 * 1024


def dot(a, b):
    return lax.dot_general(a, b, (((1,), (0,)), ((), ())), preferred_element_type=F32)


def dot_nt(a, b):
    return lax.dot_general(a, b, (((1,), (1,)), ((), ())), preferred_element_type=F32)


def dot_tn(a, b):
    return lax.dot_general(a, b, (((0,), (0,)), ((), ())), preferred_element_type=F32)


def low_half():
    return lax.broadcasted_iota(jnp.int32, (1, 128), 1) < 64


def norm_parts(x):
    center = x - jnp.mean(x, -1, keepdims=True)
    spread = jnp.mean(center * center, -1, keepdims=True)
    rstd = lax.rsqrt(spread + EPS)
    return center * rstd, rstd


def norm_back(d_normed, xhat, rstd, gain):
    d_hat = d_normed * gain
    first = jnp.mean(d_hat, -1, keepdims=True)
    second = jnp.mean(d_hat * xhat, -1, keepdims=True)
    return rstd * (d_hat - first - xhat * second)


def rows_at(index, size):
    return pl.ds(pl.multiple_of(index * size, size), size)


def call(body, in_views, out_views, out_shape, scratch=(), us=1.0, vmem=VMEM_BYTES, steps=None):
    views = list(in_views) + list(out_views)
    taken = 1 + len(in_views)

    def run(info, *args, deps=()):
        def kernel(*refs):
            scalars, arrays = refs[0], refs[1:taken] + refs[taken + len(deps) :]
            for step in range(steps or 1):
                seen = [
                    r if v is None else v(r, step, scalars)
                    for r, v in zip(arrays, views + [None] * len(scratch))
                ]
                if steps is None:
                    body(scalars, *seen)
                else:
                    body(step, scalars, *seen)

        return pl.pallas_call(
            kernel,
            in_specs=[pl.BlockSpec(memory_space=pltpu.SMEM)]
            + [pl.BlockSpec(memory_space=pltpu.VMEM)] * len(in_views)
            + [ANY] * len(deps),
            out_specs=[pl.BlockSpec(memory_space=pltpu.VMEM)] * len(out_views),
            out_shape=out_shape,
            scratch_shapes=list(scratch),
            compiler_params=pltpu.CompilerParams(vmem_limit_bytes=vmem),
            cost_estimate=pl.CostEstimate(
                flops=int(us * COST * 1.1e9), bytes_accessed=int(us * COST * 1e6), transcendentals=0
            ),
        )(info, *args, *deps)

    return run


def lanes(ref, p, info):
    return ref.at[:, p * 128 : (p + 1) * 128]


def lead(ref, p, info):
    return ref.at[p : p + 1]


def lead_two(ref, p, info):
    return ref.at[2 * p : 2 * p + 2]


def half_lanes(ref, p, info):
    half = ref.shape[1] // 2
    return ref.at[:, pl.ds(pl.multiple_of(info[0] * half + p * 128, 128), 128)]


def my_columns(ref, p, info):
    half = ref.shape[1] // 2
    return ref.at[:, pl.ds(pl.multiple_of(info[0] * half, 128), half)]


def my_rows(ref, p, info):
    return ref.at[rows_at(info[0], ref.shape[0] // 2), :]


def other_rows(ref, p, info):
    return ref.at[rows_at(1 - info[0], ref.shape[0] // 2), :]


def split3(x):
    first = x.astype(BF)
    left = x - first.astype(F32)
    second = left.astype(BF)
    return first, second, (left - second.astype(F32)).astype(BF)


def half_of(e):
    lo = low_half()
    return lo if e == 0 else ~lo


def spare(e):
    lane = lax.broadcasted_iota(jnp.int32, (1, 128), 1)
    base = 64 if e == 0 else 0
    return [lane == base + i for i in range(3)]


def spare_ones(e):
    marks = spare(e)
    return jnp.where(marks[0] | marks[1] | marks[2], 1.0, 0.0).astype(BF)


def hits_of(ids_row, rows):
    return lax.broadcasted_iota(jnp.int32, (rows, ids_row.shape[1]), 0) == ids_row


def as_hot(hits):
    return jnp.where(hits, 1.0, 0.0).astype(BF)


def top_offsets(tops, stride):
    lane = lax.broadcasted_iota(jnp.int32, tops.shape, 1)
    return (tops - lane * stride).astype(F32).astype(BF)


def top_mask(offs, own, stride, slot):
    shape = (offs.shape[1], own)
    lane = lax.broadcasted_iota(jnp.int32, shape, 1)
    ranges = (lane >> int(math.log2(stride))) + slot * (own // stride)
    expand = as_hot(ranges == lax.broadcasted_iota(jnp.int32, shape, 0))
    spot = (lax.broadcasted_iota(jnp.int32, (1, own), 1) & (stride - 1)).astype(F32)
    return dot(offs, expand) == spot


def chip_at(info, slot, slots):
    return lax.rem(info[1] - slot + slots, slots)


def pair_tops(tops, p, info, stride):
    _, rows, chosen = tops.shape
    first = info[0] * (tops.shape[0] // 2) + 2 * p
    return top_offsets(tops[pl.ds(first, 2)].reshape(2 * rows, chosen), stride)


def pair_ids(ids, p, info):
    return [ids[2 * p + e : 2 * p + e + 1, :] for e in range(2)]


def pair_rows(rows):
    row = lax.broadcasted_iota(jnp.int32, (2 * rows, 128), 0)
    lane = lax.broadcasted_iota(jnp.int32, (2 * rows, 128), 1)
    column = lax.broadcasted_iota(jnp.int32, (2 * rows, 1), 0)
    return (row < rows) == (lane < 64), column < rows


def pair_hot(lines, rows):
    return jnp.concatenate([as_hot(hits_of(line, rows)) for line in lines], axis=0)


def slot_body(slot, slots, scale, stride, p, info, xa, xb, gain, bias, wq, wk, wv, tops, *rest):
    first = slot == 0
    if first:
        q_out, k_out, v_out, csum, acc, den, top, prob, ids, bar_out, n_out, bar_t, normed = rest
        ids_own = ids
    else:
        ids_own, q_own, q_out, k_out, v_out, csum, acc, den, top, prob, ids, bar_out, normed = rest
    rows = tops.shape[1]
    core = info[0]
    block = xa.shape[0] - 16
    own = 2 * block

    if p == 0:
        for rel, ref in enumerate((xa, xb)):
            at = rows_at(core ^ rel, block)
            xhat, _ = norm_parts(ref[:block, :].astype(F32))
            low = (xhat * gain[...][None] + bias[...][None]).astype(BF)
            normed[at, :] = low
            if first:
                n_out[at, :] = low
        lines = [ref[block:, :block].astype(F32) for ref in (xa, xb)]
        heads = tops.shape[0] // 2
        lines = [jnp.where(core == 0, a[:heads], a[heads : 2 * heads]) for a in lines]
        lines = jnp.where(
            core == 0,
            jnp.concatenate(lines, axis=1),
            jnp.concatenate(lines[::-1], axis=1),
        )
        ids[:heads, :] = lines.astype(jnp.int32)

    weights = jnp.concatenate([wq[...], wk[...], wv[...]], axis=1)
    made = dot(normed[...], weights).astype(BF)
    query, key, value = made[:, :128], made[:, 128:256], made[:, 256:]
    q_out[...] = query
    k_out[...] = key
    v_out[...] = value
    key_t = key.T
    asked = (query if first else q_own[...]) * jnp.asarray(scale, BF)
    peaks, outs = [], []
    one = jnp.ones((), BF)
    hot = pair_hot(pair_ids(ids, p, info), rows)
    hot_own = (hot if first else pair_hot(pair_ids(ids_own, p, info), rows)).T
    count = jnp.sum(hot.astype(F32), axis=1, keepdims=True)
    csum[0] = jnp.where(pair_rows(rows)[0], dot(hot, query), count)
    mask = top_mask(pair_tops(tops, p, info, stride), own, stride, chip_at(info, slot, slots))
    bars = jnp.where(mask, 0.0, NEG).astype(BF)
    bar_out[0] = bars
    if first:
        bar_t[0] = bars.T
    for e in range(2):
        sel = half_of(e)
        bar = bars[e * rows : (e + 1) * rows]
        right = jnp.concatenate([key_t, bar], axis=0)
        member_of = hot_own[:, e * rows : (e + 1) * rows]
        left = jnp.concatenate([jnp.where(sel, asked, jnp.zeros((), BF)), member_of], axis=1)
        score = dot(left, right)
        peak = jnp.max(score, axis=1, keepdims=True)
        grown = jnp.exp(score - peak).astype(BF)
        prob[e] = grown
        peaks.append(peak)
        outs.append(dot(grown, jnp.where(sel, value, one)))
    lo = low_half()
    acc[...] = jnp.where(lo, outs[0], outs[1])
    den[...] = pltpu.roll(jnp.where(lo, outs[1], outs[0]), 64, 1)
    top[...] = jnp.where(lo, peaks[0], peaks[1])


def cluster_body(scale, slots, p, info, ids_own, *rest):
    ks, vs, bars, csums, accs, dens, tops = (rest[i * slots : (i + 1) * slots] for i in range(7))
    att, mem, lse, lse_col, rm, cen, cst = rest[7 * slots :]
    keys = jnp.concatenate([k[...] for k in ks], axis=0)
    values = jnp.concatenate([v[...] for v in vs], axis=0)
    own = ks[0].shape[0]
    rows = bars[0].shape[1] // 2
    lo = low_half()
    lane = lax.broadcasted_iota(jnp.int32, (1, 128), 1)
    sel, upper = pair_rows(rows)
    sums = csums[0][0]
    for c in csums[1:]:
        sums = sums + c[0]
    safe = jnp.maximum(jnp.where(upper, sums[:, 64:65], sums[:, 0:1]), 1.0)
    center = jnp.where(sel, sums / safe, 0.0).astype(BF)
    score = dot_nt(center * jnp.asarray(scale, BF), keys)
    peak = jnp.max(score, axis=1, keepdims=True)
    grown = jnp.exp(score - peak)
    total = jnp.sum(grown, axis=1, keepdims=True)
    inverse = 1.0 / total
    mask = jnp.concatenate([b[0] for b in bars], axis=1) == 0
    mass = (jnp.sum(jnp.where(mask, grown, 0.0), axis=1, keepdims=True) * inverse).astype(BF)
    kept = jnp.where(mask, 0.0, grown).astype(BF)
    attended = jnp.where(sel, dot(kept, values) * inverse, 0.0).astype(BF)
    wide = jnp.where(sel, mass, jnp.zeros((), BF))
    both = jnp.concatenate([attended, wide], axis=1)
    cen[0] = center
    cst[0] = jnp.where(lane == 0, peak + jnp.log(total), safe)
    rm[0] = both
    hot = pair_hot(pair_ids(ids_own, p, info), rows)
    token = dot_tn(hot, both)
    peak = tops[0][...]
    for t in tops[1:]:
        peak = jnp.maximum(peak, t[...])
    total, member = 0.0, 0.0
    for t, d, a in zip(tops, dens, accs):
        weight = jnp.exp(t[...] - peak)
        total += weight * d[...]
        member += weight * a[...]
    member = member / total
    log_total = peak + jnp.log(total)
    lse_col[...] = log_total
    turned = log_total.T
    lse[0] = jnp.concatenate([turned[0:1], turned[64:65], jnp.zeros((6, own), F32)], axis=0)
    mem[...] = member
    att[...] = (token[:, 128:] * member + token[:, :128]).astype(BF)


def ffn_body(steps, step, info, x, cot, att_mine, att_other, wo_mine, wo_other, gain, bias, w_up,
             w_down, out, d_mid, d_attn, da_mine, da_other, normed_out, act_out, du_mine, du_send,
             vecs, acc, dacc):
    if step == 0:
        mid = x[...].astype(F32) + dot(att_mine[...], wo_mine[...]) + dot(att_other[...], wo_other[...])
        d_mid[...] = mid
        xhat, _ = norm_parts(mid)
        normed_out[...] = (xhat * gain[...][None] + bias[...][None]).astype(BF)
    upper = dot(normed_out[...], w_up[...])
    c0 = math.sqrt(2.0 / math.pi)
    square = upper * upper
    tanh = jnp.tanh(c0 * (upper + 0.044715 * square * upper))
    cdf = 0.5 * (1.0 + tanh)
    active = (upper * cdf).astype(BF)
    act_out[...] = active
    more = dot(active, w_down[...])
    acc[...] = more + (d_mid[...] if step == 0 else acc[...])
    slope = cdf + 0.5 * upper * (1.0 - tanh * tanh) * (c0 * (1.0 + 3 * 0.044715 * square))
    d_upper = (dot_nt(cot[...], w_down[...]) * slope).astype(BF)
    half = d_upper.shape[1] // 2
    first = info[0] == 0
    du_mine[0] = jnp.where(first, d_upper[:, :half], d_upper[:, half:])
    du_send[0] = jnp.where(first, d_upper[:, half:], d_upper[:, :half])
    more = dot_nt(d_upper, w_up[...])
    dacc[...] = more if step == 0 else dacc[...] + more
    if step == steps - 1:
        out[...] = acc[...]
        xhat, rstd = norm_parts(d_mid[...])
        d_normed = dacc[...]
        vecs[...] = jnp.concatenate(
            [
                jnp.sum(d_normed * xhat, axis=0, keepdims=True),
                jnp.sum(d_normed, axis=0, keepdims=True),
                jnp.zeros((6, d_normed.shape[1]), F32),
            ],
            axis=0,
        )
        grad = cot[...].astype(F32) + norm_back(d_normed, xhat, rstd, gain[...][None])
        d_mid[...] = grad
        low = grad.astype(BF)
        d_attn[...] = low
        da_mine[...] = dot_nt(low, wo_mine[...]).astype(BF)
        da_other[...] = dot_nt(low, wo_other[...]).astype(BF)


def join_body(info, mine, other, mem, lse, joined):
    core = info[0]
    block, half = mine.shape
    lo = low_half()
    lane = lax.broadcasted_iota(jnp.int32, (1, 128), 1)
    found = {}
    for rel, ref in enumerate((mine, other)):
        at = rows_at(core ^ rel, block)
        joined[at, :] = ref[...]
        for p in range(half // 128):
            part = slice(p * 128, (p + 1) * 128)
            product = ref[:, part].astype(F32) * mem[at, part]
            first = jnp.sum(jnp.where(lo, product, 0.0), axis=1, keepdims=True)
            second = jnp.sum(jnp.where(lo, 0.0, product), axis=1, keepdims=True)
            table = jnp.where(lane == 0, first, jnp.where(lane == 1, second, 0.0)).T
            stat = lse[p, :, at]
            for e in range(2):
                found[p, e, rel] = split3(table[e : e + 1])[:2] + split3(-stat[e : e + 1])
    lines = []
    for p in range(half // 128):
        for e in range(2):
            for rel in range(2):
                lines += [line.astype(F32) for line in found[p, e, rel]]
    lines.append(jnp.zeros((64 - len(lines), block), F32))
    table = jnp.concatenate(lines, axis=0).astype(BF)
    joined[2 * block :, :] = jnp.concatenate(
        [table, jnp.zeros((64, half - block), BF)], axis=1
    )


def query_body(scale, slots, p, info, ids_own, message, mem, rm, lse_col, *rest):
    tops, probs, ks, vs = (rest[i * slots : (i + 1) * slots] for i in range(4))
    dq = rest[4 * slots]
    own = mem.shape[0]
    rows = rm.shape[1] // 2
    lo = low_half()
    hot = pair_hot(pair_ids(ids_own, p, info), rows)
    mass = dot_tn(hot, rm[0, :, 128:])
    grad = message[:own, p * 128 : (p + 1) * 128].astype(F32)
    product = grad * mem[...]
    d_member = (mass * grad).astype(BF)
    lefts = []
    for e in range(2):
        sel = half_of(e)
        other = 0 if e == 0 else 64
        delta = mass[:, other : other + 1] * jnp.sum(
            jnp.where(sel, product, 0.0), axis=1, keepdims=True
        )
        left = jnp.where(sel, d_member, jnp.zeros((), BF))
        for mark, term in zip(spare(e), split3(-delta)):
            left = jnp.where(mark, term, left)
        lefts.append(left)
    total = 0.0
    for s in range(slots):
        d_scores = []
        for e in range(2):
            right = jnp.where(half_of(e), vs[s][...], spare_ones(e))
            moved = dot_nt(lefts[e], right)
            d_scores.append((probs[s][e].astype(F32) * moved).astype(BF))
        made = dot(jnp.concatenate(d_scores, axis=0), ks[s][...])
        total += jnp.exp(tops[s][...] - lse_col[...]) * jnp.where(lo, made[:own], made[own:])
    dq[...] = total * scale


def key_body(scale, p, info, k_own, v_own, query, message, ids, bar_t, rm, dk, dv, dr):
    core = info[0]
    own = k_own.shape[0]
    block = own // 2
    rows = rm.shape[1] // 2
    lo = low_half()
    picked = message[own:, :block].astype(F32)[20 * p : 20 * p + 20]
    datt = message[:own, p * 128 : (p + 1) * 128]

    def term(e, i):
        a, b = picked[10 * e + i : 10 * e + i + 1], picked[10 * e + 5 + i : 10 * e + 6 + i]
        return jnp.where(
            core == 0, jnp.concatenate([a, b], axis=1), jnp.concatenate([b, a], axis=1)
        )

    hot = [as_hot(hits_of(line, rows)) for line in pair_ids(ids, p, info)]
    mass_t = dot_tn(rm[0, :, 128:], jnp.concatenate(hot, axis=0))
    grad = datt
    dm_t = (mass_t * grad.T.astype(F32)).astype(BF)
    d_member = dm_t.T
    asked = query[...]
    asked_t = asked.T
    blank = jnp.zeros((48, own), BF)
    weights, d_scores, d_masses = [], [], []
    pad = jnp.zeros((13, own), F32)
    for e in range(2):
        sel = half_of(e)
        other = 0 if e == 0 else 64
        d_mass = term(e, 0) + term(e, 1)
        d_masses.append(d_mass)
        delta = mass_t[other : other + 1] * d_mass
        aux_s = jnp.concatenate([term(e, 2), term(e, 3), term(e, 4), pad], axis=0).astype(BF)
        aux_d = jnp.concatenate([t.astype(F32) for t in split3(-delta)] + [pad], axis=0).astype(BF)

        def beside(turned, aux):
            if e == 0:
                return jnp.concatenate([turned[:64], aux, blank], axis=0)
            return jnp.concatenate([aux, blank, turned[64:]], axis=0)

        right = jnp.concatenate([beside(asked_t, aux_s), hot[e]], axis=0)
        bar = bar_t[0, :, e * rows : (e + 1) * rows]
        ones = spare_ones(e)
        left = jnp.concatenate(
            [jnp.where(sel, k_own[...] * jnp.asarray(scale, BF), ones), bar], axis=1
        )
        weight = jnp.exp(dot(left, right))
        moved = dot(jnp.where(sel, v_own[...], ones), beside(dm_t, aux_d))
        weights.append(weight.astype(BF))
        d_scores.append((weight * moved).astype(BF))
    made = dot(jnp.concatenate(weights, axis=0), d_member)
    dv[...] = jnp.where(lo, made[:own], made[own:])
    made = dot(jnp.concatenate(d_scores, axis=0), asked)
    dk[...] = jnp.where(lo, made[:own], made[own:])
    hot_both = jnp.concatenate(hot, axis=0)
    d_mass_c = jnp.concatenate(
        [jnp.sum(h.astype(F32) * m, axis=1, keepdims=True) for h, m in zip(hot, d_masses)], axis=0
    )
    dr[0] = jnp.where(pair_rows(rows)[0], dot(hot_both, grad), d_mass_c)


def cluster_back_body(scale, slots, p, info, ids_own, cen, cst, dqm, *rest):
    ks, vs, bars, drs, dks, dvs = (rest[i * slots : (i + 1) * slots] for i in range(6))
    dq, dk, dv = rest[6 * slots :]
    own = ks[0].shape[0]
    keys = jnp.concatenate([k[...] for k in ks], axis=0)
    values = jnp.concatenate([v[...] for v in vs], axis=0)
    rows = cen.shape[1] // 2
    sel, upper = pair_rows(rows)
    log_total, safe = cst[0, :, 0:1], cst[0, :, 1:2]
    both = drs[0][0]
    for r in drs[1:]:
        both = both + r[0]
    d_rest = jnp.where(sel, both, 0.0).astype(BF)
    d_mass = jnp.where(upper, both[:, 64:65], both[:, 0:1])
    cprob = jnp.exp(dot_nt(cen[0] * jnp.asarray(scale, BF), keys) - log_total)
    mask = jnp.concatenate([b[0] for b in bars], axis=1) == 0
    d_prob = jnp.where(mask, d_mass, dot_nt(d_rest, values))
    inner = jnp.sum(cprob * d_prob, axis=1, keepdims=True)
    d_score = (cprob * (d_prob - inner)).astype(BF)
    keeps = jnp.where(mask[:, :own], 0.0, cprob[:, :own]).astype(BF)
    d_sums = jnp.where(sel, dot(d_score, keys) * (scale / safe), 0.0).astype(BF)
    hot = pair_hot(pair_ids(ids_own, p, info), rows)
    dq[...] = (dqm[...] + dot_tn(hot, d_sums)).astype(BF)
    d_key = dot_tn(d_score[:, :own], cen[0])
    d_value = dot_tn(keeps, d_rest)
    for a, b in zip(dks, dvs):
        d_key = d_key + a[...]
        d_value = d_value + b[...]
    dk[...] = (d_key * scale).astype(BF)
    dv[...] = d_value.astype(BF)


def halving_orders(count):
    bits = (count - 1).bit_length()
    low = sorted(range(count), key=lambda r: int(format(r, "0%db" % bits)[::-1], 2) if bits else 0)
    return low, list(range(count))


def emit_chunks(info, flat, outs, places, q_count, per):
    core, place, mine = info[0], info[1], info[2]
    for rel, order in enumerate(halving_orders(q_count)):
        for i, r in enumerate(order):
            out = outs[2 * rel + (0 if i < q_count // 2 else 1)]
            for s in range(places):
                at = lax.rem(place + s, places)
                out[i % (q_count // 2), s] = flat[at, core ^ rel, rows_at(mine ^ r, per), :]


def store_rows(flat, value, row, chunk):
    for owner in range(value.shape[0] // chunk):
        flat[owner // 2, owner % 2, row : row + chunk, :] = value[
            owner * chunk : (owner + 1) * chunk
        ].astype(BF)


def store_vecs(flat, vecs, row):
    half = vecs.shape[1] // 2
    lines = jnp.concatenate(
        [vecs[0:1, :half], vecs[0:1, half:], vecs[1:2, :half], vecs[1:2, half:]]
        + [jnp.zeros((12, half), F32)],
        axis=0,
    ).astype(BF)
    for z in range(flat.shape[0]):
        for c in range(2):
            flat[z, c, row : row + 16, :] = lines


def ffn_grad_body(places, q_count, per, info, n_mine, n_other, du_mine, du_other, act_mine, act_other,
                  cot_mine, cot_other, att_mine, att_other, da_mine, da_other, vecs, *rest):
    outs, (flat,) = rest[:-1], rest[-1:]
    core = info[0]
    width = n_mine.shape[1]
    chunk = width // (2 * places)
    step_count = du_mine.shape[0]
    hidden = act_mine.shape[1]
    down_chunk = hidden // (2 * places)
    block = n_mine.shape[0]
    n_t = [n_mine[...].T, n_other[...].T]
    n_t = jnp.concatenate(n_t, axis=1)
    half = du_mine.shape[2]
    for f in range(0, step_count, 2):
        right = [jnp.concatenate([du_mine[i], du_other[i]], axis=0) for i in (f, f + 1)]
        up = dot(n_t, jnp.concatenate(right, axis=1))
        for i in range(2):
            store_rows(flat, up[:, i * half : (i + 1) * half], (f + i) * chunk, chunk)
    base = step_count * chunk
    span = hidden // step_count
    for f in range(step_count):
        part = slice(f * span, (f + 1) * span)
        down = dot_tn(act_mine[:, part], cot_mine[...]) + dot_tn(act_other[:, part], cot_other[...])
        for i in range(span // down_chunk):
            owner = f * (span // down_chunk) + i
            flat[owner // 2, owner % 2, base : base + down_chunk, :] = down[
                i * down_chunk : (i + 1) * down_chunk
            ].astype(BF)
    base += down_chunk
    mine_rows, other_rows = rows_at(core, block), rows_at(1 - core, block)
    halves = []
    for ref in (att_mine, att_other):
        halves.append(
            dot_tn(ref[mine_rows, :], da_mine[...]) + dot_tn(ref[other_rows, :], da_other[...])
        )
    first = core == 0
    store_rows(
        flat,
        jnp.concatenate(
            [jnp.where(first, halves[0], halves[1]), jnp.where(first, halves[1], halves[0])], axis=0
        ),
        base,
        chunk,
    )
    base += chunk
    store_vecs(flat, vecs[...], base)
    emit_chunks(info, flat, outs, places, q_count, per)


def qkv_grad_body(places, q_count, per, info, normed, dq, dk, dv, wq, wk, wv, xa, xb, *rest):
    dn_mine, dn_send = rest[0], rest[1]
    outs, flat, d_all = rest[2:-2], rest[-2], rest[-1]
    core = info[0]
    block, width = dn_mine.shape
    chunk = width // (2 * places)
    n_t = normed[...].T
    half = dq.shape[1]
    grads = jnp.concatenate([dq[...], dk[...], dv[...]], axis=1)
    made = dot(n_t, grads)
    for i in range(3):
        store_rows(flat, made[:, i * half : (i + 1) * half], i * chunk, chunk)
    weights = jnp.concatenate([wq[...], wk[...], wv[...]], axis=1)
    d_all[...] = dot_nt(grads, weights)
    gains, biases = 0.0, 0.0
    for rel, (ref, out) in enumerate(((xa, dn_mine), (xb, dn_send))):
        rows = rows_at(core ^ rel, block)
        d_normed = d_all[rows, :]
        out[...] = d_normed
        xhat, _ = norm_parts(ref[:block, :].astype(F32))
        gains += jnp.sum(d_normed * xhat, axis=0, keepdims=True)
        biases += jnp.sum(d_normed, axis=0, keepdims=True)
    store_vecs(flat, jnp.concatenate([gains, biases], axis=0), 3 * chunk)
    emit_chunks(info, flat, outs, places, q_count, per)


def input_body(info, x, gain, dn_mine, dn_other, d_mid, out):
    xhat, rstd = norm_parts(x[...].astype(F32))
    out[...] = d_mid[...] + norm_back(dn_mine[...] + dn_other[...], xhat, rstd, gain[...][None])


def gather_flat(info, parts, flat, per):
    own = info[2]
    for r, part in enumerate(parts):
        rows = rows_at(own ^ r, per)
        flat[0, rows, :] = part[0]
        flat[1, rows, :] = part[1]


def ffn_out_body(q_count, per, info, *rest):
    up, down, out, vec, flat = rest[q_count:]
    gather_flat(info, rest[:q_count], flat, per)
    core = info[0]
    half = flat.shape[2]
    chunk = up.shape[0]
    steps = up.shape[1] // (2 * half)
    for c in range(2):
        src = core ^ c
        for f in range(steps):
            at = (2 * f + c) * half
            up[:, at : at + half] = flat[src, f * chunk : (f + 1) * chunk, :].astype(F32)
        base = steps * chunk
        down[:, c * half : (c + 1) * half] = flat[src, base : base + down.shape[0], :].astype(F32)
        base += down.shape[0]
        out[:, c * half : (c + 1) * half] = flat[src, base : base + chunk, :].astype(F32)
        base += chunk
    vec[...] = flat[0, base : base + 16, :].astype(F32) + flat[1, base : base + 16, :].astype(F32)


def qkv_out_body(q_count, per, info, *rest):
    outs, vec, flat = rest[q_count : q_count + 3], rest[-2], rest[-1]
    gather_flat(info, rest[:q_count], flat, per)
    core = info[0]
    half = flat.shape[2]
    chunk = outs[0].shape[0]
    for c in range(2):
        src = core ^ c
        for i, out in enumerate(outs):
            out[:, c * half : (c + 1) * half] = flat[src, i * chunk : (i + 1) * chunk, :].astype(F32)
    base = 3 * chunk
    vec[...] = flat[0, base : base + 16, :].astype(F32) + flat[1, base : base + 16, :].astype(F32)


def pack_body(info, x, ids, out):
    block, width = x.shape
    heads = ids.shape[0]
    out[:block, :] = x[...]
    lines = jnp.concatenate([ids[...].astype(F32), jnp.zeros((16 - heads, block), F32)], axis=0)
    out[block:, :] = jnp.concatenate(
        [lines, jnp.zeros((16, width - block), F32)], axis=1
    ).astype(BF)


def hold_body(info, *refs):
    count = len(refs) // 2
    for source, target in zip(refs[:count], refs[count:]):
        target[...] = source[...]


def fold_body(info, keep_a, came_a, keep_b, came_b, *outs):
    for i, (keep, came) in enumerate(((keep_a, came_a), (keep_b, came_b))):
        cut = keep.shape[0] // 2
        for j in range(2):
            part = slice(j * cut, (j + 1) * cut)
            outs[2 * i + j][...] = (keep[part].astype(F32) + came[part].astype(F32)).astype(BF)


def merge_body(info, keep_a, came_a, keep_b, came_b, *outs):
    for s, out in enumerate(outs):
        out[0] = (keep_a[0, s].astype(F32) + came_a[0, s].astype(F32)).astype(BF)
        out[1] = (keep_b[0, s].astype(F32) + came_b[0, s].astype(F32)).astype(BF)


def total_body(info, *refs):
    parts, stay, go = refs[:-2], refs[-2], refs[-1]
    for i, out in enumerate((stay, go)):
        total = parts[0][i].astype(F32)
        for part in parts[1:]:
            total = total + part[i].astype(F32)
        out[...] = total.astype(BF)


def per_device(tokens, gain_one, bias_one, w_query, w_key, w_value, w_out, gain_two, bias_two,
               w_up, w_down, cotangent, cluster_ids, top_keys):
    _, block, width = tokens.shape
    heads = cluster_ids.shape[2]
    clusters, chosen = top_keys.shape[2], top_keys.shape[3]
    ctx, q_count = lax.axis_size("ctx"), lax.axis_size("seq")
    places = ctx // 2
    index, mine = lax.axis_index("ctx"), lax.axis_index("seq")
    core, place = index % 2, index // 2
    full_len = block * ctx
    own = 2 * block
    half = width // 2
    hidden = w_up.shape[1]
    pairs = half // 128
    stride = full_len // chosen
    rows = -(-clusters // 128) * 128
    scale = 1.0 / math.sqrt(width // heads)
    info = jnp.stack([core, place, mine]).astype(jnp.int32)
    sds = jax.ShapeDtypeStruct
    swap_to = [(i, i ^ 1) for i in range(ctx)]

    def swap(a):
        return lax.ppermute(a, "ctx", swap_to)

    def along(a, s):
        to = [(2 * z + c, 2 * ((z + s) % places) + c) for z in range(places) for c in range(2)]
        return lax.ppermute(a, "ctx", to)

    def hold(arrays, deps):
        shapes = [sds(a.shape, a.dtype) for a in arrays]
        return call(hold_body, [None] * len(arrays), [None] * len(arrays), shapes)(
            info, *arrays, deps=tuple(deps)
        )

    def across(a, r):
        return lax.ppermute(a, "seq", [(i, i ^ r) for i in range(q_count)])

    stages = [sorted({s, places - s}) for s in range(1, places // 2 + 1)]
    order = [0] + [s for stage in stages for s in stage]
    x, cot = tokens[0], cotangent[0]

    packed = call(pack_body, [None] * 2, [None], [sds((block + 16, width), BF)])(
        info, x, cluster_ids[0].T
    )[0]
    came = {s: along(packed, s) for s in stages[0]}
    packed_other = swap(packed)
    cot_other = swap(cot)
    keys_top = jnp.pad(top_keys[0], ((0, 0), (0, rows - clusters), (0, 0)))

    flat_half = sds((own, half), F32)

    def slot_call(s, xa, xb, slot0=None, deps=()):
        first = s == 0
        in_views = [None] * 4 + [half_lanes] * 3 + [None]
        operands = [xa, xb, gain_one, bias_one, w_query, w_key, w_value, keys_top]
        out_views = [lanes] * 3 + [lead] + [lanes] * 3 + [lead_two, None, lead]
        out_shape = [sds((own, half), BF)] * 3 + [sds((pairs, 2 * rows, 128), F32)]
        out_shape += [flat_half] * 3 + [sds((2 * pairs, own, own), BF), sds((8, own), jnp.int32),
                      sds((pairs, 2 * rows, own), BF)]
        if first:
            out_views += [None, lead]
            out_shape += [sds((own, width), BF), sds((pairs, own, 2 * rows), BF)]
        else:
            in_views += [None, lanes]
            operands += [slot0[8], slot0[0]]
        return call(
            functools.partial(slot_body, s, places, scale, stride),
            in_views, out_views, out_shape,
            scratch=[pltpu.VMEM((own, width), BF)], us=8.0, steps=pairs,
        )(info, *operands, deps=deps)

    *slot0, normed, bar_t = slot_call(0, packed, packed_other)
    slots = {0: slot0}
    last = slot0[0]
    for i, stage in enumerate(stages):
        done = [slots[s][0] for s in stages[i - 1]] if i else [last]
        if i + 1 < len(stages):
            sent = hold([packed], (last,))[0]
            came.update({s: along(sent, s) for s in stages[i + 1]})
            done.append(sent)
        arrays = hold([came[s] for s in stage], done)
        others = [swap(a) for a in arrays]
        for s, mine_block, other_block in zip(stage, arrays, others):
            deps = (last,) if s == stage[-1] else ()
            slots[s] = slot_call(s, mine_block, other_block, slot0, deps)
            last = slots[s][0] if s == stage[0] else last
    slots = [slots[s] for s in range(places)]
    query, key, value, csums, accs, dens, tops, probs, ids, bars = zip(*slots)

    att, mem, lse, lse_col, rm, cen, cst = call(
        functools.partial(cluster_body, scale, places),
        [None] + [lanes] * (2 * places) + [lead] * (2 * places) + [lanes] * (3 * places),
        [lanes, lanes, lead, lanes, lead, lead, lead],
        [sds((own, half), BF), flat_half, sds((pairs, 8, own), F32), flat_half,
         sds((pairs, 2 * rows, 256), BF), sds((pairs, 2 * rows, 128), BF),
         sds((pairs, 2 * rows, 128), F32)],
        us=10.0, steps=pairs,
    )(info, ids[0], *key, *value, *bars, *csums, *accs, *dens, *tops)

    att_other = swap(att)

    steps = hidden // width
    def step_columns(ref, f, info):
        return ref.at[:, f * width : (f + 1) * width]

    def step_rows(ref, f, info):
        return ref.at[f * width : (f + 1) * width, :]

    out, d_mid, d_attn, da_mine, da_send, normed_two, act, du_mine, du_send, vecs_two = call(
        functools.partial(ffn_body, steps),
        [None, None, my_rows, my_rows, my_rows, other_rows, None, None, step_columns, step_rows],
        [None] * 6 + [step_columns, lead, lead, None],
        [sds((block, width), F32), sds((block, width), F32), sds((block, width), BF),
         sds((block, half), BF), sds((block, half), BF), sds((block, width), BF),
         sds((block, hidden), BF), sds((steps, block, half), BF), sds((steps, block, half), BF),
         sds((8, width), F32)],
        scratch=[pltpu.VMEM((block, width), F32), pltpu.VMEM((block, width), F32)],
        us=13.0, steps=steps,
    )(info, x, cot, att, att_other, w_out, w_out, gain_two, bias_two, w_up, w_down)

    message = call(
        join_body,
        [None] * 4,
        [None],
        [sds((own + 64, half), BF)],
        us=1.5,
    )(info, da_mine, swap(da_send), mem, lse)[0]
    messages = {0: message}
    messages.update({s: along(message, s) for s in stages[0]})

    chunk, down_chunk = width // ctx, hidden // ctx

    def padded(n):
        return -(-n // (16 * q_count)) * 16 * q_count

    def chunk_outs(count):
        shape = (q_count // 2, places, count // q_count, half)
        return [None] * 4, [sds(shape, BF)] * 4

    ffn_rows = padded(steps * chunk + down_chunk + chunk + 16)
    per = ffn_rows // q_count
    ffn_pieces = call(
        functools.partial(ffn_grad_body, places, q_count, per),
        [None] * 6 + [my_columns, my_columns, None, None, my_columns, my_columns, None],
        *chunk_outs(ffn_rows),
        scratch=[pltpu.VMEM((places, 2, ffn_rows, half), BF)],
        us=9.0,
    )(info, normed_two, swap(normed_two), du_mine, swap(du_send), act, swap(act), cot, cot_other,
      att, att_other, d_attn, swap(d_attn), vecs_two, deps=(message,))

    bits = [1 << i for i in range((q_count - 1).bit_length())]

    def reduce_first(pieces):
        return across(pieces[1], bits[0]), across(pieces[3], bits[-1])

    def reduce_second(pieces, got, deps=()):
        ends = [pieces[0], got[0], pieces[2], got[1]]
        for low_bit, high_bit in zip(bits[1:], bits[-2::-1]):
            shape = sds((ends[0].shape[0] // 2,) + ends[0].shape[1:], BF)
            keep_a, send_a, keep_b, send_b = call(fold_body, [None] * 4, [None] * 4, [shape] * 4)(
                info, *ends, deps=deps
            )
            ends = [keep_a, across(send_a, low_bit), keep_b, across(send_b, high_bit)]
        return ends

    def reduce_third(ends, deps=()):
        shape = sds((2,) + ends[0].shape[2:], BF)
        parts = call(merge_body, [None] * 4, [None] * places, [shape] * places)(info, *ends, deps=deps)
        return parts[0], [along(parts[s], s) for s in range(1, places)], parts

    def reduce_total(part, others, deps=()):
        one = sds(part.shape[1:], BF)
        return call(total_body, [None] * places, [None] * 2, [one] * 2, us=1.5)(
            info, part, *others, deps=deps
        )

    def spread(stay, go):
        mixed = jnp.stack([stay, swap(go)])
        return [mixed] + [across(mixed, r) for r in range(1, q_count)]

    ffn_got = reduce_first(ffn_pieces)

    def key_call(s, deps):
        return call(
            functools.partial(key_body, scale),
            [lanes] * 3 + [None] * 2 + [lead] * 2,
            [lanes, lanes, lead],
            [flat_half, flat_half, sds((pairs, 2 * rows, 128), F32)],
            us=6.0, steps=pairs,
        )(info, key[0], value[0], query[s], messages[s], ids[s], bar_t, rm, deps=deps)

    grads = {0: key_call(0, (ffn_pieces[0],))}
    def query_call(deps):
        return call(
            functools.partial(query_body, scale, places),
            [None, None, lanes, lead, lanes] + [lanes] * places + [lead_two] * places
            + [lanes] * (2 * places),
            [lanes],
            [flat_half],
            us=10.0, steps=pairs,
        )(info, ids[0], message, mem, rm, lse_col, *tops, *probs, *key, *value, deps=deps)[0]

    last = grads[0][0]
    dqm = None
    for i, stage in enumerate(stages):
        deps = (last,)
        if i + 1 < len(stages):
            sent = hold([message], (last,))[0]
            messages.update({s: along(sent, s) for s in stages[i + 1]})
            deps = (sent,)
        if dqm is None:
            dqm = query_call(deps)
            deps = (dqm,)
        for s in stage:
            if s == order[-1]:
                ffn_ends = reduce_second(ffn_pieces, ffn_got, (last,))
                deps = (ffn_ends[0],)
            grads[s] = key_call(s, deps)
            last = grads[s][0]
            deps = (last,)
    dks, dvs, drs = zip(*[grads[s] for s in range(places)])

    dq, dk, dv = call(
        functools.partial(cluster_back_body, scale, places),
        [None] + [lead] * 2 + [lanes] * (2 * places + 1) + [lead] * (2 * places) + [lanes] * (2 * places),
        [lanes] * 3,
        [sds((own, half), BF)] * 3,
        us=10.0, steps=pairs,
    )(info, ids[0], cen, cst, dqm, *key, *value, *bars, *drs, *dks, *dvs)

    qkv_rows = padded(3 * chunk + 16)
    per_one = qkv_rows // q_count
    specs, shapes = chunk_outs(qkv_rows)
    dn_mine, dn_send, *qkv_pieces = call(
        functools.partial(qkv_grad_body, places, q_count, per_one),
        [None] * 4 + [my_columns] * 3 + [None] * 2,
        [None] * 2 + specs,
        [sds((block, width), F32)] * 2 + shapes,
        scratch=[pltpu.VMEM((places, 2, qkv_rows, half), BF), pltpu.VMEM((own, width), F32)],
        us=7.0,
    )(info, normed, dq, dk, dv, w_query, w_key, w_value, packed, packed_other)
    qkv_got = reduce_first(qkv_pieces)
    ffn_third = reduce_third(ffn_ends, (dn_mine,))
    input_grad = call(
        input_body,
        [None] * 5,
        [None],
        [sds((block, width), F32)],
        us=2.3,
    )(info, x, gain_one, dn_mine, swap(dn_send), d_mid)[0]

    qkv_ends = reduce_second(qkv_pieces, qkv_got)
    qkv_third = reduce_third(qkv_ends, deps=(input_grad,))
    ffn_total = reduce_total(*ffn_third[:2], deps=(qkv_third[0],))
    ffn_parts = spread(*ffn_total)
    grad_up, grad_down, grad_out, vec_two = call(
        functools.partial(ffn_out_body, q_count, per),
        [None] * q_count,
        [None] * 4,
        [sds((chunk, hidden), F32), sds((down_chunk, width), F32), sds((chunk, width), F32),
         sds((16, half), F32)],
        scratch=[pltpu.VMEM((2, ffn_rows, half), BF)],
        us=3.0,
    )(info, *ffn_parts)
    qkv_parts = spread(*reduce_total(*qkv_third[:2], deps=(grad_up,)))
    grad_query, grad_key, grad_value, vec_one = call(
        functools.partial(qkv_out_body, q_count, per_one),
        [None] * q_count,
        [None] * 4,
        [sds((chunk, width), F32)] * 3 + [sds((16, half), F32)],
        scratch=[pltpu.VMEM((2, qkv_rows, half), BF)],
        us=1.5,
    )(info, *qkv_parts)

    def vectors(lines):
        both = lines[:4].reshape(2, width)
        cut = lax.dynamic_slice_in_dim(both, index * chunk, chunk, 1)
        return cut[0], cut[1]

    grad_gain_one, grad_bias_one = vectors(vec_one)
    grad_gain_two, grad_bias_two = vectors(vec_two)
    return (out[None], input_grad[None], grad_gain_one, grad_bias_one, grad_query, grad_key,
            grad_value, grad_out, grad_gain_two, grad_bias_two, grad_up, grad_down)


def solution(mesh):
    split = P("seq", "ctx", None)
    in_specs = (split,) + (P(),) * 10 + (split, split, P("seq", None, None, None))
    vec, mat = P("ctx"), P("ctx", None)
    out_specs = (split, split, vec, vec, mat, mat, mat, mat, vec, vec, mat, mat)
    return jax.shard_map(
        per_device, mesh=mesh, in_specs=in_specs, out_specs=out_specs, check_vma=False
    )
```

```python
import functools
import math

import jax
import jax.numpy as jnp
import numpy as np
from jax import lax
from jax.experimental import pallas as pl
from jax.experimental.pallas import tpu as pltpu
from jax.sharding import PartitionSpec as P

EPS = 1e-05
NEG = -1e30
F32 = jnp.float32
BF = jnp.bfloat16
COST = 0.5
ANY = pl.BlockSpec(memory_space=pl.ANY)
VMEM_BYTES = 7 * 1024 * 1024


def dot(a, b):
    return lax.dot_general(a, b, (((1,), (0,)), ((), ())), preferred_element_type=F32)


def dot_nt(a, b):
    return lax.dot_general(a, b, (((1,), (1,)), ((), ())), preferred_element_type=F32)


def dot_tn(a, b):
    return lax.dot_general(a, b, (((0,), (0,)), ((), ())), preferred_element_type=F32)


def low_half():
    return lax.broadcasted_iota(jnp.int32, (1, 128), 1) < 64


def norm_parts(x):
    center = x - jnp.mean(x, -1, keepdims=True)
    spread = jnp.mean(center * center, -1, keepdims=True)
    rstd = lax.rsqrt(spread + EPS)
    return center * rstd, rstd


def norm_back(d_normed, xhat, rstd, gain):
    d_hat = d_normed * gain
    first = jnp.mean(d_hat, -1, keepdims=True)
    second = jnp.mean(d_hat * xhat, -1, keepdims=True)
    return rstd * (d_hat - first - xhat * second)


def rows_at(index, size):
    return pl.ds(pl.multiple_of(index * size, size), size)


def call(body, in_views, out_views, out_shape, scratch=(), us=1.0, vmem=VMEM_BYTES, steps=None):
    views = list(in_views) + list(out_views)
    taken = 1 + len(in_views)

    def run(info, *args, deps=()):
        def kernel(*refs):
            scalars, arrays = refs[0], refs[1:taken] + refs[taken + len(deps) :]
            for step in range(steps or 1):
                seen = [
                    r if v is None else v(r, step, scalars)
                    for r, v in zip(arrays, views + [None] * len(scratch))
                ]
                if steps is None:
                    body(scalars, *seen)
                else:
                    body(step, scalars, *seen)

        return pl.pallas_call(
            kernel,
            in_specs=[pl.BlockSpec(memory_space=pltpu.SMEM)]
            + [pl.BlockSpec(memory_space=pltpu.VMEM)] * len(in_views)
            + [ANY] * len(deps),
            out_specs=[pl.BlockSpec(memory_space=pltpu.VMEM)] * len(out_views),
            out_shape=out_shape,
            scratch_shapes=list(scratch),
            compiler_params=pltpu.CompilerParams(vmem_limit_bytes=vmem),
            cost_estimate=pl.CostEstimate(
                flops=int(us * COST * 1.1e9), bytes_accessed=int(us * COST * 1e6), transcendentals=0
            ),
        )(info, *args, *deps)

    return run


def lanes(ref, p, info):
    return ref.at[:, p * 128 : (p + 1) * 128]


def lead(ref, p, info):
    return ref.at[p : p + 1]


def lead_two(ref, p, info):
    return ref.at[2 * p : 2 * p + 2]


def half_lanes(ref, p, info):
    half = ref.shape[1] // 2
    return ref.at[:, pl.ds(pl.multiple_of(info[0] * half + p * 128, 128), 128)]


def my_columns(ref, p, info):
    half = ref.shape[1] // 2
    return ref.at[:, pl.ds(pl.multiple_of(info[0] * half, 128), half)]


def my_rows(ref, p, info):
    return ref.at[rows_at(info[0], ref.shape[0] // 2), :]


def other_rows(ref, p, info):
    return ref.at[rows_at(1 - info[0], ref.shape[0] // 2), :]


def split3(x):
    first = x.astype(BF)
    left = x - first.astype(F32)
    second = left.astype(BF)
    return first, second, (left - second.astype(F32)).astype(BF)


def half_of(e):
    lo = low_half()
    return lo if e == 0 else ~lo


def spare(e):
    lane = lax.broadcasted_iota(jnp.int32, (1, 128), 1)
    base = 64 if e == 0 else 0
    return [lane == base + i for i in range(3)]


def spare_ones(e):
    marks = spare(e)
    return jnp.where(marks[0] | marks[1] | marks[2], 1.0, 0.0).astype(BF)


def hits_of(ids_row, rows):
    return lax.broadcasted_iota(jnp.int32, (rows, ids_row.shape[1]), 0) == ids_row


def as_hot(hits):
    return jnp.where(hits, 1.0, 0.0).astype(BF)


def top_offsets(tops, stride):
    lane = lax.broadcasted_iota(jnp.int32, tops.shape, 1)
    return (tops - lane * stride).astype(F32).astype(BF)


def top_mask(offs, own, stride, slot):
    shape = (offs.shape[1], own)
    lane = lax.broadcasted_iota(jnp.int32, shape, 1)
    ranges = (lane >> int(math.log2(stride))) + slot * (own // stride)
    expand = as_hot(ranges == lax.broadcasted_iota(jnp.int32, shape, 0))
    spot = (lax.broadcasted_iota(jnp.int32, (1, own), 1) & (stride - 1)).astype(F32)
    return dot(offs, expand) == spot


def chip_at(info, slot):
    return info[1] ^ slot


def pair_tops(tops, p, info, stride):
    _, rows, chosen = tops.shape
    first = info[0] * (tops.shape[0] // 2) + 2 * p
    return top_offsets(tops[pl.ds(first, 2)].reshape(2 * rows, chosen), stride)


def pair_ids(ids, p, info):
    return [ids[2 * p + e : 2 * p + e + 1, :] for e in range(2)]


def pair_rows(rows):
    row = lax.broadcasted_iota(jnp.int32, (2 * rows, 128), 0)
    lane = lax.broadcasted_iota(jnp.int32, (2 * rows, 128), 1)
    column = lax.broadcasted_iota(jnp.int32, (2 * rows, 1), 0)
    return (row < rows) == (lane < 64), column < rows


def pair_hot(lines, rows):
    return jnp.concatenate([as_hot(hits_of(line, rows)) for line in lines], axis=0)


def slot_body(slot, scale, stride, p, info, xa, xb, gain, bias, wq, wk, wv, tops, *rest):
    first = slot == 0
    if first:
        q_out, k_out, v_out, csum, acc, den, top, prob, ids, bar_out, n_out, bar_t, normed = rest
        ids_own = ids
    else:
        ids_own, q_own, q_out, k_out, v_out, csum, acc, den, top, prob, ids, bar_out, normed = rest
    rows = tops.shape[1]
    core = info[0]
    block = xa.shape[0] - 16
    own = 2 * block

    if p == 0:
        for rel, ref in enumerate((xa, xb)):
            at = rows_at(core ^ rel, block)
            xhat, _ = norm_parts(ref[:block, :].astype(F32))
            low = (xhat * gain[...][None] + bias[...][None]).astype(BF)
            normed[at, :] = low
            if first:
                n_out[at, :] = low
        lines = [ref[block:, :block].astype(F32) for ref in (xa, xb)]
        heads = tops.shape[0] // 2
        lines = [jnp.where(core == 0, a[:heads], a[heads : 2 * heads]) for a in lines]
        lines = jnp.where(
            core == 0,
            jnp.concatenate(lines, axis=1),
            jnp.concatenate(lines[::-1], axis=1),
        )
        ids[:heads, :] = lines.astype(jnp.int32)

    weights = jnp.concatenate([wq[...], wk[...], wv[...]], axis=1)
    made = dot(normed[...], weights).astype(BF)
    query, key, value = made[:, :128], made[:, 128:256], made[:, 256:]
    q_out[...] = query
    k_out[...] = key
    v_out[...] = value
    key_t = key.T
    asked = (query if first else q_own[...]) * jnp.asarray(scale, BF)
    peaks, outs = [], []
    one = jnp.ones((), BF)
    hot = pair_hot(pair_ids(ids, p, info), rows)
    hot_own = (hot if first else pair_hot(pair_ids(ids_own, p, info), rows)).T
    count = jnp.sum(hot.astype(F32), axis=1, keepdims=True)
    csum[0] = jnp.where(pair_rows(rows)[0], dot(hot, query), count)
    mask = top_mask(pair_tops(tops, p, info, stride), own, stride, chip_at(info, slot))
    bars = jnp.where(mask, 0.0, NEG).astype(BF)
    bar_out[0] = bars
    if first:
        bar_t[0] = bars.T
    for e in range(2):
        sel = half_of(e)
        bar = bars[e * rows : (e + 1) * rows]
        right = jnp.concatenate([key_t, bar], axis=0)
        member_of = hot_own[:, e * rows : (e + 1) * rows]
        left = jnp.concatenate([jnp.where(sel, asked, jnp.zeros((), BF)), member_of], axis=1)
        score = dot(left, right)
        peak = jnp.max(score, axis=1, keepdims=True)
        grown = jnp.exp(score - peak).astype(BF)
        prob[e] = grown
        peaks.append(peak)
        outs.append(dot(grown, jnp.where(sel, value, one)))
    lo = low_half()
    acc[...] = jnp.where(lo, outs[0], outs[1])
    den[...] = pltpu.roll(jnp.where(lo, outs[1], outs[0]), 64, 1)
    top[...] = jnp.where(lo, peaks[0], peaks[1])


def cluster_body(scale, slots, p, info, ids_own, *rest):
    ks, vs, bars, csums, accs, dens, tops = (rest[i * slots : (i + 1) * slots] for i in range(7))
    att, mem, lse, lse_col, rm, cen, cst = rest[7 * slots :]
    keys = jnp.concatenate([k[...] for k in ks], axis=0)
    values = jnp.concatenate([v[...] for v in vs], axis=0)
    own = ks[0].shape[0]
    rows = bars[0].shape[1] // 2
    lo = low_half()
    lane = lax.broadcasted_iota(jnp.int32, (1, 128), 1)
    sel, upper = pair_rows(rows)
    sums = csums[0][0]
    for c in csums[1:]:
        sums = sums + c[0]
    safe = jnp.maximum(jnp.where(upper, sums[:, 64:65], sums[:, 0:1]), 1.0)
    center = jnp.where(sel, sums / safe, 0.0).astype(BF)
    score = dot_nt(center * jnp.asarray(scale, BF), keys)
    peak = jnp.max(score, axis=1, keepdims=True)
    grown = jnp.exp(score - peak)
    total = jnp.sum(grown, axis=1, keepdims=True)
    inverse = 1.0 / total
    mask = jnp.concatenate([b[0] for b in bars], axis=1) == 0
    mass = (jnp.sum(jnp.where(mask, grown, 0.0), axis=1, keepdims=True) * inverse).astype(BF)
    kept = jnp.where(mask, 0.0, grown).astype(BF)
    attended = jnp.where(sel, dot(kept, values) * inverse, 0.0).astype(BF)
    wide = jnp.where(sel, mass, jnp.zeros((), BF))
    both = jnp.concatenate([attended, wide], axis=1)
    cen[0] = center
    cst[0] = jnp.where(lane == 0, peak + jnp.log(total), safe)
    rm[0] = both
    hot = pair_hot(pair_ids(ids_own, p, info), rows)
    token = dot_tn(hot, both)
    peak = tops[0][...]
    for t in tops[1:]:
        peak = jnp.maximum(peak, t[...])
    total, member = 0.0, 0.0
    for t, d, a in zip(tops, dens, accs):
        weight = jnp.exp(t[...] - peak)
        total += weight * d[...]
        member += weight * a[...]
    member = member / total
    log_total = peak + jnp.log(total)
    lse_col[...] = log_total
    turned = log_total.T
    lse[0] = jnp.concatenate([turned[0:1], turned[64:65], jnp.zeros((6, own), F32)], axis=0)
    mem[...] = member
    att[...] = (token[:, 128:] * member + token[:, :128]).astype(BF)


def ffn_body(steps, step, info, x, cot, att_mine, att_other, wo_mine, wo_other, gain, bias, w_up,
             w_down, out, d_mid, d_attn, da_mine, da_other, normed_out, act_out, du_mine, du_send,
             vecs, acc, dacc):
    if step == 0:
        mid = x[...].astype(F32) + dot(att_mine[...], wo_mine[...]) + dot(att_other[...], wo_other[...])
        d_mid[...] = mid
        xhat, _ = norm_parts(mid)
        normed_out[...] = (xhat * gain[...][None] + bias[...][None]).astype(BF)
    upper = dot(normed_out[...], w_up[...])
    c0 = math.sqrt(2.0 / math.pi)
    square = upper * upper
    tanh = jnp.tanh(c0 * (upper + 0.044715 * square * upper))
    cdf = 0.5 * (1.0 + tanh)
    active = (upper * cdf).astype(BF)
    act_out[...] = active
    more = dot(active, w_down[...])
    acc[...] = more + (d_mid[...] if step == 0 else acc[...])
    slope = cdf + 0.5 * upper * (1.0 - tanh * tanh) * (c0 * (1.0 + 3 * 0.044715 * square))
    d_upper = (dot_nt(cot[...], w_down[...]) * slope).astype(BF)
    half = d_upper.shape[1] // 2
    first = info[0] == 0
    du_mine[0] = jnp.where(first, d_upper[:, :half], d_upper[:, half:])
    du_send[0] = jnp.where(first, d_upper[:, half:], d_upper[:, :half])
    more = dot_nt(d_upper, w_up[...])
    dacc[...] = more if step == 0 else dacc[...] + more
    if step == steps - 1:
        out[...] = acc[...]
        xhat, rstd = norm_parts(d_mid[...])
        d_normed = dacc[...]
        vecs[...] = jnp.concatenate(
            [
                jnp.sum(d_normed * xhat, axis=0, keepdims=True),
                jnp.sum(d_normed, axis=0, keepdims=True),
                jnp.zeros((6, d_normed.shape[1]), F32),
            ],
            axis=0,
        )
        grad = cot[...].astype(F32) + norm_back(d_normed, xhat, rstd, gain[...][None])
        d_mid[...] = grad
        low = grad.astype(BF)
        d_attn[...] = low
        da_mine[...] = dot_nt(low, wo_mine[...]).astype(BF)
        da_other[...] = dot_nt(low, wo_other[...]).astype(BF)


def join_body(info, mine, other, mem, lse, joined):
    core = info[0]
    block, half = mine.shape
    lo = low_half()
    lane = lax.broadcasted_iota(jnp.int32, (1, 128), 1)
    found = {}
    for rel, ref in enumerate((mine, other)):
        at = rows_at(core ^ rel, block)
        joined[at, :] = ref[...]
        for p in range(half // 128):
            part = slice(p * 128, (p + 1) * 128)
            product = ref[:, part].astype(F32) * mem[at, part]
            first = jnp.sum(jnp.where(lo, product, 0.0), axis=1, keepdims=True)
            second = jnp.sum(jnp.where(lo, 0.0, product), axis=1, keepdims=True)
            table = jnp.where(lane == 0, first, jnp.where(lane == 1, second, 0.0)).T
            stat = lse[p, :, at]
            for e in range(2):
                found[p, e, rel] = split3(table[e : e + 1])[:2] + split3(-stat[e : e + 1])
    lines = []
    for p in range(half // 128):
        for e in range(2):
            for rel in range(2):
                lines += [line.astype(F32) for line in found[p, e, rel]]
    lines.append(jnp.zeros((64 - len(lines), block), F32))
    table = jnp.concatenate(lines, axis=0).astype(BF)
    joined[2 * block :, :] = jnp.concatenate(
        [table, jnp.zeros((64, half - block), BF)], axis=1
    )


def query_body(scale, slots, p, info, ids_own, message, mem, rm, lse_col, *rest):
    tops, probs, ks, vs = (rest[i * slots : (i + 1) * slots] for i in range(4))
    dq = rest[4 * slots]
    own = mem.shape[0]
    rows = rm.shape[1] // 2
    lo = low_half()
    hot = pair_hot(pair_ids(ids_own, p, info), rows)
    mass = dot_tn(hot, rm[0, :, 128:])
    grad = message[:own, p * 128 : (p + 1) * 128].astype(F32)
    product = grad * mem[...]
    d_member = (mass * grad).astype(BF)
    lefts = []
    for e in range(2):
        sel = half_of(e)
        other = 0 if e == 0 else 64
        delta = mass[:, other : other + 1] * jnp.sum(
            jnp.where(sel, product, 0.0), axis=1, keepdims=True
        )
        left = jnp.where(sel, d_member, jnp.zeros((), BF))
        for mark, term in zip(spare(e), split3(-delta)):
            left = jnp.where(mark, term, left)
        lefts.append(left)
    total = 0.0
    for s in range(slots):
        d_scores = []
        for e in range(2):
            right = jnp.where(half_of(e), vs[s][...], spare_ones(e))
            moved = dot_nt(lefts[e], right)
            d_scores.append((probs[s][e].astype(F32) * moved).astype(BF))
        made = dot(jnp.concatenate(d_scores, axis=0), ks[s][...])
        total += jnp.exp(tops[s][...] - lse_col[...]) * jnp.where(lo, made[:own], made[own:])
    dq[...] = total * scale


def key_body(scale, p, info, k_own, v_own, query, message, ids, bar_t, rm, dk, dv, dr):
    core = info[0]
    own = k_own.shape[0]
    block = own // 2
    rows = rm.shape[1] // 2
    lo = low_half()
    picked = message[own:, :block].astype(F32)[20 * p : 20 * p + 20]
    datt = message[:own, p * 128 : (p + 1) * 128]

    def term(e, i):
        a, b = picked[10 * e + i : 10 * e + i + 1], picked[10 * e + 5 + i : 10 * e + 6 + i]
        return jnp.where(
            core == 0, jnp.concatenate([a, b], axis=1), jnp.concatenate([b, a], axis=1)
        )

    hot = [as_hot(hits_of(line, rows)) for line in pair_ids(ids, p, info)]
    mass_t = dot_tn(rm[0, :, 128:], jnp.concatenate(hot, axis=0))
    grad = datt
    dm_t = (mass_t * grad.T.astype(F32)).astype(BF)
    d_member = dm_t.T
    asked = query[...]
    asked_t = asked.T
    blank = jnp.zeros((48, own), BF)
    weights, d_scores, d_masses = [], [], []
    pad = jnp.zeros((13, own), F32)
    for e in range(2):
        sel = half_of(e)
        other = 0 if e == 0 else 64
        d_mass = term(e, 0) + term(e, 1)
        d_masses.append(d_mass)
        delta = mass_t[other : other + 1] * d_mass
        aux_s = jnp.concatenate([term(e, 2), term(e, 3), term(e, 4), pad], axis=0).astype(BF)
        aux_d = jnp.concatenate([t.astype(F32) for t in split3(-delta)] + [pad], axis=0).astype(BF)

        def beside(turned, aux):
            if e == 0:
                return jnp.concatenate([turned[:64], aux, blank], axis=0)
            return jnp.concatenate([aux, blank, turned[64:]], axis=0)

        right = jnp.concatenate([beside(asked_t, aux_s), hot[e]], axis=0)
        bar = bar_t[0, :, e * rows : (e + 1) * rows]
        ones = spare_ones(e)
        left = jnp.concatenate(
            [jnp.where(sel, k_own[...] * jnp.asarray(scale, BF), ones), bar], axis=1
        )
        weight = jnp.exp(dot(left, right))
        moved = dot(jnp.where(sel, v_own[...], ones), beside(dm_t, aux_d))
        weights.append(weight.astype(BF))
        d_scores.append((weight * moved).astype(BF))
    made = dot(jnp.concatenate(weights, axis=0), d_member)
    dv[...] = jnp.where(lo, made[:own], made[own:])
    made = dot(jnp.concatenate(d_scores, axis=0), asked)
    dk[...] = jnp.where(lo, made[:own], made[own:])
    hot_both = jnp.concatenate(hot, axis=0)
    d_mass_c = jnp.concatenate(
        [jnp.sum(h.astype(F32) * m, axis=1, keepdims=True) for h, m in zip(hot, d_masses)], axis=0
    )
    dr[0] = jnp.where(pair_rows(rows)[0], dot(hot_both, grad), d_mass_c)


def cluster_back_body(scale, slots, p, info, ids_own, cen, cst, dqm, *rest):
    ks, vs, bars, drs, dks, dvs = (rest[i * slots : (i + 1) * slots] for i in range(6))
    dq, dk, dv = rest[6 * slots :]
    own = ks[0].shape[0]
    keys = jnp.concatenate([k[...] for k in ks], axis=0)
    values = jnp.concatenate([v[...] for v in vs], axis=0)
    rows = cen.shape[1] // 2
    sel, upper = pair_rows(rows)
    log_total, safe = cst[0, :, 0:1], cst[0, :, 1:2]
    both = drs[0][0]
    for r in drs[1:]:
        both = both + r[0]
    d_rest = jnp.where(sel, both, 0.0).astype(BF)
    d_mass = jnp.where(upper, both[:, 64:65], both[:, 0:1])
    cprob = jnp.exp(dot_nt(cen[0] * jnp.asarray(scale, BF), keys) - log_total)
    mask = jnp.concatenate([b[0] for b in bars], axis=1) == 0
    d_prob = jnp.where(mask, d_mass, dot_nt(d_rest, values))
    inner = jnp.sum(cprob * d_prob, axis=1, keepdims=True)
    d_score = (cprob * (d_prob - inner)).astype(BF)
    keeps = jnp.where(mask[:, :own], 0.0, cprob[:, :own]).astype(BF)
    d_sums = jnp.where(sel, dot(d_score, keys) * (scale / safe), 0.0).astype(BF)
    hot = pair_hot(pair_ids(ids_own, p, info), rows)
    dq[...] = (dqm[...] + dot_tn(hot, d_sums)).astype(BF)
    d_key = dot_tn(d_score[:, :own], cen[0])
    d_value = dot_tn(keeps, d_rest)
    for a, b in zip(dks, dvs):
        d_key = d_key + a[...]
        d_value = d_value + b[...]
    dk[...] = (d_key * scale).astype(BF)
    dv[...] = d_value.astype(BF)


def halving_orders(count):
    bits = (count - 1).bit_length()
    low = sorted(range(count), key=lambda r: int(format(r, "0%db" % bits)[::-1], 2) if bits else 0)
    return low, list(range(count))


def emit_chunks(info, flat, outs, places, q_count, per):
    core, place, mine = info[0], info[1], info[2]
    for rel, order in enumerate(halving_orders(q_count)):
        for i, r in enumerate(order):
            out = outs[2 * rel + (0 if i < q_count // 2 else 1)]
            for s in range(places):
                at = place ^ s
                out[i % (q_count // 2), s] = flat[at, core ^ rel, rows_at(mine ^ r, per), :]


def store_rows(flat, value, row, chunk):
    for owner in range(value.shape[0] // chunk):
        flat[owner // 2, owner % 2, row : row + chunk, :] = value[
            owner * chunk : (owner + 1) * chunk
        ].astype(BF)


def store_vecs(flat, vecs, row):
    half = vecs.shape[1] // 2
    lines = jnp.concatenate(
        [vecs[0:1, :half], vecs[0:1, half:], vecs[1:2, :half], vecs[1:2, half:]]
        + [jnp.zeros((12, half), F32)],
        axis=0,
    ).astype(BF)
    for z in range(flat.shape[0]):
        for c in range(2):
            flat[z, c, row : row + 16, :] = lines


def ffn_grad_body(places, q_count, per, info, n_mine, n_other, du_mine, du_other, act_mine, act_other,
                  cot_mine, cot_other, att_mine, att_other, da_mine, da_other, vecs, *rest):
    outs, (flat,) = rest[:-1], rest[-1:]
    core = info[0]
    width = n_mine.shape[1]
    chunk = width // (2 * places)
    step_count = du_mine.shape[0]
    hidden = act_mine.shape[1]
    down_chunk = hidden // (2 * places)
    block = n_mine.shape[0]
    n_t = [n_mine[...].T, n_other[...].T]
    n_t = jnp.concatenate(n_t, axis=1)
    half = du_mine.shape[2]
    for f in range(0, step_count, 2):
        right = [jnp.concatenate([du_mine[i], du_other[i]], axis=0) for i in (f, f + 1)]
        up = dot(n_t, jnp.concatenate(right, axis=1))
        for i in range(2):
            store_rows(flat, up[:, i * half : (i + 1) * half], (f + i) * chunk, chunk)
    base = step_count * chunk
    span = hidden // step_count
    for f in range(step_count):
        part = slice(f * span, (f + 1) * span)
        down = dot_tn(act_mine[:, part], cot_mine[...]) + dot_tn(act_other[:, part], cot_other[...])
        for i in range(span // down_chunk):
            owner = f * (span // down_chunk) + i
            flat[owner // 2, owner % 2, base : base + down_chunk, :] = down[
                i * down_chunk : (i + 1) * down_chunk
            ].astype(BF)
    base += down_chunk
    mine_rows, other_rows = rows_at(core, block), rows_at(1 - core, block)
    halves = []
    for ref in (att_mine, att_other):
        halves.append(
            dot_tn(ref[mine_rows, :], da_mine[...]) + dot_tn(ref[other_rows, :], da_other[...])
        )
    first = core == 0
    store_rows(
        flat,
        jnp.concatenate(
            [jnp.where(first, halves[0], halves[1]), jnp.where(first, halves[1], halves[0])], axis=0
        ),
        base,
        chunk,
    )
    base += chunk
    store_vecs(flat, vecs[...], base)
    emit_chunks(info, flat, outs, places, q_count, per)


def qkv_grad_body(places, q_count, per, info, normed, dq, dk, dv, wq, wk, wv, xa, xb, *rest):
    dn_mine, dn_send = rest[0], rest[1]
    outs, flat, d_all = rest[2:-2], rest[-2], rest[-1]
    core = info[0]
    block, width = dn_mine.shape
    chunk = width // (2 * places)
    n_t = normed[...].T
    half = dq.shape[1]
    grads = jnp.concatenate([dq[...], dk[...], dv[...]], axis=1)
    made = dot(n_t, grads)
    for i in range(3):
        store_rows(flat, made[:, i * half : (i + 1) * half], i * chunk, chunk)
    weights = jnp.concatenate([wq[...], wk[...], wv[...]], axis=1)
    d_all[...] = dot_nt(grads, weights)
    gains, biases = 0.0, 0.0
    for rel, (ref, out) in enumerate(((xa, dn_mine), (xb, dn_send))):
        rows = rows_at(core ^ rel, block)
        d_normed = d_all[rows, :]
        out[...] = d_normed
        xhat, _ = norm_parts(ref[:block, :].astype(F32))
        gains += jnp.sum(d_normed * xhat, axis=0, keepdims=True)
        biases += jnp.sum(d_normed, axis=0, keepdims=True)
    store_vecs(flat, jnp.concatenate([gains, biases], axis=0), 3 * chunk)
    emit_chunks(info, flat, outs, places, q_count, per)


def input_body(info, x, gain, dn_mine, dn_other, d_mid, out):
    xhat, rstd = norm_parts(x[...].astype(F32))
    out[...] = d_mid[...] + norm_back(dn_mine[...] + dn_other[...], xhat, rstd, gain[...][None])


def gather_flat(info, parts, flat, per):
    own = info[2]
    for i, part in enumerate(parts):
        rows = rows_at(own ^ (i // 2), per)
        flat[i % 2, rows, :] = part[...] if len(part.shape) == 2 else part[i % 2]


def emit_vecs(info, lines, outs, chunk):
    for i, out in enumerate(outs):
        whole = jnp.concatenate([lines[2 * i : 2 * i + 1], lines[2 * i + 1 : 2 * i + 2]], axis=1)
        width = whole.shape[1]
        whole = jnp.concatenate([whole, jnp.zeros((7, width), F32)], axis=0)
        shift = width - (2 * info[1] + info[0]) * chunk
        out[...] = pltpu.roll(whole, shift, 1)[0:1, :chunk]


def ffn_out_body(q_count, per, info, *rest):
    up, down, out, gain, bias, flat = rest[2 * q_count :]
    gather_flat(info, rest[: 2 * q_count], flat, per)
    core = info[0]
    half = flat.shape[2]
    chunk = up.shape[0]
    steps = up.shape[1] // (2 * half)
    for c in range(2):
        src = core ^ c
        for f in range(steps):
            at = (2 * f + c) * half
            up[:, at : at + half] = flat[src, f * chunk : (f + 1) * chunk, :].astype(F32)
        base = steps * chunk
        down[:, c * half : (c + 1) * half] = flat[src, base : base + down.shape[0], :].astype(F32)
        base += down.shape[0]
        out[:, c * half : (c + 1) * half] = flat[src, base : base + chunk, :].astype(F32)
        base += chunk
    lines = flat[0, base : base + 16, :].astype(F32) + flat[1, base : base + 16, :].astype(F32)
    emit_vecs(info, lines, (gain, bias), chunk)


def qkv_out_body(q_count, per, info, *rest):
    outs, gain, bias, flat = rest[2 * q_count : 2 * q_count + 3], rest[-3], rest[-2], rest[-1]
    gather_flat(info, rest[: 2 * q_count], flat, per)
    core = info[0]
    half = flat.shape[2]
    chunk = outs[0].shape[0]
    for c in range(2):
        src = core ^ c
        for i, out in enumerate(outs):
            out[:, c * half : (c + 1) * half] = flat[src, i * chunk : (i + 1) * chunk, :].astype(F32)
    base = 3 * chunk
    lines = flat[0, base : base + 16, :].astype(F32) + flat[1, base : base + 16, :].astype(F32)
    emit_vecs(info, lines, (gain, bias), chunk)


def pack_body(info, x, ids, out):
    block, width = x.shape
    heads = ids.shape[0]
    out[:block, :] = x[...]
    lines = jnp.concatenate([ids[...].astype(F32), jnp.zeros((16 - heads, block), F32)], axis=0)
    out[block:, :] = jnp.concatenate(
        [lines, jnp.zeros((16, width - block), F32)], axis=1
    ).astype(BF)


def hold_body(info, *refs):
    count = len(refs) // 2
    for source, target in zip(refs[:count], refs[count:]):
        target[...] = source[...]


def fold_body(info, keep_a, came_a, keep_b, came_b, *outs):
    for i, (keep, came) in enumerate(((keep_a, came_a), (keep_b, came_b))):
        cut = keep.shape[0] // 2
        for j in range(2):
            part = slice(j * cut, (j + 1) * cut)
            outs[2 * i + j][...] = (keep[part].astype(F32) + came[part].astype(F32)).astype(BF)


def merge_body(info, keep_a, came_a, keep_b, came_b, *outs):
    for s, out in enumerate(outs):
        out[0] = (keep_a[0, s].astype(F32) + came_a[0, s].astype(F32)).astype(BF)
        out[1] = (keep_b[0, s].astype(F32) + came_b[0, s].astype(F32)).astype(BF)


def sum_body(info, *refs):
    total = refs[0][...].astype(F32)
    for ref in refs[1:-1]:
        total = total + ref[...].astype(F32)
    refs[-1][...] = total.astype(BF)


def total_body(info, *refs):
    parts, stay, go = refs[:-2], refs[-2], refs[-1]
    for i, out in enumerate((stay, go)):
        total = parts[0][i].astype(F32)
        for part in parts[1:]:
            total = total + part[i].astype(F32)
        out[...] = total.astype(BF)


def per_device(tokens, gain_one, bias_one, w_query, w_key, w_value, w_out, gain_two, bias_two,
               w_up, w_down, cotangent, cluster_ids, top_keys):
    _, block, width = tokens.shape
    heads = cluster_ids.shape[2]
    clusters, chosen = top_keys.shape[2], top_keys.shape[3]
    ctx, q_count = lax.axis_size("ctx"), lax.axis_size("seq")
    places = ctx // 2
    index, mine = lax.axis_index("ctx"), lax.axis_index("seq")
    core, place = index % 2, index // 2
    full_len = block * ctx
    own = 2 * block
    half = width // 2
    hidden = w_up.shape[1]
    pairs = half // 128
    stride = full_len // chosen
    rows = -(-clusters // 128) * 128
    scale = 1.0 / math.sqrt(width // heads)
    info = jnp.stack([core, place, mine]).astype(jnp.int32)
    sds = jax.ShapeDtypeStruct
    swap_to = [(i, i ^ 1) for i in range(ctx)]

    def swap(a):
        return lax.ppermute(a, "ctx", swap_to)

    def along(a, s):
        to = [(2 * z + c, 2 * (z ^ s) + c) for z in range(places) for c in range(2)]
        return lax.ppermute(a, "ctx", to)

    def hold(arrays, deps):
        shapes = [sds(a.shape, a.dtype) for a in arrays]
        return call(hold_body, [None] * len(arrays), [None] * len(arrays), shapes)(
            info, *arrays, deps=tuple(deps)
        )

    def across(a, r):
        return lax.ppermute(a, "seq", [(i, i ^ r) for i in range(q_count)])

    hops = [1 << i for i in range((places - 1).bit_length())][::-1]
    known, paths = [0], {}
    for hop in hops:
        paths.update({k ^ hop: (k, hop) for k in known})
        known += [k ^ hop for k in known]
    depth = {0: 0}
    for s in paths:
        depth[s] = depth[paths[s][0]] + 1
    stages = [[s for s in paths if depth[s] == d] for d in range(1, max(depth.values()) + 1)]
    order = [0] + [s for stage in stages for s in stage]

    x, cot = tokens[0], cotangent[0]

    packed = call(pack_body, [None] * 2, [None], [sds((block + 16, width), BF)])(
        info, x, cluster_ids[0].T
    )[0]
    came = {s: along(packed, s) for s in stages[0]}
    packed_other = swap(packed)
    cot_other = swap(cot)
    keys_top = jnp.pad(top_keys[0], ((0, 0), (0, rows - clusters), (0, 0)))

    flat_half = sds((own, half), F32)

    def slot_call(s, xa, xb, slot0=None, deps=()):
        first = s == 0
        in_views = [None] * 4 + [half_lanes] * 3 + [None]
        operands = [xa, xb, gain_one, bias_one, w_query, w_key, w_value, keys_top]
        out_views = [lanes] * 3 + [lead] + [lanes] * 3 + [lead_two, None, lead]
        out_shape = [sds((own, half), BF)] * 3 + [sds((pairs, 2 * rows, 128), F32)]
        out_shape += [flat_half] * 3 + [sds((2 * pairs, own, own), BF), sds((8, own), jnp.int32),
                      sds((pairs, 2 * rows, own), BF)]
        if first:
            out_views += [None, lead]
            out_shape += [sds((own, width), BF), sds((pairs, own, 2 * rows), BF)]
        else:
            in_views += [None, lanes]
            operands += [slot0[8], slot0[0]]
        return call(
            functools.partial(slot_body, s, scale, stride),
            in_views, out_views, out_shape,
            scratch=[pltpu.VMEM((own, width), BF)], us=8.0, steps=pairs,
        )(info, *operands, deps=deps)

    *slot0, normed, bar_t = slot_call(0, packed, packed_other)
    slots = {0: slot0}
    last = slot0[0]
    for i, stage in enumerate(stages):
        done = [slots[s][0] for s in stages[i - 1]] if i else [last]
        arrays = hold([came[s] for s in stage], done)
        held = dict(zip(stage, arrays))
        if i + 1 < len(stages):
            came.update({s: along(held[paths[s][0]], paths[s][1]) for s in stages[i + 1]})
        others = [swap(a) for a in arrays]
        for s, mine_block, other_block in zip(stage, arrays, others):
            deps = (last,) if s == stage[-1] else ()
            slots[s] = slot_call(s, mine_block, other_block, slot0, deps)
            last = slots[s][0] if s == stage[0] else last
    slots = [slots[s] for s in range(places)]
    query, key, value, csums, accs, dens, tops, probs, ids, bars = zip(*slots)

    att, mem, lse, lse_col, rm, cen, cst = call(
        functools.partial(cluster_body, scale, places),
        [None] + [lanes] * (2 * places) + [lead] * (2 * places) + [lanes] * (3 * places),
        [lanes, lanes, lead, lanes, lead, lead, lead],
        [sds((own, half), BF), flat_half, sds((pairs, 8, own), F32), flat_half,
         sds((pairs, 2 * rows, 256), BF), sds((pairs, 2 * rows, 128), BF),
         sds((pairs, 2 * rows, 128), F32)],
        us=10.0, steps=pairs,
    )(info, ids[0], *key, *value, *bars, *csums, *accs, *dens, *tops)

    att_other = swap(att)

    steps = hidden // width
    def step_columns(ref, f, info):
        return ref.at[:, f * width : (f + 1) * width]

    def step_rows(ref, f, info):
        return ref.at[f * width : (f + 1) * width, :]

    out, d_mid, d_attn, da_mine, da_send, normed_two, act, du_mine, du_send, vecs_two = call(
        functools.partial(ffn_body, steps),
        [None, None, my_rows, my_rows, my_rows, other_rows, None, None, step_columns, step_rows],
        [None] * 6 + [step_columns, lead, lead, None],
        [sds((block, width), F32), sds((block, width), F32), sds((block, width), BF),
         sds((block, half), BF), sds((block, half), BF), sds((block, width), BF),
         sds((block, hidden), BF), sds((steps, block, half), BF), sds((steps, block, half), BF),
         sds((8, width), F32)],
        scratch=[pltpu.VMEM((block, width), F32), pltpu.VMEM((block, width), F32)],
        us=13.0, steps=steps,
    )(info, x, cot, att, att_other, w_out, w_out, gain_two, bias_two, w_up, w_down)

    message = call(
        join_body,
        [None] * 4,
        [None],
        [sds((own + 64, half), BF)],
        us=1.5,
    )(info, da_mine, swap(da_send), mem, lse)[0]
    messages = {0: message}
    messages.update({s: along(message, s) for s in stages[0]})

    chunk, down_chunk = width // ctx, hidden // ctx

    def padded(n):
        return -(-n // (16 * q_count)) * 16 * q_count

    def chunk_outs(count):
        shape = (q_count // 2, places, count // q_count, half)
        return [None] * 4, [sds(shape, BF)] * 4

    ffn_rows = padded(steps * chunk + down_chunk + chunk + 16)
    per = ffn_rows // q_count
    ffn_pieces = call(
        functools.partial(ffn_grad_body, places, q_count, per),
        [None] * 6 + [my_columns, my_columns, None, None, my_columns, my_columns, None],
        *chunk_outs(ffn_rows),
        scratch=[pltpu.VMEM((places, 2, ffn_rows, half), BF)],
        us=9.0,
    )(info, normed_two, swap(normed_two), du_mine, swap(du_send), act, swap(act), cot, cot_other,
      att, att_other, d_attn, swap(d_attn), vecs_two, deps=(message,))

    bits = [1 << i for i in range((q_count - 1).bit_length())]

    def reduce_first(pieces):
        return across(pieces[1], bits[0]), across(pieces[3], bits[-1])

    def reduce_second(pieces, got, deps=()):
        ends = [pieces[0], got[0], pieces[2], got[1]]
        for low_bit, high_bit in zip(bits[1:], bits[-2::-1]):
            shape = sds((ends[0].shape[0] // 2,) + ends[0].shape[1:], BF)
            keep_a, send_a, keep_b, send_b = call(fold_body, [None] * 4, [None] * 4, [shape] * 4)(
                info, *ends, deps=deps
            )
            ends = [keep_a, across(send_a, low_bit), keep_b, across(send_b, high_bit)]
        return ends

    def reduce_third(ends, deps=()):
        shape = sds((2,) + ends[0].shape[2:], BF)
        parts = call(merge_body, [None] * 4, [None] * places, [shape] * places)(info, *ends, deps=deps)
        parts = dict(enumerate(parts))
        first = parts[0]
        for stage in stages[:0:-1]:
            added = {}
            for s in stage:
                keep, hop = paths[s]
                added.setdefault(keep, []).append(along(parts.pop(s), hop))
            for keep, others in added.items():
                parts[keep] = sum_call([parts[keep], *others])
        return first, [along(parts[s], paths[s][1]) for s in stages[0]]

    def sum_call(arrays, deps=()):
        shape = sds(arrays[0].shape, BF)
        return call(sum_body, [None] * len(arrays), [None], [shape], us=1.5)(info, *arrays, deps=deps)[0]

    def reduce_total(part, others, deps=()):
        one = sds(part.shape[1:], BF)
        count = 1 + len(others)
        return call(total_body, [None] * count, [None] * 2, [one] * 2, us=1.5)(
            info, part, *others, deps=deps
        )

    def spread(stay, go, relay=False):
        if not relay:
            mixed = jnp.stack([stay, swap(go)])
            return [(mixed, mixed)] + [(a, a) for a in [across(mixed, r) for r in range(1, q_count)]]
        go = swap(go)
        parts = [(stay, go)] + [(across(stay, r), across(go, r)) for r in (1, 2)]
        return parts + [(across(parts[2][0], 1), across(parts[1][1], 2))]

    def flat_parts(parts):
        return [half for pair in parts for half in pair]

    ffn_got = reduce_first(ffn_pieces)

    def key_call(s, deps):
        return call(
            functools.partial(key_body, scale),
            [lanes] * 3 + [None] * 2 + [lead] * 2,
            [lanes, lanes, lead],
            [flat_half, flat_half, sds((pairs, 2 * rows, 128), F32)],
            us=6.0, steps=pairs,
        )(info, key[0], value[0], query[s], messages[s], ids[s], bar_t, rm, deps=deps)

    grads = {0: key_call(0, (ffn_pieces[0],))}
    def query_call(deps):
        return call(
            functools.partial(query_body, scale, places),
            [None, None, lanes, lead, lanes] + [lanes] * places + [lead_two] * places
            + [lanes] * (2 * places),
            [lanes],
            [flat_half],
            us=10.0, steps=pairs,
        )(info, ids[0], message, mem, rm, lse_col, *tops, *probs, *key, *value, deps=deps)[0]

    dqm = query_call((grads[0][0],))
    last = dqm
    for i, stage in enumerate(stages):
        deps = (last,)
        if i + 1 < len(stages):
            begun = {paths[s][0] for s in stages[i + 1]}
            held = hold([messages[k] for k in begun], (last,))
            held = dict(zip(begun, held))
            messages.update({s: along(held[paths[s][0]], paths[s][1]) for s in stages[i + 1]})
            deps = tuple(held.values())
        for s in stage:
            if s == order[-1]:
                ffn_ends = reduce_second(ffn_pieces, ffn_got, (last,))
                deps = (ffn_ends[0],)
            grads[s] = key_call(s, deps)
            last = grads[s][0]
            deps = (last,)
    dks, dvs, drs = zip(*[grads[s] for s in range(places)])

    dq, dk, dv = call(
        functools.partial(cluster_back_body, scale, places),
        [None] + [lead] * 2 + [lanes] * (2 * places + 1) + [lead] * (2 * places) + [lanes] * (2 * places),
        [lanes] * 3,
        [sds((own, half), BF)] * 3,
        us=10.0, steps=pairs,
    )(info, ids[0], cen, cst, dqm, *key, *value, *bars, *drs, *dks, *dvs)

    qkv_rows = padded(3 * chunk + 16)
    per_one = qkv_rows // q_count
    specs, shapes = chunk_outs(qkv_rows)
    dn_mine, dn_send, *qkv_pieces = call(
        functools.partial(qkv_grad_body, places, q_count, per_one),
        [None] * 4 + [my_columns] * 3 + [None] * 2,
        [None] * 2 + specs,
        [sds((block, width), F32)] * 2 + shapes,
        scratch=[pltpu.VMEM((places, 2, qkv_rows, half), BF), pltpu.VMEM((own, width), F32)],
        us=7.0,
    )(info, normed, dq, dk, dv, w_query, w_key, w_value, packed, packed_other)
    qkv_got = reduce_first(qkv_pieces)
    ffn_third = reduce_third(ffn_ends, (dn_mine,))
    input_grad = call(
        input_body,
        [None] * 5,
        [None],
        [sds((block, width), F32)],
        us=2.3,
    )(info, x, gain_one, dn_mine, swap(dn_send), d_mid)[0]

    qkv_ends = reduce_second(qkv_pieces, qkv_got)
    qkv_third = reduce_third(qkv_ends, deps=(input_grad,))
    ffn_total = reduce_total(*ffn_third, deps=(qkv_third[0],))
    ffn_parts = spread(*ffn_total, relay=q_count == 4)
    grad_up, grad_down, grad_out, grad_gain_two, grad_bias_two = call(
        functools.partial(ffn_out_body, q_count, per),
        [None] * (2 * q_count),
        [None] * 5,
        [sds((chunk, hidden), F32), sds((down_chunk, width), F32), sds((chunk, width), F32),
         sds((1, chunk), F32), sds((1, chunk), F32)],
        scratch=[pltpu.VMEM((2, ffn_rows, half), BF)],
        us=3.0,
    )(info, *flat_parts(ffn_parts))
    qkv_parts = spread(*reduce_total(*qkv_third, deps=(ffn_parts[1][0], ffn_parts[2][0])))
    grad_query, grad_key, grad_value, grad_gain_one, grad_bias_one = call(
        functools.partial(qkv_out_body, q_count, per_one),
        [None] * (2 * q_count),
        [None] * 5,
        [sds((chunk, width), F32)] * 3 + [sds((1, chunk), F32)] * 2,
        scratch=[pltpu.VMEM((2, qkv_rows, half), BF)],
        us=1.5,
    )(info, *flat_parts(qkv_parts))

    return (out[None], input_grad[None], grad_gain_one[0], grad_bias_one[0], grad_query, grad_key,
            grad_value, grad_out, grad_gain_two[0], grad_bias_two[0], grad_up, grad_down)


def solution(mesh):
    split = P("seq", "ctx", None)
    in_specs = (split,) + (P(),) * 10 + (split, split, P("seq", None, None, None))
    vec, mat = P("ctx"), P("ctx", None)
    out_specs = (split, split, vec, vec, mat, mat, mat, mat, vec, vec, mat, mat)
    return jax.shard_map(
        per_device, mesh=mesh, in_specs=in_specs, out_specs=out_specs, check_vma=False
    )
```

```python
import functools
import math

import jax
import jax.numpy as jnp
import numpy as np
from jax import lax
from jax.experimental import pallas as pl
from jax.experimental.pallas import tpu as pltpu
from jax.sharding import PartitionSpec as P

EPS = 1e-05
NEG = -1e30
F32 = jnp.float32
BF = jnp.bfloat16
COST = 0.5
ANY = pl.BlockSpec(memory_space=pl.ANY)
VMEM_BYTES = 7 * 1024 * 1024


def dot(a, b):
    return lax.dot_general(a, b, (((1,), (0,)), ((), ())), preferred_element_type=F32)


def dot_nt(a, b):
    return lax.dot_general(a, b, (((1,), (1,)), ((), ())), preferred_element_type=F32)


def dot_tn(a, b):
    return lax.dot_general(a, b, (((0,), (0,)), ((), ())), preferred_element_type=F32)


def low_half():
    return lax.broadcasted_iota(jnp.int32, (1, 128), 1) < 64


def norm_parts(x):
    center = x - jnp.mean(x, -1, keepdims=True)
    spread = jnp.mean(center * center, -1, keepdims=True)
    rstd = lax.rsqrt(spread + EPS)
    return center * rstd, rstd


def norm_back(d_normed, xhat, rstd, gain):
    d_hat = d_normed * gain
    first = jnp.mean(d_hat, -1, keepdims=True)
    second = jnp.mean(d_hat * xhat, -1, keepdims=True)
    return rstd * (d_hat - first - xhat * second)


def rows_at(index, size):
    return pl.ds(pl.multiple_of(index * size, size), size)


def call(body, in_views, out_views, out_shape, scratch=(), us=1.0, vmem=VMEM_BYTES, steps=None,
         in_main=False):
    views = list(in_views) + list(out_views)
    taken = 1 + len(in_views)
    space = pl.BlockSpec(memory_space=pltpu.VMEM)

    def run(info, *args, deps=()):
        def kernel(*refs):
            scalars, arrays = refs[0], refs[1:taken] + refs[taken + len(deps) :]
            for step in range(steps or 1):
                seen = [
                    r if v is None else v(r, step, scalars)
                    for r, v in zip(arrays, views + [None] * len(scratch))
                ]
                if steps is None:
                    body(scalars, *seen)
                else:
                    body(step, scalars, *seen)

        return pl.pallas_call(
            kernel,
            in_specs=[pl.BlockSpec(memory_space=pltpu.SMEM)]
            + [space] * len(in_views)
            + [ANY] * len(deps),
            out_specs=[ANY if in_main else space] * len(out_views),
            out_shape=out_shape,
            scratch_shapes=list(scratch),
            compiler_params=pltpu.CompilerParams(vmem_limit_bytes=vmem),
            cost_estimate=pl.CostEstimate(
                flops=int(us * COST * 1.1e9), bytes_accessed=int(us * COST * 1e6), transcendentals=0
            ),
        )(info, *args, *deps)

    return run


def lanes(ref, p, info):
    return ref.at[:, p * 128 : (p + 1) * 128]


def lead(ref, p, info):
    return ref.at[p : p + 1]


def lead_two(ref, p, info):
    return ref.at[2 * p : 2 * p + 2]


def half_lanes(ref, p, info):
    half = ref.shape[1] // 2
    return ref.at[:, pl.ds(pl.multiple_of(info[0] * half + p * 128, 128), 128)]


def my_columns(ref, p, info):
    half = ref.shape[1] // 2
    return ref.at[:, pl.ds(pl.multiple_of(info[0] * half, 128), half)]


def my_rows(ref, p, info):
    return ref.at[rows_at(info[0], ref.shape[0] // 2), :]


def other_rows(ref, p, info):
    return ref.at[rows_at(1 - info[0], ref.shape[0] // 2), :]


def split3(x):
    first = x.astype(BF)
    left = x - first.astype(F32)
    second = left.astype(BF)
    return first, second, (left - second.astype(F32)).astype(BF)


def half_of(e):
    lo = low_half()
    return lo if e == 0 else ~lo


def spare(e):
    lane = lax.broadcasted_iota(jnp.int32, (1, 128), 1)
    base = 64 if e == 0 else 0
    return [lane == base + i for i in range(3)]


def spare_ones(e):
    marks = spare(e)
    return jnp.where(marks[0] | marks[1] | marks[2], 1.0, 0.0).astype(BF)


def hits_of(ids_row, rows):
    return lax.broadcasted_iota(jnp.int32, (rows, ids_row.shape[1]), 0) == ids_row


def as_hot(hits):
    return jnp.where(hits, 1.0, 0.0).astype(BF)


def top_offsets(tops, stride):
    lane = lax.broadcasted_iota(jnp.int32, tops.shape, 1)
    return (tops - lane * stride).astype(F32).astype(BF)


def top_mask(offs, own, stride, slot):
    shape = (offs.shape[1], own)
    lane = lax.broadcasted_iota(jnp.int32, shape, 1)
    ranges = (lane >> int(math.log2(stride))) + slot * (own // stride)
    expand = as_hot(ranges == lax.broadcasted_iota(jnp.int32, shape, 0))
    spot = (lax.broadcasted_iota(jnp.int32, (1, own), 1) & (stride - 1)).astype(F32)
    return dot(offs, expand) == spot


def chip_at(info, slot):
    return info[1] ^ slot


def pair_tops(tops, p, info, stride):
    _, rows, chosen = tops.shape
    first = info[0] * (tops.shape[0] // 2) + 2 * p
    return top_offsets(tops[pl.ds(first, 2)].reshape(2 * rows, chosen), stride)


def pair_ids(ids, p, info):
    return [ids[2 * p + e : 2 * p + e + 1, :] for e in range(2)]


def pair_rows(rows):
    row = lax.broadcasted_iota(jnp.int32, (2 * rows, 128), 0)
    lane = lax.broadcasted_iota(jnp.int32, (2 * rows, 128), 1)
    column = lax.broadcasted_iota(jnp.int32, (2 * rows, 1), 0)
    return (row < rows) == (lane < 64), column < rows


def pair_hot(lines, rows):
    return jnp.concatenate([as_hot(hits_of(line, rows)) for line in lines], axis=0)


def slot_body(slot, scale, stride, p, info, xa, xb, gain, bias, wq, wk, wv, tops, *rest):
    first = slot == 0
    if first:
        q_out, k_out, v_out, csum, acc, den, top, prob, ids, bar_out, n_out, bar_t, normed = rest
        ids_own = ids
    else:
        ids_own, q_own, q_out, k_out, v_out, csum, acc, den, top, prob, ids, bar_out, normed = rest
    rows = tops.shape[1]
    core = info[0]
    block = xa.shape[0] - 16
    own = 2 * block

    if p == 0:
        for rel, ref in enumerate((xa, xb)):
            at = rows_at(core ^ rel, block)
            xhat, _ = norm_parts(ref[:block, :].astype(F32))
            low = (xhat * gain[...][None] + bias[...][None]).astype(BF)
            normed[at, :] = low
            if first:
                n_out[at, :] = low
        lines = [ref[block:, :block].astype(F32) for ref in (xa, xb)]
        heads = tops.shape[0] // 2
        lines = [jnp.where(core == 0, a[:heads], a[heads : 2 * heads]) for a in lines]
        lines = jnp.where(
            core == 0,
            jnp.concatenate(lines, axis=1),
            jnp.concatenate(lines[::-1], axis=1),
        )
        ids[:heads, :] = lines.astype(jnp.int32)

    weights = jnp.concatenate([wq[...], wk[...], wv[...]], axis=1)
    made = dot(normed[...], weights).astype(BF)
    query, key, value = made[:, :128], made[:, 128:256], made[:, 256:]
    q_out[...] = query
    k_out[...] = key
    v_out[...] = value
    key_t = key.T
    asked = (query if first else q_own[...]) * jnp.asarray(scale, BF)
    peaks, outs = [], []
    one = jnp.ones((), BF)
    hot = pair_hot(pair_ids(ids, p, info), rows)
    hot_own = (hot if first else pair_hot(pair_ids(ids_own, p, info), rows)).T
    count = jnp.sum(hot.astype(F32), axis=1, keepdims=True)
    csum[0] = jnp.where(pair_rows(rows)[0], dot(hot, query), count)
    mask = top_mask(pair_tops(tops, p, info, stride), own, stride, chip_at(info, slot))
    bars = jnp.where(mask, 0.0, NEG).astype(BF)
    bar_out[0] = bars
    if first:
        bar_t[0] = bars.T
    for e in range(2):
        sel = half_of(e)
        bar = bars[e * rows : (e + 1) * rows]
        right = jnp.concatenate([key_t, bar], axis=0)
        member_of = hot_own[:, e * rows : (e + 1) * rows]
        left = jnp.concatenate([jnp.where(sel, asked, jnp.zeros((), BF)), member_of], axis=1)
        score = dot(left, right)
        peak = jnp.max(score, axis=1, keepdims=True)
        grown = jnp.exp(score - peak).astype(BF)
        prob[e] = grown
        peaks.append(peak)
        outs.append(dot(grown, jnp.where(sel, value, one)))
    lo = low_half()
    acc[...] = jnp.where(lo, outs[0], outs[1])
    den[...] = pltpu.roll(jnp.where(lo, outs[1], outs[0]), 64, 1)
    top[...] = jnp.where(lo, peaks[0], peaks[1])


def cluster_body(scale, slots, p, info, ids_own, *rest):
    ks, vs, bars, csums, accs, dens, tops = (rest[i * slots : (i + 1) * slots] for i in range(7))
    att, mem, lse, lse_col, rm, cen, cst = rest[7 * slots :]
    keys = jnp.concatenate([k[...] for k in ks], axis=0)
    values = jnp.concatenate([v[...] for v in vs], axis=0)
    own = ks[0].shape[0]
    rows = bars[0].shape[1] // 2
    lo = low_half()
    lane = lax.broadcasted_iota(jnp.int32, (1, 128), 1)
    sel, upper = pair_rows(rows)
    sums = csums[0][0]
    for c in csums[1:]:
        sums = sums + c[0]
    safe = jnp.maximum(jnp.where(upper, sums[:, 64:65], sums[:, 0:1]), 1.0)
    center = jnp.where(sel, sums / safe, 0.0).astype(BF)
    score = dot_nt(center * jnp.asarray(scale, BF), keys)
    peak = jnp.max(score, axis=1, keepdims=True)
    grown = jnp.exp(score - peak)
    total = jnp.sum(grown, axis=1, keepdims=True)
    inverse = 1.0 / total
    mask = jnp.concatenate([b[0] for b in bars], axis=1) == 0
    mass = (jnp.sum(jnp.where(mask, grown, 0.0), axis=1, keepdims=True) * inverse).astype(BF)
    kept = jnp.where(mask, 0.0, grown).astype(BF)
    attended = jnp.where(sel, dot(kept, values) * inverse, 0.0).astype(BF)
    wide = jnp.where(sel, mass, jnp.zeros((), BF))
    both = jnp.concatenate([attended, wide], axis=1)
    cen[0] = center
    cst[0] = jnp.where(lane == 0, peak + jnp.log(total), safe)
    rm[0] = both
    hot = pair_hot(pair_ids(ids_own, p, info), rows)
    token = dot_tn(hot, both)
    peak = tops[0][...]
    for t in tops[1:]:
        peak = jnp.maximum(peak, t[...])
    total, member = 0.0, 0.0
    for t, d, a in zip(tops, dens, accs):
        weight = jnp.exp(t[...] - peak)
        total += weight * d[...]
        member += weight * a[...]
    member = member / total
    log_total = peak + jnp.log(total)
    lse_col[...] = log_total
    turned = log_total.T
    lse[0] = jnp.concatenate([turned[0:1], turned[64:65], jnp.zeros((6, own), F32)], axis=0)
    mem[...] = member
    att[...] = (token[:, 128:] * member + token[:, :128]).astype(BF)


def ffn_body(steps, step, info, x, cot, att_mine, att_other, wo_mine, wo_other, gain, bias, w_up,
             w_down, out, d_mid, d_attn, da_mine, da_other, normed_out, act_out, du_mine, du_send,
             vecs, acc, dacc):
    if step == 0:
        mid = x[...].astype(F32) + dot(att_mine[...], wo_mine[...]) + dot(att_other[...], wo_other[...])
        d_mid[...] = mid
        xhat, _ = norm_parts(mid)
        normed_out[...] = (xhat * gain[...][None] + bias[...][None]).astype(BF)
    upper = dot(normed_out[...], w_up[...])
    c0 = math.sqrt(2.0 / math.pi)
    square = upper * upper
    tanh = jnp.tanh(c0 * (upper + 0.044715 * square * upper))
    cdf = 0.5 * (1.0 + tanh)
    active = (upper * cdf).astype(BF)
    act_out[...] = active
    more = dot(active, w_down[...])
    acc[...] = more + (d_mid[...] if step == 0 else acc[...])
    slope = cdf + 0.5 * upper * (1.0 - tanh * tanh) * (c0 * (1.0 + 3 * 0.044715 * square))
    d_upper = (dot_nt(cot[...], w_down[...]) * slope).astype(BF)
    half = d_upper.shape[1] // 2
    first = info[0] == 0
    du_mine[0] = jnp.where(first, d_upper[:, :half], d_upper[:, half:])
    du_send[0] = jnp.where(first, d_upper[:, half:], d_upper[:, :half])
    more = dot_nt(d_upper, w_up[...])
    dacc[...] = more if step == 0 else dacc[...] + more
    if step == steps - 1:
        out[...] = acc[...]
        xhat, rstd = norm_parts(d_mid[...])
        d_normed = dacc[...]
        vecs[...] = jnp.concatenate(
            [
                jnp.sum(d_normed * xhat, axis=0, keepdims=True),
                jnp.sum(d_normed, axis=0, keepdims=True),
                jnp.zeros((6, d_normed.shape[1]), F32),
            ],
            axis=0,
        )
        grad = cot[...].astype(F32) + norm_back(d_normed, xhat, rstd, gain[...][None])
        d_mid[...] = grad
        low = grad.astype(BF)
        d_attn[...] = low
        da_mine[...] = dot_nt(low, wo_mine[...]).astype(BF)
        da_other[...] = dot_nt(low, wo_other[...]).astype(BF)


def join_body(info, mine, other, mem, lse, joined):
    core = info[0]
    block, half = mine.shape
    lo = low_half()
    lane = lax.broadcasted_iota(jnp.int32, (1, 128), 1)
    found = {}
    for rel, ref in enumerate((mine, other)):
        at = rows_at(core ^ rel, block)
        joined[at, :] = ref[...]
        for p in range(half // 128):
            part = slice(p * 128, (p + 1) * 128)
            product = ref[:, part].astype(F32) * mem[at, part]
            first = jnp.sum(jnp.where(lo, product, 0.0), axis=1, keepdims=True)
            second = jnp.sum(jnp.where(lo, 0.0, product), axis=1, keepdims=True)
            table = jnp.where(lane == 0, first, jnp.where(lane == 1, second, 0.0)).T
            stat = lse[p, :, at]
            for e in range(2):
                found[p, e, rel] = split3(table[e : e + 1])[:2] + split3(-stat[e : e + 1])
    lines = []
    for p in range(half // 128):
        for e in range(2):
            for rel in range(2):
                lines += [line.astype(F32) for line in found[p, e, rel]]
    lines.append(jnp.zeros((64 - len(lines), block), F32))
    table = jnp.concatenate(lines, axis=0).astype(BF)
    joined[2 * block :, :] = jnp.concatenate(
        [table, jnp.zeros((64, half - block), BF)], axis=1
    )


def query_body(scale, slots, p, info, ids_own, message, mem, rm, lse_col, *rest):
    tops, probs, ks, vs = (rest[i * slots : (i + 1) * slots] for i in range(4))
    dq = rest[4 * slots]
    own = mem.shape[0]
    rows = rm.shape[1] // 2
    lo = low_half()
    hot = pair_hot(pair_ids(ids_own, p, info), rows)
    mass = dot_tn(hot, rm[0, :, 128:])
    grad = message[:own, p * 128 : (p + 1) * 128].astype(F32)
    product = grad * mem[...]
    d_member = (mass * grad).astype(BF)
    lefts = []
    for e in range(2):
        sel = half_of(e)
        other = 0 if e == 0 else 64
        delta = mass[:, other : other + 1] * jnp.sum(
            jnp.where(sel, product, 0.0), axis=1, keepdims=True
        )
        left = jnp.where(sel, d_member, jnp.zeros((), BF))
        for mark, term in zip(spare(e), split3(-delta)):
            left = jnp.where(mark, term, left)
        lefts.append(left)
    total = 0.0
    for s in range(slots):
        d_scores = []
        for e in range(2):
            right = jnp.where(half_of(e), vs[s][...], spare_ones(e))
            moved = dot_nt(lefts[e], right)
            d_scores.append((probs[s][e].astype(F32) * moved).astype(BF))
        made = dot(jnp.concatenate(d_scores, axis=0), ks[s][...])
        total += jnp.exp(tops[s][...] - lse_col[...]) * jnp.where(lo, made[:own], made[own:])
    dq[...] = total * scale


def key_body(scale, p, info, k_own, v_own, query, message, ids, bar_t, rm, dk, dv, dr):
    core = info[0]
    own = k_own.shape[0]
    block = own // 2
    rows = rm.shape[1] // 2
    lo = low_half()
    picked = message[own:, :block].astype(F32)[20 * p : 20 * p + 20]
    datt = message[:own, p * 128 : (p + 1) * 128]

    def term(e, i):
        a, b = picked[10 * e + i : 10 * e + i + 1], picked[10 * e + 5 + i : 10 * e + 6 + i]
        return jnp.where(
            core == 0, jnp.concatenate([a, b], axis=1), jnp.concatenate([b, a], axis=1)
        )

    hot = [as_hot(hits_of(line, rows)) for line in pair_ids(ids, p, info)]
    mass_t = dot_tn(rm[0, :, 128:], jnp.concatenate(hot, axis=0))
    grad = datt
    dm_t = (mass_t * grad.T.astype(F32)).astype(BF)
    d_member = dm_t.T
    asked = query[...]
    asked_t = asked.T
    blank = jnp.zeros((48, own), BF)
    weights, d_scores, d_masses = [], [], []
    pad = jnp.zeros((13, own), F32)
    for e in range(2):
        sel = half_of(e)
        other = 0 if e == 0 else 64
        d_mass = term(e, 0) + term(e, 1)
        d_masses.append(d_mass)
        delta = mass_t[other : other + 1] * d_mass
        aux_s = jnp.concatenate([term(e, 2), term(e, 3), term(e, 4), pad], axis=0).astype(BF)
        aux_d = jnp.concatenate([t.astype(F32) for t in split3(-delta)] + [pad], axis=0).astype(BF)

        def beside(turned, aux):
            if e == 0:
                return jnp.concatenate([turned[:64], aux, blank], axis=0)
            return jnp.concatenate([aux, blank, turned[64:]], axis=0)

        right = jnp.concatenate([beside(asked_t, aux_s), hot[e]], axis=0)
        bar = bar_t[0, :, e * rows : (e + 1) * rows]
        ones = spare_ones(e)
        left = jnp.concatenate(
            [jnp.where(sel, k_own[...] * jnp.asarray(scale, BF), ones), bar], axis=1
        )
        weight = jnp.exp(dot(left, right))
        moved = dot(jnp.where(sel, v_own[...], ones), beside(dm_t, aux_d))
        weights.append(weight.astype(BF))
        d_scores.append((weight * moved).astype(BF))
    made = dot(jnp.concatenate(weights, axis=0), d_member)
    dv[...] = jnp.where(lo, made[:own], made[own:])
    made = dot(jnp.concatenate(d_scores, axis=0), asked)
    dk[...] = jnp.where(lo, made[:own], made[own:])
    hot_both = jnp.concatenate(hot, axis=0)
    d_mass_c = jnp.concatenate(
        [jnp.sum(h.astype(F32) * m, axis=1, keepdims=True) for h, m in zip(hot, d_masses)], axis=0
    )
    dr[0] = jnp.where(pair_rows(rows)[0], dot(hot_both, grad), d_mass_c)


def cluster_back_body(scale, slots, p, info, ids_own, cen, cst, dqm, *rest):
    ks, vs, bars, drs, dks, dvs = (rest[i * slots : (i + 1) * slots] for i in range(6))
    dq, dk, dv = rest[6 * slots :]
    own = ks[0].shape[0]
    keys = jnp.concatenate([k[...] for k in ks], axis=0)
    values = jnp.concatenate([v[...] for v in vs], axis=0)
    rows = cen.shape[1] // 2
    sel, upper = pair_rows(rows)
    log_total, safe = cst[0, :, 0:1], cst[0, :, 1:2]
    both = drs[0][0]
    for r in drs[1:]:
        both = both + r[0]
    d_rest = jnp.where(sel, both, 0.0).astype(BF)
    d_mass = jnp.where(upper, both[:, 64:65], both[:, 0:1])
    cprob = jnp.exp(dot_nt(cen[0] * jnp.asarray(scale, BF), keys) - log_total)
    mask = jnp.concatenate([b[0] for b in bars], axis=1) == 0
    d_prob = jnp.where(mask, d_mass, dot_nt(d_rest, values))
    inner = jnp.sum(cprob * d_prob, axis=1, keepdims=True)
    d_score = (cprob * (d_prob - inner)).astype(BF)
    keeps = jnp.where(mask[:, :own], 0.0, cprob[:, :own]).astype(BF)
    d_sums = jnp.where(sel, dot(d_score, keys) * (scale / safe), 0.0).astype(BF)
    hot = pair_hot(pair_ids(ids_own, p, info), rows)
    dq[...] = (dqm[...] + dot_tn(hot, d_sums)).astype(BF)
    d_key = dot_tn(d_score[:, :own], cen[0])
    d_value = dot_tn(keeps, d_rest)
    for a, b in zip(dks, dvs):
        d_key = d_key + a[...]
        d_value = d_value + b[...]
    dk[...] = (d_key * scale).astype(BF)
    dv[...] = d_value.astype(BF)


def halving_orders(count):
    bits = (count - 1).bit_length()
    low = sorted(range(count), key=lambda r: int(format(r, "0%db" % bits)[::-1], 2) if bits else 0)
    return low, list(range(count))


def emit_chunks(info, flat, outs, places, q_count, per):
    core, place, mine = info[0], info[1], info[2]
    for rel, order in enumerate(halving_orders(q_count)):
        for i, r in enumerate(order):
            out = outs[2 * rel + (0 if i < q_count // 2 else 1)]
            for s in range(places):
                at = place ^ s
                out[i % (q_count // 2), s] = flat[at, core ^ rel, rows_at(mine ^ r, per), :]


def store_rows(flat, value, row, chunk):
    for owner in range(value.shape[0] // chunk):
        flat[owner // 2, owner % 2, row : row + chunk, :] = value[
            owner * chunk : (owner + 1) * chunk
        ].astype(BF)


def store_vecs(flat, vecs, row):
    half = vecs.shape[1] // 2
    lines = jnp.concatenate(
        [vecs[0:1, :half], vecs[0:1, half:], vecs[1:2, :half], vecs[1:2, half:]]
        + [jnp.zeros((12, half), F32)],
        axis=0,
    ).astype(BF)
    for z in range(flat.shape[0]):
        for c in range(2):
            flat[z, c, row : row + 16, :] = lines


def ffn_grad_body(places, q_count, per, info, n_mine, n_other, du_mine, du_other, act_mine, act_other,
                  cot_mine, cot_other, att_mine, att_other, da_mine, da_other, vecs, *rest):
    outs, (flat,) = rest[:-1], rest[-1:]
    core = info[0]
    width = n_mine.shape[1]
    chunk = width // (2 * places)
    step_count = du_mine.shape[0]
    hidden = act_mine.shape[1]
    down_chunk = hidden // (2 * places)
    block = n_mine.shape[0]
    n_t = [n_mine[...].T, n_other[...].T]
    n_t = jnp.concatenate(n_t, axis=1)
    half = du_mine.shape[2]
    for f in range(0, step_count, 2):
        right = [jnp.concatenate([du_mine[i], du_other[i]], axis=0) for i in (f, f + 1)]
        up = dot(n_t, jnp.concatenate(right, axis=1))
        for i in range(2):
            store_rows(flat, up[:, i * half : (i + 1) * half], (f + i) * chunk, chunk)
    base = step_count * chunk
    span = hidden // step_count
    for f in range(step_count):
        part = slice(f * span, (f + 1) * span)
        down = dot_tn(act_mine[:, part], cot_mine[...]) + dot_tn(act_other[:, part], cot_other[...])
        for i in range(span // down_chunk):
            owner = f * (span // down_chunk) + i
            flat[owner // 2, owner % 2, base : base + down_chunk, :] = down[
                i * down_chunk : (i + 1) * down_chunk
            ].astype(BF)
    base += down_chunk
    mine_rows, other_rows = rows_at(core, block), rows_at(1 - core, block)
    halves = []
    for ref in (att_mine, att_other):
        halves.append(
            dot_tn(ref[mine_rows, :], da_mine[...]) + dot_tn(ref[other_rows, :], da_other[...])
        )
    first = core == 0
    store_rows(
        flat,
        jnp.concatenate(
            [jnp.where(first, halves[0], halves[1]), jnp.where(first, halves[1], halves[0])], axis=0
        ),
        base,
        chunk,
    )
    base += chunk
    store_vecs(flat, vecs[...], base)
    emit_chunks(info, flat, outs, places, q_count, per)


def qkv_grad_body(places, q_count, per, info, normed, dq, dk, dv, wq, wk, wv, xa, xb, *rest):
    dn_mine, dn_send = rest[0], rest[1]
    outs, flat, d_all = rest[2:-2], rest[-2], rest[-1]
    core = info[0]
    block, width = dn_mine.shape
    chunk = width // (2 * places)
    n_t = normed[...].T
    half = dq.shape[1]
    grads = jnp.concatenate([dq[...], dk[...], dv[...]], axis=1)
    made = dot(n_t, grads)
    for i in range(3):
        store_rows(flat, made[:, i * half : (i + 1) * half], i * chunk, chunk)
    weights = jnp.concatenate([wq[...], wk[...], wv[...]], axis=1)
    d_all[...] = dot_nt(grads, weights)
    gains, biases = 0.0, 0.0
    for rel, (ref, out) in enumerate(((xa, dn_mine), (xb, dn_send))):
        rows = rows_at(core ^ rel, block)
        d_normed = d_all[rows, :]
        out[...] = d_normed
        xhat, _ = norm_parts(ref[:block, :].astype(F32))
        gains += jnp.sum(d_normed * xhat, axis=0, keepdims=True)
        biases += jnp.sum(d_normed, axis=0, keepdims=True)
    store_vecs(flat, jnp.concatenate([gains, biases], axis=0), 3 * chunk)
    emit_chunks(info, flat, outs, places, q_count, per)


def input_body(info, x, gain, dn_mine, dn_other, d_mid, forward, out, forward_out, made):
    xhat, rstd = norm_parts(x[...].astype(F32))
    made[...] = d_mid[...] + norm_back(dn_mine[...] + dn_other[...], xhat, rstd, gain[...][None])
    pltpu.sync_copy(made, out)
    pltpu.sync_copy(forward, forward_out)


def place_parts(info, parts, segments, vec_row, vecs, q_count, per):
    core, own = info[0], info[2]

    def half_of_part(part, i):
        return part if len(part.shape) == 2 else part.at[i]

    for r in range(q_count):
        halves = [half_of_part(part, i) for i, part in enumerate(parts[2 * r : 2 * r + 2])]
        for q in range(q_count):

            @pl.when((own ^ r) == q)
            def _(halves=halves, q=q):
                low, high = q * per, (q + 1) * per
                for first, out, column in segments:
                    begin, end = max(low, first), min(high, first + out.shape[0])
                    if begin >= end:
                        continue
                    for i, half in enumerate(halves):
                        width = half.shape[1]
                        at = pl.multiple_of((core ^ i) * width + column, 128)
                        out[begin - first : end - first, pl.ds(at, width)] = half[
                            begin - low : end - low, :
                        ].astype(F32)
                if low <= vec_row < high:
                    rows = slice(vec_row - low, vec_row - low + 16)
                    lines = halves[0][rows, :].astype(F32) + halves[1][rows, :].astype(F32)
                    emit_vecs(info, lines, vecs, vecs[0].shape[1])


def emit_vecs(info, lines, outs, chunk):
    for i, out in enumerate(outs):
        whole = jnp.concatenate([lines[2 * i : 2 * i + 1], lines[2 * i + 1 : 2 * i + 2]], axis=1)
        width = whole.shape[1]
        whole = jnp.concatenate([whole, jnp.zeros((7, width), F32)], axis=0)
        shift = width - (2 * info[1] + info[0]) * chunk
        out[...] = pltpu.roll(whole, shift, 1)[0:1, :chunk]


def ffn_out_body(q_count, per, info, *rest):
    up, down, out, gain, bias = rest[2 * q_count :]
    chunk, half = up.shape[0], out.shape[1] // 2
    steps = up.shape[1] // (2 * half)
    segments = [(f * chunk, up, 2 * f * half) for f in range(steps)]
    base = steps * chunk
    segments += [(base, down, 0), (base + down.shape[0], out, 0)]
    base += down.shape[0] + chunk
    place_parts(info, rest[: 2 * q_count], segments, base, (gain, bias), q_count, per)


def qkv_out_body(q_count, per, info, *rest):
    outs, vecs = rest[2 * q_count : 2 * q_count + 3], rest[2 * q_count + 3 :]
    chunk = outs[0].shape[0]
    segments = [(i * chunk, out, 0) for i, out in enumerate(outs)]
    place_parts(info, rest[: 2 * q_count], segments, 3 * chunk, vecs, q_count, per)


def pack_body(info, x, ids, out):
    block, width = x.shape
    heads = ids.shape[0]
    out[:block, :] = x[...]
    lines = jnp.concatenate([ids[...].astype(F32), jnp.zeros((16 - heads, block), F32)], axis=0)
    out[block:, :] = jnp.concatenate(
        [lines, jnp.zeros((16, width - block), F32)], axis=1
    ).astype(BF)


def hold_body(info, *refs):
    count = len(refs) // 2
    for source, target in zip(refs[:count], refs[count:]):
        target[...] = source[...]


def fold_body(info, keep_a, came_a, keep_b, came_b, *outs):
    for i, (keep, came) in enumerate(((keep_a, came_a), (keep_b, came_b))):
        cut = keep.shape[0] // 2
        for j in range(2):
            part = slice(j * cut, (j + 1) * cut)
            outs[2 * i + j][...] = (keep[part].astype(F32) + came[part].astype(F32)).astype(BF)


def merge_body(info, keep_a, came_a, keep_b, came_b, *outs):
    for s, out in enumerate(outs):
        out[0] = (keep_a[0, s].astype(F32) + came_a[0, s].astype(F32)).astype(BF)
        out[1] = (keep_b[0, s].astype(F32) + came_b[0, s].astype(F32)).astype(BF)


def sum_body(info, *refs):
    total = refs[0][...].astype(F32)
    for ref in refs[1:-1]:
        total = total + ref[...].astype(F32)
    refs[-1][...] = total.astype(BF)


def total_body(info, *refs):
    parts, stay, go = refs[:-2], refs[-2], refs[-1]
    for i, out in enumerate((stay, go)):
        total = parts[0][i].astype(F32)
        for part in parts[1:]:
            total = total + part[i].astype(F32)
        out[...] = total.astype(BF)


def per_device(tokens, gain_one, bias_one, w_query, w_key, w_value, w_out, gain_two, bias_two,
               w_up, w_down, cotangent, cluster_ids, top_keys):
    _, block, width = tokens.shape
    heads = cluster_ids.shape[2]
    clusters, chosen = top_keys.shape[2], top_keys.shape[3]
    ctx, q_count = lax.axis_size("ctx"), lax.axis_size("seq")
    places = ctx // 2
    index, mine = lax.axis_index("ctx"), lax.axis_index("seq")
    core, place = index % 2, index // 2
    full_len = block * ctx
    own = 2 * block
    half = width // 2
    hidden = w_up.shape[1]
    pairs = half // 128
    stride = full_len // chosen
    rows = -(-clusters // 128) * 128
    scale = 1.0 / math.sqrt(width // heads)
    info = jnp.stack([core, place, mine]).astype(jnp.int32)
    sds = jax.ShapeDtypeStruct
    swap_to = [(i, i ^ 1) for i in range(ctx)]

    def swap(a):
        return lax.ppermute(a, "ctx", swap_to)

    def along(a, s):
        to = [(2 * z + c, 2 * (z ^ s) + c) for z in range(places) for c in range(2)]
        return lax.ppermute(a, "ctx", to)

    def hold(arrays, deps):
        shapes = [sds(a.shape, a.dtype) for a in arrays]
        return call(hold_body, [None] * len(arrays), [None] * len(arrays), shapes)(
            info, *arrays, deps=tuple(deps)
        )

    def across(a, r):
        return lax.ppermute(a, "seq", [(i, i ^ r) for i in range(q_count)])

    hops = [1 << i for i in range((places - 1).bit_length())][::-1]
    known, paths = [0], {}
    for hop in hops:
        paths.update({k ^ hop: (k, hop) for k in known})
        known += [k ^ hop for k in known]
    depth = {0: 0}
    for s in paths:
        depth[s] = depth[paths[s][0]] + 1
    stages = [[s for s in paths if depth[s] == d] for d in range(1, max(depth.values()) + 1)]
    order = [0] + [s for stage in stages for s in stage]

    x, cot = tokens[0], cotangent[0]

    packed = call(pack_body, [None] * 2, [None], [sds((block + 16, width), BF)])(
        info, x, cluster_ids[0].T
    )[0]
    came = {s: along(packed, s) for s in stages[0]}
    packed_other = swap(packed)
    cot_other = swap(cot)
    keys_top = jnp.pad(top_keys[0], ((0, 0), (0, rows - clusters), (0, 0)))

    flat_half = sds((own, half), F32)

    def slot_call(s, xa, xb, slot0=None, deps=()):
        first = s == 0
        in_views = [None] * 4 + [half_lanes] * 3 + [None]
        operands = [xa, xb, gain_one, bias_one, w_query, w_key, w_value, keys_top]
        out_views = [lanes] * 3 + [lead] + [lanes] * 3 + [lead_two, None, lead]
        out_shape = [sds((own, half), BF)] * 3 + [sds((pairs, 2 * rows, 128), F32)]
        out_shape += [flat_half] * 3 + [sds((2 * pairs, own, own), BF), sds((8, own), jnp.int32),
                      sds((pairs, 2 * rows, own), BF)]
        if first:
            out_views += [None, lead]
            out_shape += [sds((own, width), BF), sds((pairs, own, 2 * rows), BF)]
        else:
            in_views += [None, lanes]
            operands += [slot0[8], slot0[0]]
        return call(
            functools.partial(slot_body, s, scale, stride),
            in_views, out_views, out_shape,
            scratch=[pltpu.VMEM((own, width), BF)], us=8.0, steps=pairs,
        )(info, *operands, deps=deps)

    *slot0, normed, bar_t = slot_call(0, packed, packed_other)
    slots = {0: slot0}
    last = slot0[0]
    for i, stage in enumerate(stages):
        done = [slots[s][0] for s in stages[i - 1]] if i else [last]
        arrays = hold([came[s] for s in stage], done)
        held = dict(zip(stage, arrays))
        if i + 1 < len(stages):
            came.update({s: along(held[paths[s][0]], paths[s][1]) for s in stages[i + 1]})
        others = [swap(a) for a in arrays]
        for s, mine_block, other_block in zip(stage, arrays, others):
            deps = (last,) if s == stage[-1] else ()
            slots[s] = slot_call(s, mine_block, other_block, slot0, deps)
            last = slots[s][0] if s == stage[0] else last
    slots = [slots[s] for s in range(places)]
    query, key, value, csums, accs, dens, tops, probs, ids, bars = zip(*slots)

    att, mem, lse, lse_col, rm, cen, cst = call(
        functools.partial(cluster_body, scale, places),
        [None] + [lanes] * (2 * places) + [lead] * (2 * places) + [lanes] * (3 * places),
        [lanes, lanes, lead, lanes, lead, lead, lead],
        [sds((own, half), BF), flat_half, sds((pairs, 8, own), F32), flat_half,
         sds((pairs, 2 * rows, 256), BF), sds((pairs, 2 * rows, 128), BF),
         sds((pairs, 2 * rows, 128), F32)],
        us=10.0, steps=pairs,
    )(info, ids[0], *key, *value, *bars, *csums, *accs, *dens, *tops)

    att_other = swap(att)

    steps = hidden // width
    def step_columns(ref, f, info):
        return ref.at[:, f * width : (f + 1) * width]

    def step_rows(ref, f, info):
        return ref.at[f * width : (f + 1) * width, :]

    out, d_mid, d_attn, da_mine, da_send, normed_two, act, du_mine, du_send, vecs_two = call(
        functools.partial(ffn_body, steps),
        [None, None, my_rows, my_rows, my_rows, other_rows, None, None, step_columns, step_rows],
        [None] * 6 + [step_columns, lead, lead, None],
        [sds((block, width), F32), sds((block, width), F32), sds((block, width), BF),
         sds((block, half), BF), sds((block, half), BF), sds((block, width), BF),
         sds((block, hidden), BF), sds((steps, block, half), BF), sds((steps, block, half), BF),
         sds((8, width), F32)],
        scratch=[pltpu.VMEM((block, width), F32), pltpu.VMEM((block, width), F32)],
        us=13.0, steps=steps,
    )(info, x, cot, att, att_other, w_out, w_out, gain_two, bias_two, w_up, w_down)

    message = call(
        join_body,
        [None] * 4,
        [None],
        [sds((own + 64, half), BF)],
        us=1.5,
    )(info, da_mine, swap(da_send), mem, lse)[0]
    messages = {0: message}
    messages.update({s: along(message, s) for s in stages[0]})

    chunk, down_chunk = width // ctx, hidden // ctx

    def padded(n):
        return -(-n // (16 * q_count)) * 16 * q_count

    def chunk_outs(count):
        shape = (q_count // 2, places, count // q_count, half)
        return [None] * 4, [sds(shape, BF)] * 4

    ffn_rows = padded(steps * chunk + down_chunk + chunk + 16)
    per = ffn_rows // q_count
    ffn_pieces = call(
        functools.partial(ffn_grad_body, places, q_count, per),
        [None] * 6 + [my_columns, my_columns, None, None, my_columns, my_columns, None],
        *chunk_outs(ffn_rows),
        scratch=[pltpu.VMEM((places, 2, ffn_rows, half), BF)],
        us=9.0,
    )(info, normed_two, swap(normed_two), du_mine, swap(du_send), act, swap(act), cot, cot_other,
      att, att_other, d_attn, swap(d_attn), vecs_two, deps=(message,))

    bits = [1 << i for i in range((q_count - 1).bit_length())]

    def reduce_first(pieces):
        return across(pieces[1], bits[0]), across(pieces[3], bits[-1])

    def reduce_second(pieces, got, deps=()):
        ends = [pieces[0], got[0], pieces[2], got[1]]
        for low_bit, high_bit in zip(bits[1:], bits[-2::-1]):
            shape = sds((ends[0].shape[0] // 2,) + ends[0].shape[1:], BF)
            keep_a, send_a, keep_b, send_b = call(fold_body, [None] * 4, [None] * 4, [shape] * 4)(
                info, *ends, deps=deps
            )
            ends = [keep_a, across(send_a, low_bit), keep_b, across(send_b, high_bit)]
        return ends

    def reduce_third(ends, deps=()):
        shape = sds((2,) + ends[0].shape[2:], BF)
        parts = call(merge_body, [None] * 4, [None] * places, [shape] * places)(info, *ends, deps=deps)
        parts = dict(enumerate(parts))
        first = parts[0]
        for stage in stages[:0:-1]:
            added = {}
            for s in stage:
                keep, hop = paths[s]
                added.setdefault(keep, []).append(along(parts.pop(s), hop))
            for keep, others in added.items():
                parts[keep] = sum_call([parts[keep], *others])
        return first, [along(parts[s], paths[s][1]) for s in stages[0]]

    def sum_call(arrays, deps=()):
        shape = sds(arrays[0].shape, BF)
        return call(sum_body, [None] * len(arrays), [None], [shape], us=1.5)(info, *arrays, deps=deps)[0]

    def reduce_total(part, others, deps=()):
        one = sds(part.shape[1:], BF)
        count = 1 + len(others)
        return call(total_body, [None] * count, [None] * 2, [one] * 2, us=1.5)(
            info, part, *others, deps=deps
        )

    def spread(stay, go, relay=False):
        if not relay:
            mixed = jnp.stack([stay, swap(go)])
            return [(mixed, mixed)] + [(a, a) for a in [across(mixed, r) for r in range(1, q_count)]]
        go = swap(go)
        parts = [(stay, go)] + [(across(stay, r), across(go, r)) for r in (1, 2)]
        return parts + [(across(parts[2][0], 1), across(parts[1][1], 2))]

    def flat_parts(parts):
        return [half for pair in parts for half in pair]

    ffn_got = reduce_first(ffn_pieces)

    def key_call(s, deps):
        return call(
            functools.partial(key_body, scale),
            [lanes] * 3 + [None] * 2 + [lead] * 2,
            [lanes, lanes, lead],
            [flat_half, flat_half, sds((pairs, 2 * rows, 128), F32)],
            us=6.0, steps=pairs,
        )(info, key[0], value[0], query[s], messages[s], ids[s], bar_t, rm, deps=deps)

    grads = {0: key_call(0, (ffn_pieces[0],))}
    def query_call(deps):
        return call(
            functools.partial(query_body, scale, places),
            [None, None, lanes, lead, lanes] + [lanes] * places + [lead_two] * places
            + [lanes] * (2 * places),
            [lanes],
            [flat_half],
            us=10.0, steps=pairs,
        )(info, ids[0], message, mem, rm, lse_col, *tops, *probs, *key, *value, deps=deps)[0]

    dqm = query_call((grads[0][0],))
    last = dqm
    for i, stage in enumerate(stages):
        deps = (last,)
        if i + 1 < len(stages):
            begun = {paths[s][0] for s in stages[i + 1]}
            held = hold([messages[k] for k in begun], (last,))
            held = dict(zip(begun, held))
            messages.update({s: along(held[paths[s][0]], paths[s][1]) for s in stages[i + 1]})
            deps = tuple(held.values())
        for s in stage:
            if s == order[-1]:
                ffn_ends = reduce_second(ffn_pieces, ffn_got, (last,))
                deps = (ffn_ends[0],)
            grads[s] = key_call(s, deps)
            last = grads[s][0]
            deps = (last,)
    dks, dvs, drs = zip(*[grads[s] for s in range(places)])

    dq, dk, dv = call(
        functools.partial(cluster_back_body, scale, places),
        [None] + [lead] * 2 + [lanes] * (2 * places + 1) + [lead] * (2 * places) + [lanes] * (2 * places),
        [lanes] * 3,
        [sds((own, half), BF)] * 3,
        us=10.0, steps=pairs,
    )(info, ids[0], cen, cst, dqm, *key, *value, *bars, *drs, *dks, *dvs)

    qkv_rows = padded(3 * chunk + 16)
    per_one = qkv_rows // q_count
    specs, shapes = chunk_outs(qkv_rows)
    dn_mine, dn_send, *qkv_pieces = call(
        functools.partial(qkv_grad_body, places, q_count, per_one),
        [None] * 4 + [my_columns] * 3 + [None] * 2,
        [None] * 2 + specs,
        [sds((block, width), F32)] * 2 + shapes,
        scratch=[pltpu.VMEM((places, 2, qkv_rows, half), BF), pltpu.VMEM((own, width), F32)],
        us=7.0,
    )(info, normed, dq, dk, dv, w_query, w_key, w_value, packed, packed_other)
    qkv_got = reduce_first(qkv_pieces)
    ffn_third = reduce_third(ffn_ends, (dn_mine,))
    input_grad, forward_out = call(
        input_body,
        [None] * 6,
        [None] * 2,
        [sds((block, width), F32)] * 2,
        scratch=[pltpu.VMEM((block, width), F32)], us=2.3, in_main=True,
    )(info, x, gain_one, dn_mine, swap(dn_send), d_mid, out)

    qkv_ends = reduce_second(qkv_pieces, qkv_got)
    qkv_third = reduce_third(qkv_ends, deps=(pltpu.with_memory_space_constraint(input_grad, pltpu.HBM),))
    ffn_total = reduce_total(*ffn_third, deps=(qkv_third[0],))
    ffn_parts = spread(*ffn_total, relay=q_count == 4)
    grad_up, grad_down, grad_out, grad_gain_two, grad_bias_two = call(
        functools.partial(ffn_out_body, q_count, per),
        [None] * (2 * q_count),
        [None] * 5,
        [sds((chunk, hidden), F32), sds((down_chunk, width), F32), sds((chunk, width), F32),
         sds((1, chunk), F32), sds((1, chunk), F32)],
        us=3.0,
    )(info, *flat_parts(ffn_parts))
    qkv_parts = spread(*reduce_total(*qkv_third, deps=(ffn_parts[1][0], ffn_parts[2][0])))
    grad_query, grad_key, grad_value, grad_gain_one, grad_bias_one = call(
        functools.partial(qkv_out_body, q_count, per_one),
        [None] * (2 * q_count),
        [None] * 5,
        [sds((chunk, width), F32)] * 3 + [sds((1, chunk), F32)] * 2,
        us=1.5,
    )(info, *flat_parts(qkv_parts))

    return (forward_out[None], input_grad[None], grad_gain_one[0], grad_bias_one[0], grad_query, grad_key,
            grad_value, grad_out, grad_gain_two[0], grad_bias_two[0], grad_up, grad_down)


def solution(mesh):
    split = P("seq", "ctx", None)
    in_specs = (split,) + (P(),) * 10 + (split, split, P("seq", None, None, None))
    vec, mat = P("ctx"), P("ctx", None)
    out_specs = (split, split, vec, vec, mat, mat, mat, mat, vec, vec, mat, mat)
    return jax.shard_map(
        per_device, mesh=mesh, in_specs=in_specs, out_specs=out_specs, check_vma=False
    )
```
